32 devices in a mesh: seq: 8 (over y, x, core), shard: 4 (over z).
Axes of the slice: x: 2, y: 2, z: 4, core: 2. Of those that a mesh axis runs over, the one named last changes fastest.
Arguments:
- tokens: bfloat16 [40960, 768], P(('seq', 'shard')), may hold values from -6 to 6
- positions: int32 [40960], P(('seq', 'shard')), may hold values from 0 to 2430, as said below
- cotangent: bfloat16 [40960, 768], P(('seq', 'shard')), may hold values from -6 to 6
- qkv_weight: float32 [768, 2304], P('shard'), may hold values from -0.21875 to 0.21875
- attn_weight: float32 [768, 768], P('shard'), may hold values from -0.875 to 0.875
- mlp_weight: float32 [768, 2304], P('shard'), may hold values from -0.21875 to 0.21875
- down_weight: float32 [1152, 768], P('shard'), may hold values from -0.1875 to 0.1875
- norm_gains: float32 [2, 768], P(None, 'shard'), may hold values from 0.5 to 1.5
- qkv_first: float32 [768, 2304], P('shard'), may hold values from -64 to 64
- qkv_second: float32 [768, 2304], P('shard'), may hold values from 208.896 to 835.584
- attn_first: float32 [768, 768], P('shard'), may hold values from -32 to 32
- attn_second: float32 [768, 768], P('shard'), may hold values from 52.224 to 208.896
- mlp_first: float32 [768, 2304], P('shard'), may hold values from -64 to 64
- mlp_second: float32 [768, 2304], P('shard'), may hold values from 169.1648 to 676.6592
- down_first: float32 [1152, 768], P('shard'), may hold values from -80 to 80
- down_second: float32 [1152, 768], P('shard'), may hold values from 300.6464 to 1203.4048
- gains_first: float32 [2, 768], P(None, 'shard'), may hold values from -112 to 112
- gains_second: float32 [2, 768], P(None, 'shard'), may hold values from 534.9376 to 2139.7505
Outputs:
- layer_output: bfloat16 [40960, 768], P(('seq', 'shard'))
- input_grad: bfloat16 [40960, 768], P(('seq', 'shard'))
- qkv_first_new: float32 [768, 2304], P('shard')
- qkv_second_new: float32 [768, 2304], P('shard')
- qkv_new: float32 [768, 2304], P('shard')
- attn_first_new: float32 [768, 768], P('shard')
- attn_second_new: float32 [768, 768], P('shard')
- attn_new: float32 [768, 768], P('shard')
- mlp_first_new: float32 [768, 2304], P('shard')
- mlp_second_new: float32 [768, 2304], P('shard')
- mlp_new: float32 [768, 2304], P('shard')
- down_first_new: float32 [1152, 768], P('shard')
- down_second_new: float32 [1152, 768], P('shard')
- down_new: float32 [1152, 768], P('shard')
- gains_first_new: float32 [2, 768], P(None, 'shard')
- gains_second_new: float32 [2, 768], P(None, 'shard')
- gains_new: float32 [2, 768], P(None, 'shard')
The draws below stay inside these ranges and needn't reach their ends.
Inputs may be any that keep to these rules, and one draw needn't show every extreme that they name: positions[t] counts the tokens of t's document before t. A document starts at token 0, and exactly once in each aligned run of 1280 tokens (the tokens of one device), never among the first 64 or the last 64 tokens of that run.
All inputs are finite; a program needn't handle non-finite values.
Results may differ from the reference program's by a relative error of at most 0.015.
Values may be sent and summed in bfloat16 or wider, within the bound.
No kernel may reach another device: no remote copies, remote signals or barrier semaphores. Data moves between devices by JAX's collectives and lax.ppermute only.
A program may use at most 320 MiB of HBM per device.

```python
import math
import jax
import jax.numpy as jnp
from jax import lax

D = 768
HEADS = 12
FF = 1152
HALF = 64
TOK_DEV = 1280
ADAM_STEP = 5
TOKENS = 40960


def draw_positions(key, part):
    longest_key = jax.random.fold_in(key, 11)
    key = jax.random.fold_in(key, 7)
    block_count = TOKENS // TOK_DEV
    offsets = jax.random.randint(key, (block_count,), HALF, TOK_DEV - HALF, dtype=jnp.int32)
    chosen = jax.random.randint(longest_key, (), 0, block_count - 1, dtype=jnp.int32)
    offsets = offsets.at[chosen].set(HALF)
    offsets = offsets.at[chosen + 1].set(TOK_DEV - HALF - 1)
    token_index = jnp.arange(TOKENS, dtype=jnp.int32)
    owner_block = token_index // TOK_DEV
    local_index = token_index - owner_block * TOK_DEV
    start_here = owner_block * TOK_DEV + offsets[owner_block]
    earlier_block = jnp.maximum(owner_block - 1, 0)
    start_before = jnp.where(owner_block > 0, earlier_block * TOK_DEV + offsets[earlier_block], 0)
    latest = jnp.where(local_index >= offsets[owner_block], start_here, start_before)
    return (token_index - latest).astype(jnp.int32)


def levels(own_key, shape, shards, smallest, largest):
    def one(axis_at, parts):
        steps = jax.random.uniform(jax.random.fold_in(jax.random.fold_in(own_key, 6), axis_at), (parts,), jnp.float32, smallest / len(shards), largest / len(shards))
        return jnp.repeat(jnp.exp(steps), shape[axis_at] // parts).reshape((-1,) + (1,) * (len(shape) - axis_at - 1))

    level = one(*shards[0])
    for cut in shards[1:]:
        level = level * one(*cut)
    return level


def gaussian(rng, dims, spread, limit, shards=(), held_as=jnp.bfloat16):
    array = jax.random.normal(rng, dims, jnp.float32) * spread
    if len(shards) > 0:
        array = levels(rng, dims, shards, -0.22, 0.18) * array
    return jnp.clip(array, min=-limit, max=limit).astype(held_as)


def setup_inputs(seed: int = 0) -> dict:
    key_list = jax.random.split(jax.random.key(seed), 19)
    tokens = gaussian(key_list[0], (TOKENS, D), 1.0, 6.0, ((0, 32),))
    positions = draw_positions(jax.random.fold_in(key_list[18], 71), 0)
    cotangent = gaussian(key_list[2], (TOKENS, D), 1.0, 6.0, ((0, 32),))
    qkv_weight = gaussian(key_list[3], (D, 3 * D), D ** -0.5, 0.21875, ((0, 4),), jnp.float32)
    attn_weight = gaussian(key_list[4], (D, D), (D // 16) ** -0.5, 0.875, ((0, 4),), jnp.float32)
    mlp_weight = gaussian(key_list[5], (D, 2 * FF), D ** -0.5, 0.21875, ((0, 4),), jnp.float32)
    down_weight = gaussian(key_list[6], (FF, D), FF ** -0.5, 0.1875, ((0, 4),), jnp.float32)
    norm_gains = jnp.clip(1.0 + 0.1 * jax.random.normal(key_list[7], (2, D), jnp.float32), 0.5, 1.5)
    qkv_first = gaussian(key_list[8], (D, 3 * D), (0.0555 * TOKENS ** 0.5), 64.0, ((0, 4),), jnp.float32)
    qkv_second = jnp.clip(jnp.exp(math.log(835.584) - 1.3862944 * jax.random.uniform(key_list[9], (D, 3 * D), jnp.float32) ** levels(key_list[9], (D, 3 * D), ((0, 4),), -0.2, 0.2)), 208.896, 835.584)
    attn_first = gaussian(key_list[10], (D, D), (0.02775 * TOKENS ** 0.5), 32.0, ((0, 4),), jnp.float32)
    attn_second = jnp.clip(jnp.exp(math.log(208.896) - 1.3862944 * jax.random.uniform(key_list[11], (D, D), jnp.float32) ** levels(key_list[11], (D, D), ((0, 4),), -0.2, 0.2)), 52.224, 208.896)
    mlp_first = gaussian(key_list[12], (D, 2 * FF), (0.05 * TOKENS ** 0.5), 64.0, ((0, 4),), jnp.float32)
    mlp_second = jnp.clip(jnp.exp(math.log(676.6592) - 1.3862944 * jax.random.uniform(key_list[13], (D, 2 * FF), jnp.float32) ** levels(key_list[13], (D, 2 * FF), ((0, 4),), -0.2, 0.2)), 169.1648, 676.6592)
    down_first = gaussian(key_list[14], (FF, D), (0.0666 * TOKENS ** 0.5), 80.0, ((0, 4),), jnp.float32)
    down_second = jnp.clip(jnp.exp(math.log(1203.4048) - 1.3869753 * jax.random.uniform(key_list[15], (FF, D), jnp.float32) ** levels(key_list[15], (FF, D), ((0, 4),), -0.2, 0.2)), 300.6464, 1203.4048)
    gains_first = gaussian(key_list[16], (2, D), (0.0888 * TOKENS ** 0.5), 112.0, ((1, 4),), jnp.float32)
    gains_second = jnp.clip(jnp.exp(math.log(2139.7505) - 1.3862944 * jax.random.uniform(key_list[17], (2, D), jnp.float32) ** levels(key_list[17], (2, D), ((1, 4),), -0.2, 0.2)), 534.9376, 2139.7505)
    return dict(tokens=tokens, positions=positions, cotangent=cotangent, qkv_weight=qkv_weight, attn_weight=attn_weight, mlp_weight=mlp_weight, down_weight=down_weight, norm_gains=norm_gains, qkv_first=qkv_first, qkv_second=qkv_second, attn_first=attn_first, attn_second=attn_second, mlp_first=mlp_first, mlp_second=mlp_second, down_first=down_first, down_second=down_second, gains_first=gains_first, gains_second=gains_second)


norm_epsilon = 1e-05
rope_theta = 10000.0
beta_first = 0.9
beta_second = 0.98
adam_epsilon = 1e-06
decay_rate = 1e-05
rate_matrix = 0.04
rate_gains = 0.2
masked_score = -1e+30
highest = lax.Precision.HIGHEST

@jax.custom_vjp
def low(v):
    return lax.optimization_barrier(v.astype(jnp.bfloat16)).astype(jnp.float32)

@jax.custom_vjp
def low_back(v):
    return v

def low_keep(v):
    return (low(v), None)

def low_pass(kept, grad):
    return (grad,)

def back_keep(v):
    return (v, None)

def back_low(kept, grad):
    return (low(grad),)
low.defvjp(low_keep, low_pass)
low_back.defvjp(back_keep, back_low)

def layer_norm(hidden, gain_row):
    centered = hidden - lax.optimization_barrier(jnp.mean(hidden, axis=-1, keepdims=True))
    inverse_dev = lax.rsqrt(lax.optimization_barrier(jnp.mean(centered * centered, axis=-1, keepdims=True)) + norm_epsilon)
    return centered * inverse_dev * gain_row

def rope_tables(positions, head_size):
    half_size = head_size // 2
    exponent = jnp.arange(half_size, dtype=jnp.float32) * (2.0 / head_size)
    inverse = rope_theta ** (-exponent)
    angles = positions.astype(jnp.float32)[:, None] * inverse[None, :]
    angles = jnp.concatenate([angles, angles], axis=-1)
    return (jnp.cos(angles)[:, None, :], jnp.sin(angles)[:, None, :])

def rotate_half(values):
    half_size = values.shape[-1] // 2
    return jnp.concatenate([-values[..., half_size:], values[..., :half_size]], axis=-1)

def geglu(expanded):
    hidden_size = expanded.shape[-1] // 2
    return jax.nn.gelu(expanded[:, :hidden_size], approximate=False) * expanded[:, hidden_size:]

def adam_update(master, first_moment, second_moment, gradient, step_rate):
    new_first = beta_first * first_moment + (1.0 - beta_first) * gradient
    new_second = beta_second * second_moment + (1.0 - beta_second) * gradient * gradient
    first_hat = new_first / (1.0 - beta_first ** ADAM_STEP)
    second_hat = new_second / (1.0 - beta_second ** ADAM_STEP)
    new_master = master - step_rate * (decay_rate * master + first_hat / (jnp.sqrt(second_hat) + adam_epsilon))
    return (new_first, new_second, new_master)

def reference(tokens, positions, cotangent, qkv_weight, attn_weight, mlp_weight, down_weight, norm_gains, qkv_first, qkv_second, attn_first, attn_second, mlp_first, mlp_second, down_first, down_second, gains_first, gains_second):
    head_size = D // HEADS
    score_scale = 1.0 / math.sqrt(head_size)
    block_rows = math.gcd(TOKENS, 512)
    block_count = TOKENS // block_rows
    cos_table, sin_table = rope_tables(positions, head_size)
    padded_positions = jnp.pad(positions, (HALF, HALF))
    starts = jnp.arange(block_count, dtype=jnp.int32) * block_rows

    def forward(residual, qkv_master, attn_master, mlp_master, down_master, gains_master):
        qkv_low = low(qkv_master)
        attn_low = low(attn_master)
        mlp_low = low(mlp_master)
        down_low = low(down_master)
        low_gains = low(gains_master)
        first_norm = low(layer_norm(residual, low_gains[0]))
        projected = low_back(jnp.dot(first_norm, qkv_low, precision=highest))
        queries_raw = projected[:, :D].reshape(TOKENS, HEADS, head_size)
        keys_raw = projected[:, D:2 * D].reshape(TOKENS, HEADS, head_size)
        queries = low(queries_raw * cos_table + rotate_half(queries_raw) * sin_table)
        keys_low = low(keys_raw * cos_table + rotate_half(keys_raw) * sin_table)
        values_low = low(projected[:, 2 * D:].reshape(TOKENS, HEADS, head_size))
        keys_pad = jnp.pad(keys_low, ((HALF, HALF), (0, 0), (0, 0)))
        values_pad = jnp.pad(values_low, ((HALF, HALF), (0, 0), (0, 0)))

        def attend(first_row):
            query_block = lax.dynamic_slice_in_dim(queries, first_row, block_rows, 0)
            key_block = lax.dynamic_slice_in_dim(keys_pad, first_row, block_rows + 2 * HALF, 0)
            value_block = lax.dynamic_slice_in_dim(values_pad, first_row, block_rows + 2 * HALF, 0)
            query_index = first_row + jnp.arange(block_rows, dtype=jnp.int32)
            key_index = first_row - HALF + jnp.arange(block_rows + 2 * HALF, dtype=jnp.int32)
            query_pos = lax.dynamic_slice_in_dim(positions, first_row, block_rows, 0)
            key_pos = lax.dynamic_slice_in_dim(padded_positions, first_row, block_rows + 2 * HALF, 0)
            distance = query_index[:, None] - key_index[None, :]
            inside_block = (key_index >= 0) & (key_index < TOKENS)
            allowed = (jnp.abs(distance) <= HALF) & inside_block[None, :] & (query_pos[:, None] - key_pos[None, :] == distance)
            scores = low_back(jnp.einsum('qhd,khd->hqk', query_block, key_block, precision=highest) * score_scale)
            masked = jnp.where(allowed[None], scores, masked_score)
            row_top = lax.optimization_barrier(jnp.max(masked, axis=-1, keepdims=True))
            weights = jnp.exp(masked - row_top)
            probabilities = low(weights / lax.optimization_barrier(jnp.sum(weights, axis=-1, keepdims=True)))
            return jnp.einsum('hqk,khd->qhd', probabilities, value_block, precision=highest)
        attended = lax.map(jax.checkpoint(attend), starts).reshape(TOKENS, D)
        attended = low(low_back(attended))
        middle = residual + low_back(jnp.dot(attended, attn_low, precision=highest))
        second_norm = low(layer_norm(middle, low_gains[1]))
        expanded = low_back(jnp.dot(second_norm, mlp_low, precision=highest))
        gated_value = low(geglu(expanded))
        return middle + low_back(jnp.dot(gated_value, down_low, precision=highest))
    outcome, backward = jax.vjp(forward, tokens.astype(jnp.float32), qkv_weight, attn_weight, mlp_weight, down_weight, norm_gains)
    input_grad, qkv_grad, attn_grad, mlp_grad, down_grad, gains_grad = backward(cotangent.astype(jnp.float32))
    qkv_first_new, qkv_second_new, qkv_new = adam_update(qkv_weight, qkv_first, qkv_second, qkv_grad, rate_matrix)
    attn_first_new, attn_second_new, attn_new = adam_update(attn_weight, attn_first, attn_second, attn_grad, rate_matrix)
    mlp_first_new, mlp_second_new, mlp_new = adam_update(mlp_weight, mlp_first, mlp_second, mlp_grad, rate_matrix)
    down_first_new, down_second_new, down_new = adam_update(down_weight, down_first, down_second, down_grad, rate_matrix)
    gains_first_new, gains_second_new, gains_new = adam_update(norm_gains, gains_first, gains_second, gains_grad, rate_gains)
    return (outcome.astype(jnp.bfloat16), input_grad.astype(jnp.bfloat16), qkv_first_new, qkv_second_new, qkv_new, attn_first_new, attn_second_new, attn_new, mlp_first_new, mlp_second_new, mlp_new, down_first_new, down_second_new, down_new, gains_first_new, gains_second_new, gains_new)
```

```python
import math

import jax
import jax.numpy as jnp
from jax import lax
from jax.sharding import PartitionSpec as P

HEADS = 12
HALF = 64
ADAM_STEP = 5


norm_epsilon = 1e-05
rope_theta = 10000.0
beta_first = 0.9
beta_second = 0.98
adam_epsilon = 1e-06
decay_rate = 1e-05
rate_matrix = 0.04
rate_gains = 0.2
masked_score = -1e30


def with_halo(cells, sides, width):
    for axis, dim in sides:
        count = lax.axis_size(axis)
        ends = count - 1
        head = lax.slice_in_dim(cells, 0, width, axis=dim)
        tail = lax.slice_in_dim(cells, cells.shape[dim] - width, cells.shape[dim], axis=dim)
        cells = jnp.concatenate(
            [
                lax.ppermute(tail, axis, [(i, (i + 1) % count) for i in range(ends)]),
                cells,
                lax.ppermute(head, axis, [((i + 1) % count, i) for i in range(ends)]),
            ],
            axis=dim,
        )
    return cells


def gather_weight(weight, two_steps):
    count = lax.axis_size("seq")
    low = weight.astype(jnp.bfloat16)
    if weight.shape[0] % count:
        return lax.all_gather(low, "shard", axis=0, tiled=True)
    rows = weight.shape[0] // count
    part = lax.dynamic_slice_in_dim(weight, lax.axis_index("seq") * rows, rows, 0)
    part = part.astype(jnp.bfloat16)
    padded = -(-rows // 8) * 8
    part = jnp.pad(part, ((0, padded - rows), (0, 0)))
    if two_steps:
        part = lax.all_gather(part, "shard", axis=0, tiled=False)
        full = lax.all_gather(part, "seq", axis=1, tiled=False)
    else:
        full = lax.all_gather(part, ("shard", "seq"), axis=0, tiled=False)
    full = full.reshape(-1, padded, weight.shape[1])[:, :rows]
    return full.reshape(-1, weight.shape[1])


def reduce_grad(grad, two_steps):
    count = lax.axis_size("seq")
    shards = lax.axis_size("shard")
    low = grad.astype(jnp.bfloat16)
    if grad.shape[0] % (count * shards):
        owned = lax.psum_scatter(low, "shard", scatter_dimension=0, tiled=True)
        return lax.psum(owned.astype(jnp.float32), "seq")
    rows = grad.shape[0] // (count * shards)
    padded = -(-rows // 8) * 8
    low = jnp.pad(low.reshape(-1, rows, grad.shape[1]), ((0, 0), (0, padded - rows), (0, 0)))
    if two_steps:
        low = low.reshape(shards, count * padded, grad.shape[1])
        owned = lax.psum_scatter(low, "seq", scatter_dimension=1, tiled=True)
        owned = lax.psum_scatter(owned, "shard", scatter_dimension=0, tiled=False)
    else:
        low = low.reshape(-1, grad.shape[1])
        owned = lax.psum_scatter(low, ("shard", "seq"), scatter_dimension=0, tiled=True)
    total = lax.all_gather(owned, "seq", axis=0, tiled=False)
    return total[:, :rows].reshape(-1, grad.shape[1]).astype(jnp.float32)


def reduce_gains(grad):
    total = lax.psum(grad, ("seq", "shard"))
    columns = grad.shape[1] // lax.axis_size("shard")
    return lax.dynamic_slice_in_dim(total, lax.axis_index("shard") * columns, columns, 1)


def from_behind(value, axis, steps):
    count = lax.axis_size(axis)
    first, last = (max(0, -steps), min(count, count - steps))
    return lax.ppermute(value, axis, [(source, source + steps) for source in range(first, last)])


def layer_norm(hidden, gain_row):
    centered = hidden - jnp.mean(hidden, axis=-1, keepdims=True)
    inverse_dev = lax.rsqrt(jnp.mean(centered * centered, axis=-1, keepdims=True) + norm_epsilon)
    return centered * inverse_dev * gain_row


def rope_tables(positions, head_size):
    half_size = head_size // 2
    exponent = jnp.arange(half_size, dtype=jnp.float32) * (2.0 / head_size)
    inverse = rope_theta ** (-exponent)
    angles = positions.astype(jnp.float32)[:, None] * inverse[None, :]
    angles = jnp.concatenate([angles, angles], axis=-1)
    return (jnp.cos(angles)[:, None, :], jnp.sin(angles)[:, None, :])


def rotate_half(values):
    half_size = values.shape[-1] // 2
    return jnp.concatenate([-values[..., half_size:], values[..., :half_size]], axis=-1)


def rotate_back(values):
    half_size = values.shape[-1] // 2
    return jnp.concatenate([values[..., half_size:], -values[..., :half_size]], axis=-1)


def geglu(expanded):
    hidden_size = expanded.shape[-1] // 2
    return jax.nn.gelu(expanded[:, :hidden_size], approximate=False) * expanded[:, hidden_size:]


def adam_update(master, first_moment, second_moment, gradient, step_rate):
    new_first = beta_first * first_moment + (1.0 - beta_first) * gradient
    new_second = beta_second * second_moment + (1.0 - beta_second) * gradient * gradient
    first_hat = new_first / (1.0 - beta_first**ADAM_STEP)
    second_hat = new_second / (1.0 - beta_second**ADAM_STEP)
    new_master = master - step_rate * (
        decay_rate * master + first_hat / (jnp.sqrt(second_hat) + adam_epsilon)
    )
    return (new_first, new_second, new_master)


def allowed_mask(positions, first_row, query_rows, device, last_device):
    local_rows = positions.shape[0]
    padded_positions = jnp.pad(positions, (HALF, HALF))
    query_index = first_row + jnp.arange(query_rows, dtype=jnp.int32)
    key_index = first_row - HALF + jnp.arange(query_rows + 2 * HALF, dtype=jnp.int32)
    query_pos = positions[first_row : first_row + query_rows]
    key_pos = padded_positions[first_row : first_row + query_rows + 2 * HALF]
    distance = query_index[:, None] - key_index[None, :]
    within_reach = jnp.abs(distance) <= HALF
    inside_block = (key_index >= 0) & (key_index < local_rows)
    same_document = query_pos[:, None] - key_pos[None, :] == distance
    left_valid = (key_index < 0) & (device > 0)
    right_valid = (key_index >= local_rows) & (device < last_device)
    return within_reach & (
        inside_block[None, :] & same_document | left_valid[None, :] | right_valid[None, :]
    )


def per_device(
    tokens,
    positions,
    cotangent,
    qkv_weight,
    attn_weight,
    mlp_weight,
    down_weight,
    norm_gains,
    qkv_first,
    qkv_second,
    attn_first,
    attn_second,
    mlp_first,
    mlp_second,
    down_first,
    down_second,
    gains_first,
    gains_second,
):
    full_qkv, full_attn, full_mlp, full_down = (
        gather_weight(qkv_weight, False),
        gather_weight(attn_weight, False),
        gather_weight(mlp_weight, True),
        gather_weight(down_weight, False),
    )
    full_gains = lax.all_gather(norm_gains.astype(jnp.bfloat16), "shard", axis=1, tiled=True)
    local_rows = tokens.shape[0]
    model_width = tokens.shape[1]
    head_size = model_width // HEADS
    score_scale = 1.0 / math.sqrt(head_size)
    block_rows = min(640, local_rows)
    device = lax.axis_index(("seq", "shard"))
    last_device = lax.axis_size(("seq", "shard")) - 1
    gain_attn = full_gains[0].astype(jnp.float32)
    gain_mlp = full_gains[1].astype(jnp.float32)
    residual = tokens.astype(jnp.float32)
    first_norm, first_norm_back = jax.vjp(layer_norm, residual, gain_attn)
    first_low = first_norm.astype(jnp.bfloat16)
    projected = jnp.dot(first_low, full_qkv, preferred_element_type=jnp.float32)
    cos_table, sin_table = rope_tables(positions, head_size)
    queries_raw = projected[:, :model_width].reshape(local_rows, HEADS, head_size)
    keys_raw = projected[:, model_width : 2 * model_width].reshape(local_rows, HEADS, head_size)
    queries = (queries_raw * cos_table + rotate_half(queries_raw) * sin_table).astype(jnp.bfloat16)
    keys_low = (
        (keys_raw * cos_table + rotate_half(keys_raw) * sin_table)
        .astype(jnp.bfloat16)
        .reshape(local_rows, model_width)
    )
    values_low = projected[:, 2 * model_width :].astype(jnp.bfloat16)
    extended = with_halo(
        jnp.concatenate([keys_low, values_low], axis=1), ((("seq", "shard"), 0),), HALF
    )
    ext_keys = extended[:, :model_width].reshape(-1, HEADS, head_size)
    ext_values = extended[:, model_width:].reshape(-1, HEADS, head_size)
    attended_parts = []
    kept_tops = []
    kept_totals = []
    kept_masks = []
    for first_row in range(0, local_rows, block_rows):
        allowed = allowed_mask(positions, first_row, block_rows, device, last_device)
        query_block = queries[first_row : first_row + block_rows]
        key_block = ext_keys[first_row : first_row + block_rows + 2 * HALF]
        value_block = ext_values[first_row : first_row + block_rows + 2 * HALF]
        scores = (
            jnp.einsum("qhd,khd->hqk", query_block, key_block, preferred_element_type=jnp.float32)
            * score_scale
        )
        masked = jnp.where(allowed[None], scores, masked_score)
        row_top = jnp.max(masked, axis=-1, keepdims=True)
        weights = jnp.exp(masked - row_top)
        row_total = jnp.sum(weights, axis=-1, keepdims=True)
        probabilities = (weights / row_total).astype(jnp.bfloat16)
        attended_parts.append(
            jnp.einsum(
                "hqk,khd->qhd", probabilities, value_block, preferred_element_type=jnp.float32
            )
        )
        kept_tops.append(row_top)
        kept_totals.append(row_total)
        kept_masks.append(allowed)
    attended = (
        jnp.concatenate(attended_parts, axis=0)
        .reshape(local_rows, model_width)
        .astype(jnp.bfloat16)
    )
    middle = residual + jnp.dot(attended, full_attn, preferred_element_type=jnp.float32)
    second_norm, second_norm_back = jax.vjp(layer_norm, middle, gain_mlp)
    second_low = second_norm.astype(jnp.bfloat16)
    expanded = jnp.dot(second_low, full_mlp, preferred_element_type=jnp.float32)
    gated_value, gated_back = jax.vjp(geglu, expanded)
    gated_low = gated_value.astype(jnp.bfloat16)
    layer_output = (
        middle + jnp.dot(gated_low, full_down, preferred_element_type=jnp.float32)
    ).astype(jnp.bfloat16)
    grad_output = cotangent.astype(jnp.float32)
    down_grad = jnp.einsum("tf,td->fd", gated_low, cotangent, preferred_element_type=jnp.float32)
    grad_gated = jnp.einsum("td,fd->tf", cotangent, full_down, preferred_element_type=jnp.float32)
    (grad_expanded,) = gated_back(grad_gated)
    expanded_low = grad_expanded.astype(jnp.bfloat16)
    mlp_grad = jnp.einsum("tc,tf->cf", second_low, expanded_low, preferred_element_type=jnp.float32)
    grad_second = jnp.einsum(
        "tf,cf->tc", expanded_low, full_mlp, preferred_element_type=jnp.float32
    )
    grad_middle_norm, gain_mlp_grad = second_norm_back(grad_second)
    grad_middle = grad_output + grad_middle_norm
    middle_low = grad_middle.astype(jnp.bfloat16)
    attn_grad = jnp.einsum("tc,td->cd", attended, middle_low, preferred_element_type=jnp.float32)
    grad_attended = (
        jnp.einsum("td,cd->tc", middle_low, full_attn, preferred_element_type=jnp.float32)
        .astype(jnp.bfloat16)
        .reshape(local_rows, HEADS, head_size)
    )
    ext_grads = jnp.zeros((local_rows + 2 * HALF, 2 * model_width), jnp.float32)
    query_grads = []
    for block_number, first_row in enumerate(range(0, local_rows, block_rows)):
        query_block = queries[first_row : first_row + block_rows]
        key_block = ext_keys[first_row : first_row + block_rows + 2 * HALF]
        value_block = ext_values[first_row : first_row + block_rows + 2 * HALF]
        grad_block = grad_attended[first_row : first_row + block_rows]
        scores = (
            jnp.einsum("qhd,khd->hqk", query_block, key_block, preferred_element_type=jnp.float32)
            * score_scale
        )
        masked = jnp.where(kept_masks[block_number][None], scores, masked_score)
        prob_exact = jnp.exp(masked - kept_tops[block_number]) / kept_totals[block_number]
        prob_low = prob_exact.astype(jnp.bfloat16)
        value_grad = jnp.einsum(
            "hqk,qhd->khd", prob_low, grad_block, preferred_element_type=jnp.float32
        )
        grad_probs = jnp.einsum(
            "qhd,khd->hqk", grad_block, value_block, preferred_element_type=jnp.float32
        )
        inner_sum = jnp.sum(prob_exact * grad_probs, axis=-1, keepdims=True)
        grad_scores = (prob_exact * (grad_probs - inner_sum)).astype(jnp.bfloat16)
        query_grads.append(
            jnp.einsum("hqk,khd->qhd", grad_scores, key_block, preferred_element_type=jnp.float32)
            * score_scale
        )
        key_grad = (
            jnp.einsum("hqk,qhd->khd", grad_scores, query_block, preferred_element_type=jnp.float32)
            * score_scale
        )
        block_grads = jnp.concatenate(
            [key_grad.reshape(-1, model_width), value_grad.reshape(-1, model_width)], axis=1
        )
        ext_grads = ext_grads.at[first_row : first_row + block_rows + 2 * HALF].add(block_grads)
    from_right = from_behind(ext_grads[:HALF].astype(jnp.bfloat16), ("seq", "shard"), -1).astype(
        jnp.float32
    )
    from_left = from_behind(
        ext_grads[local_rows + HALF :].astype(jnp.bfloat16), ("seq", "shard"), 1
    ).astype(jnp.float32)
    own_grads = ext_grads[HALF : HALF + local_rows]
    own_grads = own_grads.at[:HALF].add(from_left)
    own_grads = own_grads.at[local_rows - HALF :].add(from_right)
    key_grad_rot = own_grads[:, :model_width].reshape(local_rows, HEADS, head_size)
    value_grad_all = own_grads[:, model_width:]
    query_grad_rot = jnp.concatenate(query_grads, axis=0)
    query_raw_grad = query_grad_rot * cos_table + rotate_back(query_grad_rot * sin_table)
    key_raw_grad = key_grad_rot * cos_table + rotate_back(key_grad_rot * sin_table)
    projected_grad = jnp.concatenate(
        [
            query_raw_grad.reshape(local_rows, model_width),
            key_raw_grad.reshape(local_rows, model_width),
            value_grad_all,
        ],
        axis=1,
    ).astype(jnp.bfloat16)
    qkv_grad = jnp.einsum(
        "tc,te->ce", first_low, projected_grad, preferred_element_type=jnp.float32
    )
    grad_first = jnp.einsum(
        "te,ce->tc", projected_grad, full_qkv, preferred_element_type=jnp.float32
    )
    grad_residual_norm, gain_attn_grad = first_norm_back(grad_first)
    input_grad = (grad_middle + grad_residual_norm).astype(jnp.bfloat16)
    gains_grad = jnp.stack([gain_attn_grad, gain_mlp_grad])
    down_total = reduce_grad(down_grad, False)
    mlp_total = reduce_grad(mlp_grad, True)
    attn_total = reduce_grad(attn_grad, False)
    qkv_total = reduce_grad(qkv_grad, False)
    gains_total = reduce_gains(gains_grad)
    qkv_first_new, qkv_second_new, qkv_new = adam_update(
        qkv_weight, qkv_first, qkv_second, qkv_total, rate_matrix
    )
    attn_first_new, attn_second_new, attn_new = adam_update(
        attn_weight, attn_first, attn_second, attn_total, rate_matrix
    )
    mlp_first_new, mlp_second_new, mlp_new = adam_update(
        mlp_weight, mlp_first, mlp_second, mlp_total, rate_matrix
    )
    down_first_new, down_second_new, down_new = adam_update(
        down_weight, down_first, down_second, down_total, rate_matrix
    )
    gains_first_new, gains_second_new, gains_new = adam_update(
        norm_gains, gains_first, gains_second, gains_total, rate_gains
    )
    return (
        layer_output,
        input_grad,
        qkv_first_new,
        qkv_second_new,
        qkv_new,
        attn_first_new,
        attn_second_new,
        attn_new,
        mlp_first_new,
        mlp_second_new,
        mlp_new,
        down_first_new,
        down_second_new,
        down_new,
        gains_first_new,
        gains_second_new,
        gains_new,
    )


def solution(mesh):
    return jax.shard_map(
        per_device,
        mesh=mesh,
        in_specs=(
            P(("seq", "shard"), None),
            P(("seq", "shard")),
            P(("seq", "shard"), None),
            P("shard", None),
            P("shard", None),
            P("shard", None),
            P("shard", None),
            P(None, "shard"),
            P("shard", None),
            P("shard", None),
            P("shard", None),
            P("shard", None),
            P("shard", None),
            P("shard", None),
            P("shard", None),
            P("shard", None),
            P(None, "shard"),
            P(None, "shard"),
        ),
        out_specs=(
            P(("seq", "shard"), None),
            P(("seq", "shard"), None),
            P("shard", None),
            P("shard", None),
            P("shard", None),
            P("shard", None),
            P("shard", None),
            P("shard", None),
            P("shard", None),
            P("shard", None),
            P("shard", None),
            P("shard", None),
            P("shard", None),
            P("shard", None),
            P(None, "shard"),
            P(None, "shard"),
            P(None, "shard"),
        ),
        check_vma=False,
    )
```

```python
import functools
import math

import jax
import jax.numpy as jnp
from jax import lax
from jax.experimental import pallas as pl
from jax.experimental.pallas import tpu as pltpu
from jax.sharding import PartitionSpec as P

HEADS = 12
HALF = 64
ADAM_STEP = 5
LANES = 128
ROWS = 128
TILE = 256


norm_epsilon = 1e-05
rope_theta = 10000.0
beta_first = 0.9
beta_second = 0.98
adam_epsilon = 1e-06
decay_rate = 1e-05
rate_matrix = 0.04
rate_gains = 0.2
masked_score = -1e30
vmem_bytes = 60 * 1024 * 1024

f32 = jnp.float32
bf16 = jnp.bfloat16


def swap(value, axis, flip):
    count = lax.axis_size(axis)
    return lax.ppermute(value, axis, [(i, i ^ flip) for i in range(count)])


def spread(part, axis, unit, index, count, dim):
    out = jnp.zeros(part.shape[:dim] + (count,) + part.shape[dim:], part.dtype)
    pieces = [part] + [swap(part, axis, unit * d) for d in range(1, count)]
    for d, piece in enumerate(pieces):
        out = lax.dynamic_update_slice_in_dim(out, jnp.expand_dims(piece, dim), index ^ d, dim)
    return out


def places():
    core = lax.axis_index("seq") % 2
    return core, lax.axis_index("seq") // 2, lax.axis_index("shard")


def by_core(core, own, other):
    return jnp.where(core == 0, own, other), jnp.where(core == 0, other, own)


def split_pays():
    count, shards = lax.axis_size("seq"), lax.axis_size("shard")
    return count in (2, 4, 8) and shards in (1, 2, 4)


def halves(weight, core):
    width = weight.shape[1] // 2
    return lax.dynamic_slice_in_dim(weight, core * width, width, 1)


def gather_parts(block):
    core, quarter, shard = places()
    quarters = lax.axis_size("seq") // 2
    rows = block.shape[0] // quarters
    part = lax.dynamic_slice_in_dim(block, quarter * rows, rows, 0)
    part = spread(part, "shard", 1, shard, lax.axis_size("shard"), 0)
    part = spread(part, "seq", 2, quarter, quarters, 1)
    part = part.reshape(-1, block.shape[1])
    return by_core(core, part, swap(part, "seq", 1))


def gather_weights(qkv, attn, mlp, down):
    qkv, attn, mlp, down = (w.astype(bf16) for w in (qkv, attn, mlp, down))
    if not split_pays():
        return tuple(lax.all_gather(w, "shard", axis=0, tiled=True) for w in (qkv, attn, mlp, down))
    core, _, _ = places()
    full_qkv = jnp.concatenate(gather_parts(halves(qkv, core)), axis=1)
    first, second = gather_parts(
        jnp.concatenate([halves(mlp, core), halves(attn, core)], axis=1)
    )
    width = mlp.shape[1] // 2
    full_mlp = jnp.concatenate([first[:, :width], second[:, :width]], axis=1)
    full_attn = jnp.concatenate([first[:, width:], second[:, width:]], axis=1)
    full_down = jnp.concatenate(gather_parts(halves(down, core)), axis=1)
    return full_qkv, full_attn, full_mlp, full_down


def gather_gains(gains):
    shards = lax.axis_size("shard")
    low = gains.astype(bf16)
    if not split_pays():
        return lax.all_gather(low, "shard", axis=1, tiled=True).astype(f32)
    full = spread(low, "shard", 1, lax.axis_index("shard"), shards, 1)
    return full.reshape(gains.shape[0], -1).astype(f32)


def total_of(pieces):
    total = pieces[0].astype(f32)
    for piece in pieces[1:]:
        total = total + piece.astype(f32)
    return total.astype(bf16)


def reduce_parts(own, other):
    core, quarter, shard = places()
    quarters, shards = lax.axis_size("seq") // 2, lax.axis_size("shard")
    rows = own.shape[0] // (quarters * shards)
    half = total_of([own, swap(other, "seq", 1)]).reshape(shards, quarters, rows, -1)

    def at(value, index, dim):
        return lax.dynamic_index_in_dim(value, index, dim, keepdims=False)

    half = total_of(
        [at(half, quarter, 1)]
        + [swap(at(half, quarter ^ d, 1), "seq", 2 * d) for d in range(1, quarters)]
    )
    half = total_of(
        [at(half, shard, 0)] + [swap(at(half, shard ^ d, 0), "shard", d) for d in range(1, shards)]
    )
    half = spread(half, "seq", 2, quarter, quarters, 0).reshape(quarters * rows, -1)
    return by_core(core, half, swap(half, "seq", 1))


def reduce_whole(grad):
    owned = lax.psum_scatter(grad, "shard", scatter_dimension=0, tiled=True)
    return lax.psum(owned.astype(f32), "seq")


def reduce_pair(grad):
    core, _, _ = places()
    return reduce_parts(halves(grad, core), halves(grad, 1 - core))


def reduce_gains(grad):
    columns = grad.shape[1] // lax.axis_size("shard")
    owned = lax.psum(grad, "seq")
    owned = lax.psum(owned, "shard")
    return lax.dynamic_slice_in_dim(owned, lax.axis_index("shard") * columns, columns, 1)


def to_right(value):
    axes = ("seq", "shard")
    ends = lax.axis_size(axes) - 1
    return lax.ppermute(value, axes, [(i, i + 1) for i in range(ends)])


def to_left(value):
    axes = ("seq", "shard")
    ends = lax.axis_size(axes) - 1
    return lax.ppermute(value, axes, [(i + 1, i) for i in range(ends)])


def normed(hidden):
    centered = hidden - jnp.mean(hidden, axis=-1, keepdims=True)
    inverse = lax.rsqrt(jnp.mean(centered * centered, axis=-1, keepdims=True) + norm_epsilon)
    return centered * inverse, inverse


def normed_back(grad, gain, unit, inverse):
    inner = grad * gain
    mean = jnp.mean(inner, axis=-1, keepdims=True)
    slope = jnp.mean(inner * unit, axis=-1, keepdims=True)
    return inverse * (inner - mean - unit * slope)


def dot(a, b):
    return jnp.dot(a, b, preferred_element_type=f32)


def dot_rows(a, b):
    return lax.dot_general(a, b, (((1,), (1,)), ((), ())), preferred_element_type=f32)


def dot_columns(a, b):
    return lax.dot_general(a, b, (((0,), (0,)), ((), ())), preferred_element_type=f32)


def turned(values):
    lane = lax.broadcasted_iota(jnp.int32, values.shape, 1)
    up = pltpu.roll(values, LANES - 32, 1)
    down = pltpu.roll(values, 32, 1)
    return jnp.where(lane % 64 < 32, up, down)


def rope(values, cos, sin):
    return values * cos + turned(values) * sin


def rope_back(values, cos, sin):
    return values * cos - turned(values) * sin


def mask_bias(meta_ref, block, keys):
    first = block * ROWS
    shape = (keys, ROWS)
    key = lax.broadcasted_iota(jnp.int32, shape, 0) + (first - HALF)
    query = lax.broadcasted_iota(jnp.int32, shape, 1) + first
    start, low, high = meta_ref[0], meta_ref[1], meta_ref[2]
    apart = jnp.abs(query - key) > HALF
    other = (query >= start) != (key >= start)
    outside = (key < low) | (key >= high)
    return jnp.where(apart | other | outside, masked_score, 0.0).astype(f32)


def stacked(values):
    lane = lax.broadcasted_iota(jnp.int32, values.shape, 1)
    zero = jnp.zeros_like(values)
    return jnp.concatenate(
        [jnp.where(lane < 64, values, zero), jnp.where(lane < 64, zero, values)], axis=0
    )


def unstacked(values):
    depth = lax.broadcasted_iota(jnp.int32, (LANES, ROWS), 0)
    return jnp.where(depth < 64, values[:, :ROWS], values[:, ROWS:]).T


def window(block):
    return slice(block * ROWS, block * ROWS + ROWS + 2 * HALF)


def project_kernel(x_ref, gain_ref, w_ref, cos_ref, sin_ref, h_ref, q_ref, k_ref, v_ref):
    unit, _ = normed(x_ref[...].astype(f32))
    low = (unit * gain_ref[0:1, :]).astype(bf16)
    h_ref[...] = low
    width = low.shape[1]
    cos, sin = cos_ref[...], sin_ref[...]
    for ref, at, scale in ((q_ref, 0, 0.125), (k_ref, width, None)):
        out = dot(low, w_ref[:, at : at + width])
        for j in range(0, width, LANES):
            value = rope(out[:, j : j + LANES], cos, sin)
            if scale is not None:
                value = value * scale
            ref[:, j : j + LANES] = value.astype(bf16)
    v_ref[...] = dot(low, w_ref[:, 2 * width :]).astype(bf16)


def fill(dst, left, middle, right):
    rows = middle.shape[0]
    dst[0:HALF, :] = left[...]
    dst[HALF : HALF + rows, :] = middle[...]
    dst[HALF + rows :, :] = right[...]


def attend_kernel(meta_ref, q_ref, k_ref, v_ref, kl_ref, vl_ref, kr_ref, vr_ref, o_ref, lse_ref, kx, vx, bias):
    blocks = q_ref.shape[0] // ROWS

    @pl.when(pl.program_id(0) == 0)
    def _():
        for n in range(blocks):
            bias[n] = mask_bias(meta_ref, n, ROWS + 2 * HALF)

    fill(kx, kl_ref, k_ref, kr_ref)
    fill(vx, vl_ref, v_ref, vr_ref)
    for n in range(blocks):
        own = slice(n * ROWS, (n + 1) * ROWS)
        queries = stacked(q_ref[own, :])
        mask = bias[n]
        scores = dot_rows(kx[window(n), :], queries) + jnp.concatenate([mask, mask], axis=1)
        top = jnp.max(scores, axis=0, keepdims=True)
        weights = jnp.exp(scores - top)
        total = jnp.sum(weights, axis=0, keepdims=True)
        out = dot_columns(vx[window(n), :], weights.astype(bf16)) * (1.0 / total)
        o_ref[own, :] = unstacked(out).astype(bf16)
        lse = top + jnp.log(total)
        lse_ref[0, 0:1, own] = lse[:, :ROWS]
        lse_ref[0, 1:2, own] = lse[:, ROWS:]


def attend_back_kernel(
    meta_ref, q_ref, k_ref, v_ref, do_ref, kl_ref, vl_ref, kr_ref, vr_ref, lse_ref, cos_ref, sin_ref,
    dq_ref, dk_ref, dv_ref, hk_ref, hv_ref, ek_ref, ev_ref,
    kx, vx, bias, dkx, dvx,
):
    rows = q_ref.shape[0]
    blocks = rows // ROWS

    @pl.when(pl.program_id(0) == 0)
    def _():
        for n in range(blocks):
            bias[n] = mask_bias(meta_ref, n, ROWS + 2 * HALF)

    fill(kx, kl_ref, k_ref, kr_ref)
    fill(vx, vl_ref, v_ref, vr_ref)
    dkx[...] = jnp.zeros_like(dkx)
    dvx[...] = jnp.zeros_like(dvx)
    for n in range(blocks):
        own = slice(n * ROWS, (n + 1) * ROWS)
        queries = stacked(q_ref[own, :])
        grads = stacked(do_ref[own, :])
        keys = kx[window(n), :]
        mask = bias[n]
        lse = jnp.concatenate([lse_ref[0, 0:1, own], lse_ref[0, 1:2, own]], axis=1)
        scores = dot_rows(keys, queries) + jnp.concatenate([mask, mask], axis=1)
        probs = jnp.exp(scores - lse)
        grad_probs = dot_rows(vx[window(n), :], grads)
        inner = jnp.sum(probs * grad_probs, axis=0, keepdims=True)
        grad_scores = (probs * (grad_probs - inner)).astype(bf16)
        dvx[window(n), :] += dot(probs.astype(bf16), grads)
        dkx[window(n), :] += dot(grad_scores, queries)
        grad_query = unstacked(dot_columns(keys, grad_scores)) * 0.125
        dq_ref[own, :] = rope_back(grad_query, cos_ref[own, :], sin_ref[own, :]).astype(bf16)
    middle = slice(HALF, HALF + rows)
    dk_ref[...] = rope_back(dkx[middle, :], cos_ref[...], sin_ref[...]).astype(bf16)
    dv_ref[...] = dvx[middle, :].astype(bf16)
    for ref, acc in ((hk_ref, dkx), (hv_ref, dvx)):
        ref[0:HALF, :] = acc[0:HALF, :].astype(bf16)
        ref[HALF:, :] = acc[HALF + rows :, :].astype(bf16)
    for ref, acc in ((ek_ref, dkx), (ev_ref, dvx)):
        ref[0:HALF, :] = acc[HALF : 2 * HALF, :]
        ref[HALF:, :] = acc[rows : rows + HALF, :]


def middle_kernel(
    x_ref, o_ref, ct_ref, gain_ref, wa_ref, wm_ref, wd_ref,
    out_ref, dmid_ref, do_ref, gd_ref, gm_ref, ga_ref, gg_ref,
    acc_d, acc_m, acc_a,
):
    step = pl.program_id(0)

    @pl.when(step == 0)
    def _():
        acc_d[...] = jnp.zeros_like(acc_d)
        acc_m[...] = jnp.zeros_like(acc_m)
        acc_a[...] = jnp.zeros_like(acc_a)
        gg_ref[...] = jnp.zeros_like(gg_ref)

    gain = gain_ref[1:2, :]
    hidden = wd_ref.shape[0]
    ct = ct_ref[...]
    mid = x_ref[...].astype(f32) + dot(o_ref[...], wa_ref[...])
    unit, inverse = normed(mid)
    low = (unit * gain).astype(bf16)
    a1 = dot(low, wm_ref[:, :hidden])
    a2 = dot(low, wm_ref[:, hidden:])
    phi = 0.5 * (1.0 + lax.erf(a1 * (1.0 / math.sqrt(2.0))))
    gate = a1 * phi
    u = (gate * a2).astype(bf16)
    out_ref[...] = (mid + dot(u, wd_ref[...])).astype(bf16)
    acc_d[...] += dot_columns(u, ct)
    du = dot_rows(ct, wd_ref[...])
    slope = phi + a1 * (jnp.exp(-0.5 * a1 * a1) * (1.0 / math.sqrt(2.0 * math.pi)))
    da1 = (du * a2 * slope).astype(bf16)
    da2 = (du * gate).astype(bf16)
    acc_m[:, :hidden] += dot_columns(low, da1)
    acc_m[:, hidden:] += dot_columns(low, da2)
    dh = dot_rows(da1, wm_ref[:, :hidden]) + dot_rows(da2, wm_ref[:, hidden:])
    gg_ref[...] += jnp.sum(dh * unit, axis=0, keepdims=True)
    dmid = ct.astype(f32) + normed_back(dh, gain, unit, inverse)
    dmid_ref[...] = dmid
    dmr = dmid.astype(bf16)
    acc_a[...] += dot_columns(o_ref[...], dmr)
    do_ref[...] = dot_rows(dmr, wa_ref[...]).astype(bf16)

    @pl.when(step == pl.num_programs(0) - 1)
    def _():
        gd_ref[...] = acc_d[...].astype(bf16)
        gm_ref[...] = acc_m[...].astype(bf16)
        ga_ref[...] = acc_a[...].astype(bf16)


def patched(step, steps, rows, value_ref, edge_ref):
    value = value_ref[...]
    edge = edge_ref[...]
    head = jnp.concatenate([edge[:HALF], value[HALF:]], axis=0)
    value = jnp.where(step == 0, head, value)
    tail = jnp.concatenate([value[: rows - HALF], edge[HALF:]], axis=0)
    return jnp.where(step == steps - 1, tail, value)


def qkv_grad_kernel(h_ref, dq_ref, dk_ref, dv_ref, ek_ref, ev_ref, g_ref, acc):
    step, steps = pl.program_id(0), pl.num_programs(0)
    rows, width = h_ref.shape

    @pl.when(step == 0)
    def _():
        acc[...] = jnp.zeros_like(acc)

    low = h_ref[...]
    acc[:, :width] += dot_columns(low, dq_ref[...])
    acc[:, width : 2 * width] += dot_columns(low, patched(step, steps, rows, dk_ref, ek_ref))
    acc[:, 2 * width :] += dot_columns(low, patched(step, steps, rows, dv_ref, ev_ref))

    @pl.when(step == steps - 1)
    def _():
        g_ref[...] = acc[...].astype(bf16)


def input_kernel(x_ref, gain_ref, w_ref, dmid_ref, dq_ref, dk_ref, dv_ref, ek_ref, ev_ref, dx_ref, gg_ref):
    step, steps = pl.program_id(0), pl.num_programs(0)
    rows, width = x_ref.shape

    @pl.when(step == 0)
    def _():
        gg_ref[...] = jnp.zeros_like(gg_ref)

    dh = dot_rows(dq_ref[...], w_ref[:, :width])
    dh = dh + dot_rows(patched(step, steps, rows, dk_ref, ek_ref), w_ref[:, width : 2 * width])
    dh = dh + dot_rows(patched(step, steps, rows, dv_ref, ev_ref), w_ref[:, 2 * width :])
    unit, inverse = normed(x_ref[...].astype(f32))
    gg_ref[...] += jnp.sum(dh * unit, axis=0, keepdims=True)
    dx = dmid_ref[...] + normed_back(dh, gain_ref[0:1, :], unit, inverse)
    dx_ref[...] = dx.astype(bf16)


def shaped(shape, dtype):
    return jax.ShapeDtypeStruct(shape, dtype)


def tiles(rows, columns):
    return pl.BlockSpec((rows, columns), lambda i: (i, 0))


def pairs(rows, offset=0):
    return pl.BlockSpec((rows, LANES), lambda i: (0, i + offset))


def kept(*shape):
    return pl.BlockSpec(shape, lambda i: (0,) * len(shape), pipeline_mode=pl.Buffered(1))


def held(*shape):
    return pl.BlockSpec(shape, lambda i: (0,) * len(shape))


def call(kernel, grid, in_specs, out_specs, out_shape, scratch, flops, moved):
    return pl.pallas_call(
        kernel,
        grid=(grid,),
        in_specs=in_specs,
        out_specs=out_specs,
        out_shape=out_shape,
        scratch_shapes=scratch,
        compiler_params=pltpu.CompilerParams(
            vmem_limit_bytes=vmem_bytes, dimension_semantics=("arbitrary",)
        ),
        cost_estimate=pl.CostEstimate(flops=flops, bytes_accessed=moved, transcendentals=0),
    )


def project(x, gains, weight, cos, sin):
    rows, width = x.shape
    tile = min(TILE, rows)
    return call(
        project_kernel,
        rows // tile,
        [tiles(tile, width), held(2, width), kept(*weight.shape), tiles(tile, LANES), tiles(tile, LANES)],
        [tiles(tile, width)] * 4,
        [shaped((rows, width), bf16)] * 4,
        [],
        2 * rows * width * 3 * width,
        rows * width * 10 + weight.size * 2,
    )(x, gains, weight, cos, sin)


def attend_scratch(rows):
    extended = rows + 2 * HALF
    return [
        pltpu.VMEM((extended, LANES), bf16),
        pltpu.VMEM((extended, LANES), bf16),
        pltpu.VMEM((rows // ROWS, ROWS + 2 * HALF, ROWS), f32),
    ]


def attend(meta, q, k, v, left, right):
    rows, width = q.shape
    steps = width // LANES
    return call(
        attend_kernel,
        steps,
        [pl.BlockSpec(memory_space=pltpu.SMEM)]
        + [pairs(rows)] * 3
        + [pairs(HALF), pairs(HALF, steps)] * 2,
        [pairs(rows), pl.BlockSpec((1, 2, rows), lambda i: (i, 0, 0))],
        [shaped((rows, width), bf16), shaped((steps, 2, rows), f32)],
        attend_scratch(rows),
        8 * rows * width * 256,
        rows * width * 8,
    )(meta, q, k, v, left, left, right, right)


def attend_back(meta, q, k, v, do, left, right, lse, cos, sin):
    rows, width = q.shape
    steps = width // LANES
    extended = rows + 2 * HALF
    return call(
        attend_back_kernel,
        steps,
        [pl.BlockSpec(memory_space=pltpu.SMEM)]
        + [pairs(rows)] * 4
        + [pairs(HALF), pairs(HALF, steps)] * 2
        + [pl.BlockSpec((1, 2, rows), lambda i: (i, 0, 0)), held(rows, LANES), held(rows, LANES)],
        [pairs(rows)] * 3 + [pairs(2 * HALF)] * 4,
        [shaped((rows, width), bf16)] * 3
        + [shaped((2 * HALF, width), bf16)] * 2
        + [shaped((2 * HALF, width), f32)] * 2,
        attend_scratch(rows)
        + [pltpu.VMEM((extended, LANES), f32), pltpu.VMEM((extended, LANES), f32)],
        20 * rows * width * 256,
        rows * width * 14,
    )(meta, q, k, v, do, left, left, right, right, lse, cos, sin)


def middle(x, o, ct, gains, wa, wm, wd):
    rows, width = x.shape
    tile = min(TILE, rows)
    return call(
        middle_kernel,
        rows // tile,
        [tiles(tile, width)] * 3 + [held(2, width), kept(*wa.shape), kept(*wm.shape), kept(*wd.shape)],
        [tiles(tile, width)] * 3 + [held(*wd.shape), held(*wm.shape), held(*wa.shape), held(1, width)],
        [
            shaped((rows, width), bf16),
            shaped((rows, width), f32),
            shaped((rows, width), bf16),
            shaped(wd.shape, bf16),
            shaped(wm.shape, bf16),
            shaped(wa.shape, bf16),
            shaped((1, width), f32),
        ],
        [pltpu.VMEM(wd.shape, f32), pltpu.VMEM(wm.shape, f32), pltpu.VMEM(wa.shape, f32)],
        6 * rows * (wa.size + wm.size + wd.size),
        rows * width * 14 + 4 * (wa.size + wm.size + wd.size),
    )(x, o, ct, gains, wa, wm, wd)


def qkv_gradient(h, dq, dk, dv, ek, ev):
    rows, width = h.shape
    tile = min(TILE, rows)
    return call(
        qkv_grad_kernel,
        rows // tile,
        [tiles(tile, width)] * 4 + [held(2 * HALF, width)] * 2,
        held(width, 3 * width),
        shaped((width, 3 * width), bf16),
        [pltpu.VMEM((width, 3 * width), f32)],
        6 * rows * width * width,
        rows * width * 8 + 6 * width * width,
    )(h, dq, dk, dv, ek, ev)


def input_gradient(x, gains, weight, dmid, dq, dk, dv, ek, ev):
    rows, width = x.shape
    tile = min(TILE, rows)
    return call(
        input_kernel,
        rows // tile,
        [tiles(tile, width), held(2, width), kept(*weight.shape)]
        + [tiles(tile, width)] * 4
        + [held(2 * HALF, width)] * 2,
        [tiles(tile, width), held(1, width)],
        [shaped((rows, width), bf16), shaped((1, width), f32)],
        [],
        6 * rows * width * width,
        rows * width * 14 + 6 * width * width,
    )(x, gains, weight, dmid, dq, dk, dv, ek, ev)


def rope_tables(positions, head_size):
    half_size = head_size // 2
    exponent = jnp.arange(half_size, dtype=f32) * (2.0 / head_size)
    inverse = rope_theta ** (-exponent)
    inverse = jnp.tile(inverse, LANES // half_size)
    angles = positions.astype(f32)[:, None] * inverse[None, :]
    sign = jnp.where(jnp.arange(LANES) % head_size < half_size, -1.0, 1.0).astype(f32)
    return jnp.cos(angles), jnp.sin(angles) * sign


def adam_update(master, first_moment, second_moment, gradient, step_rate):
    gradient = gradient.astype(f32)
    new_first = beta_first * first_moment + (1.0 - beta_first) * gradient
    new_second = beta_second * second_moment + (1.0 - beta_second) * gradient * gradient
    first_hat = new_first / (1.0 - beta_first**ADAM_STEP)
    second_hat = new_second / (1.0 - beta_second**ADAM_STEP)
    new_master = master - step_rate * (
        decay_rate * master + first_hat / (jnp.sqrt(second_hat) + adam_epsilon)
    )
    return (new_first, new_second, new_master)


def edge_rows(value):
    return value[:HALF], value[value.shape[0] - HALF :]


def rope_back_wide(values, cos, sin):
    half = 32
    rows, width = values.shape
    parts = values.reshape(rows, width // (2 * half), 2, half)
    wide_cos = cos[:, None, : 2 * half].reshape(rows, 1, 2, half)
    wide_sin = sin[:, None, : 2 * half].reshape(rows, 1, 2, half)
    return (parts * wide_cos - parts[:, :, ::-1] * wide_sin).reshape(rows, width)


def per_device(
    tokens,
    positions,
    cotangent,
    qkv_weight,
    attn_weight,
    mlp_weight,
    down_weight,
    norm_gains,
    qkv_first,
    qkv_second,
    attn_first,
    attn_second,
    mlp_first,
    mlp_second,
    down_first,
    down_second,
    gains_first,
    gains_second,
):
    rows, width = tokens.shape
    device = lax.axis_index(("seq", "shard"))
    last_device = lax.axis_size(("seq", "shard")) - 1
    full_qkv, full_attn, full_mlp, full_down = gather_weights(
        qkv_weight, attn_weight, mlp_weight, down_weight
    )
    gains = gather_gains(norm_gains)
    cos, sin = rope_tables(positions, width // HEADS)
    start = jnp.max(jnp.where(positions == 0, jnp.arange(rows, dtype=jnp.int32), 0))
    low = jnp.where(device > 0, -HALF, 0)
    high = jnp.where(device < last_device, rows + HALF, rows)
    meta = jnp.stack([start, low, high]).astype(jnp.int32)

    h, q, k, v = project(tokens, gains, full_qkv, cos, sin)
    k_head, k_tail = edge_rows(k)
    v_head, v_tail = edge_rows(v)
    left = to_right(jnp.concatenate([k_tail, v_tail], axis=1))
    right = to_left(jnp.concatenate([k_head, v_head], axis=1))
    o, lse = attend(meta, q, k, v, left, right)
    layer_output, dmid, do, down_grad, mlp_grad, attn_grad, gain_mlp_grad = middle(
        tokens, o, cotangent, gains, full_attn, full_mlp, full_down
    )
    dq, dk, dv, halo_k, halo_v, edge_k, edge_v = attend_back(
        meta, q, k, v, do, left, right, lse, cos, sin
    )
    halo = jnp.concatenate([halo_k, halo_v], axis=1)
    from_right = to_left(halo[:HALF])
    from_left = to_right(halo[HALF:])
    arrived = jnp.concatenate([from_left, from_right], axis=0).astype(f32)
    edge_cos = jnp.concatenate(edge_rows(cos), axis=0)
    edge_sin = jnp.concatenate(edge_rows(sin), axis=0)
    edge_k = rope_back_wide(edge_k + arrived[:, :width], edge_cos, edge_sin).astype(bf16)
    edge_v = (edge_v + arrived[:, width:]).astype(bf16)
    qkv_grad = qkv_gradient(h, dq, dk, dv, edge_k, edge_v)
    input_grad, gain_attn_grad = input_gradient(
        tokens, gains, full_qkv, dmid, dq, dk, dv, edge_k, edge_v
    )
    gains_total = reduce_gains(jnp.concatenate([gain_attn_grad, gain_mlp_grad], axis=0))
    if split_pays():
        core, _, _ = places()
        wide = mlp_weight.shape[1] // 2
        down_total = jnp.concatenate(reduce_pair(down_grad), axis=1)
        own, other = (
            jnp.concatenate([halves(mlp_grad, c), halves(attn_grad, c)], axis=1)
            for c in (core, 1 - core)
        )
        first, second = reduce_parts(own, other)
        mlp_total = jnp.concatenate([first[:, :wide], second[:, :wide]], axis=1)
        attn_total = jnp.concatenate([first[:, wide:], second[:, wide:]], axis=1)
        qkv_total = jnp.concatenate(reduce_pair(qkv_grad), axis=1)
    else:
        down_total, mlp_total, attn_total, qkv_total = (
            reduce_whole(g) for g in (down_grad, mlp_grad, attn_grad, qkv_grad)
        )
    qkv_new = adam_update(qkv_weight, qkv_first, qkv_second, qkv_total, rate_matrix)
    attn_new = adam_update(attn_weight, attn_first, attn_second, attn_total, rate_matrix)
    mlp_new = adam_update(mlp_weight, mlp_first, mlp_second, mlp_total, rate_matrix)
    down_new = adam_update(down_weight, down_first, down_second, down_total, rate_matrix)
    gains_new = adam_update(norm_gains, gains_first, gains_second, gains_total, rate_gains)
    return (layer_output, input_grad, *qkv_new, *attn_new, *mlp_new, *down_new, *gains_new)


def solution(mesh):
    tokens, rows, columns = P(("seq", "shard"), None), P("shard", None), P(None, "shard")
    matrices = (rows,) * 4
    return jax.shard_map(
        per_device,
        mesh=mesh,
        in_specs=(tokens, P(("seq", "shard")), tokens, *matrices, columns)
        + (rows,) * 8
        + (columns,) * 2,
        out_specs=(tokens, tokens) + (rows,) * 12 + (columns,) * 3,
        check_vma=False,
    )
```

```python
import functools
import math

import jax
import jax.numpy as jnp
from jax import lax
from jax.experimental import pallas as pl
from jax.experimental.pallas import tpu as pltpu
from jax.sharding import PartitionSpec as P

HEADS = 12
HALF = 64
ADAM_STEP = 5
LANES = 128
ROWS = 128
TILE = 256


norm_epsilon = 1e-05
rope_theta = 10000.0
beta_first = 0.9
beta_second = 0.98
adam_epsilon = 1e-06
decay_rate = 1e-05
rate_matrix = 0.04
rate_gains = 0.2
masked_score = -1e30
vmem_bytes = 60 * 1024 * 1024

f32 = jnp.float32
bf16 = jnp.bfloat16


def swap(value, axis, flip):
    count = lax.axis_size(axis)
    return lax.ppermute(value, axis, [(i, i ^ flip) for i in range(count)])


def after(value, *others):
    return lax.optimization_barrier((value, *others))[0]


def spread(part, axis, unit, index, count, dim, then=()):
    out = jnp.zeros(part.shape[:dim] + (count,) + part.shape[dim:], part.dtype)
    pieces = [part] + [after(swap(part, axis, unit * d), *then) for d in range(1, count)]
    for d, piece in enumerate(pieces):
        out = lax.dynamic_update_slice_in_dim(out, jnp.expand_dims(piece, dim), index ^ d, dim)
    return out, pieces[1:]


def places():
    core = lax.axis_index("seq") % 2
    return core, lax.axis_index("seq") // 2, lax.axis_index("shard")


def by_core(core, own, other):
    return jnp.where(core == 0, own, other), jnp.where(core == 0, other, own)


def split_pays():
    count, shards = lax.axis_size("seq"), lax.axis_size("shard")
    return count in (2, 4, 8) and shards in (1, 2, 4)


def halves(weight, core):
    width = weight.shape[1] // 2
    return lax.dynamic_slice_in_dim(weight, core * width, width, 1)


def quarter_rows(block):
    quarters = lax.axis_size("seq") // 2
    rows = block.shape[0] // quarters
    return lax.dynamic_slice_in_dim(block, (lax.axis_index("seq") // 2) * rows, rows, 0)


def over_shard(part):
    return spread(part, "shard", 1, lax.axis_index("shard"), lax.axis_size("shard"), 0)


def over_quarters(part, then=()):
    count = lax.axis_size("seq")
    part, _ = spread(part, "seq", 2, lax.axis_index("seq") // 2, count // 2, 1, then)
    return part.reshape(-1, part.shape[-1])


def pack_down(blocks, rows):
    rest = blocks.shape[1] - rows
    second = jnp.pad(blocks[:, rows:], ((0, 0), (0, rows - rest), (0, 0)))
    columns = blocks.shape[2]
    return [blocks[:, :rows].reshape(-1, columns), second.reshape(-1, columns)]


def unpack_down(packed, blocks, rest):
    columns = packed.shape[1] // 2
    packed = packed.reshape(blocks, -1, 2 * columns)
    whole = jnp.concatenate([packed[:, :, :columns], packed[:, :rest, columns:]], axis=1)
    return whole.reshape(-1, columns)


def side_by_side(first, second):
    return jnp.concatenate([first, second], axis=1)


def total_of(pieces):
    total = pieces[0].astype(f32)
    for piece in pieces[1:]:
        total = total + piece.astype(f32)
    return total.astype(bf16)


def keep_half(own, got):
    shards, quarters = lax.axis_size("shard"), lax.axis_size("seq") // 2
    return total_of([own, got]).reshape(shards, quarters, -1, own.shape[1])


def sum_after(parts, *others):
    return total_of(parts[:1] + [after(part, *others) for part in parts[1:]])


def pieces(value, axis, unit, index, count, dim):
    def at(place):
        return lax.dynamic_index_in_dim(value, place, dim, keepdims=False)

    return [at(index)] + [swap(at(index ^ d), axis, unit * d) for d in range(1, count)]


def quarter_pieces(half):
    return pieces(half, "seq", 2, lax.axis_index("seq") // 2, lax.axis_size("seq") // 2, 1)


def shard_pieces(half):
    return pieces(half, "shard", 1, lax.axis_index("shard"), lax.axis_size("shard"), 0)


def owners_half(part, then=()):
    count = lax.axis_size("seq")
    part, _ = spread(part, "seq", 2, lax.axis_index("seq") // 2, count // 2, 0, then)
    return part.reshape(-1, part.shape[-1])


def reduce_whole(grad):
    owned = lax.psum_scatter(grad, "shard", scatter_dimension=0, tiled=True)
    return lax.psum(owned.astype(f32), "seq")


def gain_grad(weight, gradient, gain):
    low = weight.astype(bf16).astype(f32)
    return jnp.sum(low * gradient.astype(f32), axis=1) / gain.astype(bf16).astype(f32)


def to_right(value):
    axes = ("seq", "shard")
    ends = lax.axis_size(axes) - 1
    return lax.ppermute(value, axes, [(i, i + 1) for i in range(ends)])


def to_left(value):
    axes = ("seq", "shard")
    ends = lax.axis_size(axes) - 1
    return lax.ppermute(value, axes, [(i + 1, i) for i in range(ends)])


def normed(hidden):
    centered = hidden - jnp.mean(hidden, axis=-1, keepdims=True)
    inverse = lax.rsqrt(jnp.mean(centered * centered, axis=-1, keepdims=True) + norm_epsilon)
    return centered * inverse, inverse


def normed_back(grad, gain, unit, inverse):
    inner = grad * gain
    mean = jnp.mean(inner, axis=-1, keepdims=True)
    slope = jnp.mean(inner * unit, axis=-1, keepdims=True)
    return inverse * (inner - mean - unit * slope)


def dot(a, b):
    return jnp.dot(a, b, preferred_element_type=f32)


def dot_rows(a, b):
    return lax.dot_general(a, b, (((1,), (1,)), ((), ())), preferred_element_type=f32)


def dot_columns(a, b):
    return lax.dot_general(a, b, (((0,), (0,)), ((), ())), preferred_element_type=f32)


def turned(values):
    lane = lax.broadcasted_iota(jnp.int32, values.shape, 1)
    up = pltpu.roll(values, LANES - 32, 1)
    down = pltpu.roll(values, 32, 1)
    return jnp.where(lane % 64 < 32, up, down)


def rope(values, cos, sin):
    return values * cos + turned(values) * sin


def rope_back(values, cos, sin):
    return values * cos - turned(values) * sin


def mask_bias(meta_ref, block, keys):
    first = block * ROWS
    shape = (keys, ROWS)
    key = lax.broadcasted_iota(jnp.int32, shape, 0) + (first - HALF)
    query = lax.broadcasted_iota(jnp.int32, shape, 1) + first
    start, low, high = meta_ref[0], meta_ref[1], meta_ref[2]
    apart = jnp.abs(query - key) > HALF
    other = (query >= start) != (key >= start)
    outside = (key < low) | (key >= high)
    return jnp.where(apart | other | outside, masked_score, 0.0).astype(f32)


def stacked(values):
    lane = lax.broadcasted_iota(jnp.int32, values.shape, 1)
    zero = jnp.zeros_like(values)
    return jnp.concatenate(
        [jnp.where(lane < 64, values, zero), jnp.where(lane < 64, zero, values)], axis=0
    )


def unstacked(values):
    depth = lax.broadcasted_iota(jnp.int32, (LANES, ROWS), 0)
    return jnp.where(depth < 64, values[:, :ROWS], values[:, ROWS:]).T


def window(block):
    return slice(block * ROWS, block * ROWS + ROWS + 2 * HALF)


def project_kernel(x_ref, gain_ref, w_ref, cos_ref, sin_ref, h_ref, q_ref, k_ref, v_ref):
    unit, _ = normed(x_ref[...].astype(f32))
    low = (unit * gain_ref[0:1, :]).astype(bf16)
    h_ref[...] = low
    width = low.shape[1]
    cos, sin = cos_ref[...], sin_ref[...]
    for ref, at, scale in ((q_ref, 0, 0.125), (k_ref, width, None)):
        out = dot(low, w_ref[:, at : at + width])
        for j in range(0, width, LANES):
            value = rope(out[:, j : j + LANES], cos, sin)
            if scale is not None:
                value = value * scale
            ref[:, j : j + LANES] = value.astype(bf16)
    v_ref[...] = dot(low, w_ref[:, 2 * width :]).astype(bf16)


def project_edges_kernel(x_ref, gain_ref, w_ref, cos_ref, sin_ref, head_ref, tail_ref):
    unit, _ = normed(x_ref[...].astype(f32))
    low = (unit * gain_ref[0:1, :]).astype(bf16)
    width = low.shape[1]
    cos, sin = cos_ref[...], sin_ref[...]
    keys = dot(low, w_ref[:, width : 2 * width])
    for j in range(0, width, LANES):
        value = rope(keys[:, j : j + LANES], cos, sin).astype(bf16)
        head_ref[:, j : j + LANES] = value[:HALF]
        tail_ref[:, j : j + LANES] = value[HALF:]
    values = dot(low, w_ref[:, 2 * width :]).astype(bf16)
    head_ref[:, width:] = values[:HALF]
    tail_ref[:, width:] = values[HALF:]


def fill(dst, left, middle, right):
    rows = middle.shape[0]
    dst[0:HALF, :] = left[...]
    dst[HALF : HALF + rows, :] = middle[...]
    dst[HALF + rows :, :] = right[...]


def attend_kernel(meta_ref, q_ref, k_ref, v_ref, kl_ref, vl_ref, kr_ref, vr_ref, o_ref, lse_ref, kx, vx, bias):
    blocks = q_ref.shape[0] // ROWS

    @pl.when(pl.program_id(0) == 0)
    def _():
        for n in range(blocks):
            bias[n] = mask_bias(meta_ref, n, ROWS + 2 * HALF)

    fill(kx, kl_ref, k_ref, kr_ref)
    fill(vx, vl_ref, v_ref, vr_ref)
    for n in range(blocks):
        own = slice(n * ROWS, (n + 1) * ROWS)
        queries = stacked(q_ref[own, :])
        mask = bias[n]
        scores = dot_rows(kx[window(n), :], queries) + jnp.concatenate([mask, mask], axis=1)
        top = jnp.max(scores, axis=0, keepdims=True)
        weights = jnp.exp(scores - top)
        total = jnp.sum(weights, axis=0, keepdims=True)
        out = dot_columns(vx[window(n), :], weights.astype(bf16)) * (1.0 / total)
        o_ref[own, :] = unstacked(out).astype(bf16)
        lse = top + jnp.log(total)
        lse_ref[0, 0:1, own] = lse[:, :ROWS]
        lse_ref[0, 1:2, own] = lse[:, ROWS:]


def back_blocks(blocks, dq_at, q_ref, do_ref, kx, vx, bias, lse_ref, cos_ref, sin_ref, dq_ref, dkx, dvx):
    for n in blocks:
        own = slice(n * ROWS, (n + 1) * ROWS)
        queries = stacked(q_ref[own, :])
        grads = stacked(do_ref[own, :])
        keys = kx[window(n), :]
        mask = bias[n]
        lse = jnp.concatenate([lse_ref[0, 0:1, own], lse_ref[0, 1:2, own]], axis=1)
        scores = dot_rows(keys, queries) + jnp.concatenate([mask, mask], axis=1)
        probs = jnp.exp(scores - lse)
        grad_probs = dot_rows(vx[window(n), :], grads)
        inner = jnp.sum(probs * grad_probs, axis=0, keepdims=True)
        grad_scores = (probs * (grad_probs - inner)).astype(bf16)
        dvx[window(n), :] += dot(probs.astype(bf16), grads)
        dkx[window(n), :] += dot(grad_scores, queries)
        grad_query = unstacked(dot_columns(keys, grad_scores)) * 0.125
        at = dq_at(n) * ROWS
        dq_ref[at : at + ROWS, :] = rope_back(
            grad_query, cos_ref[own, :], sin_ref[own, :]
        ).astype(bf16)


def attend_back_edges_kernel(
    meta_ref, q_ref, k_ref, v_ref, do_ref, kl_ref, vl_ref, kr_ref, vr_ref, lse_ref, cos_ref, sin_ref,
    dq_ref, wk_ref, wv_ref, hk_ref, hv_ref,
    kx, vx, bias, dkx, dvx,
):
    rows = q_ref.shape[0]
    blocks = rows // ROWS
    span = ROWS + 2 * HALF

    @pl.when(pl.program_id(0) == 0)
    def _():
        for n in (0, blocks - 1):
            bias[n] = mask_bias(meta_ref, n, span)

    fill(kx, kl_ref, k_ref, kr_ref)
    fill(vx, vl_ref, v_ref, vr_ref)
    for acc in (dkx, dvx):
        acc[window(0), :] = jnp.zeros((span, LANES), f32)
        acc[window(blocks - 1), :] = jnp.zeros((span, LANES), f32)
    back_blocks(
        (0, blocks - 1), lambda n: min(n, 1),
        q_ref, do_ref, kx, vx, bias, lse_ref, cos_ref, sin_ref, dq_ref, dkx, dvx,
    )
    for ref, acc in ((wk_ref, dkx), (wv_ref, dvx)):
        ref[:span, :] = acc[window(0), :]
        ref[span:, :] = acc[window(blocks - 1), :]
    for ref, acc in ((hk_ref, dkx), (hv_ref, dvx)):
        ref[0:HALF, :] = acc[0:HALF, :].astype(bf16)
        ref[HALF:, :] = acc[HALF + rows :, :].astype(bf16)


def attend_back_kernel(
    meta_ref, q_ref, k_ref, v_ref, do_ref, kl_ref, vl_ref, kr_ref, vr_ref, lse_ref, cos_ref, sin_ref,
    eq_ref, wk_ref, wv_ref,
    dq_ref, dk_ref, dv_ref,
    kx, vx, bias, dkx, dvx,
):
    rows = q_ref.shape[0]
    blocks = rows // ROWS
    span = ROWS + 2 * HALF

    @pl.when(pl.program_id(0) == 0)
    def _():
        for n in range(1, blocks - 1):
            bias[n] = mask_bias(meta_ref, n, span)

    fill(kx, kl_ref, k_ref, kr_ref)
    fill(vx, vl_ref, v_ref, vr_ref)
    last = window(blocks - 1)
    for acc, ref in ((dkx, wk_ref), (dvx, wv_ref)):
        acc[window(0), :] = ref[:span, :]
        acc[span : last.start, :] = jnp.zeros((last.start - span, LANES), f32)
        acc[last, :] = ref[span:, :]
    dq_ref[:ROWS, :] = eq_ref[:ROWS, :]
    dq_ref[rows - ROWS :, :] = eq_ref[ROWS:, :]
    back_blocks(
        range(1, blocks - 1), lambda n: n,
        q_ref, do_ref, kx, vx, bias, lse_ref, cos_ref, sin_ref, dq_ref, dkx, dvx,
    )
    middle = slice(HALF, HALF + rows)
    dk_ref[...] = rope_back(dkx[middle, :], cos_ref[...], sin_ref[...]).astype(bf16)
    dv_ref[...] = dvx[middle, :].astype(bf16)


def middle_kernel(
    x_ref, o_ref, ct_ref, gain_ref, wa_ref, wm_ref, wd_ref,
    out_ref, dmid_ref, do_ref, gd_ref, gm_ref, ga_ref,
    acc_d, acc_m, acc_a,
):
    step = pl.program_id(0)

    @pl.when(step == 0)
    def _():
        acc_d[...] = jnp.zeros_like(acc_d)
        acc_m[...] = jnp.zeros_like(acc_m)
        acc_a[...] = jnp.zeros_like(acc_a)

    gain = gain_ref[1:2, :]
    hidden = wd_ref.shape[0]
    ct = ct_ref[...]
    mid = x_ref[...].astype(f32) + dot(o_ref[...], wa_ref[...])
    unit, inverse = normed(mid)
    low = (unit * gain).astype(bf16)
    a1 = dot(low, wm_ref[:, :hidden])
    a2 = dot(low, wm_ref[:, hidden:])
    phi = 0.5 * (1.0 + lax.erf(a1 * (1.0 / math.sqrt(2.0))))
    gate = a1 * phi
    u = (gate * a2).astype(bf16)
    out_ref[...] = (mid + dot(u, wd_ref[...])).astype(bf16)
    acc_d[...] += dot_columns(u, ct)
    du = dot_rows(ct, wd_ref[...])
    slope = phi + a1 * (jnp.exp(-0.5 * a1 * a1) * (1.0 / math.sqrt(2.0 * math.pi)))
    da1 = (du * a2 * slope).astype(bf16)
    da2 = (du * gate).astype(bf16)
    acc_m[:, :hidden] += dot_columns(low, da1)
    acc_m[:, hidden:] += dot_columns(low, da2)
    dh = dot_rows(da1, wm_ref[:, :hidden]) + dot_rows(da2, wm_ref[:, hidden:])
    dmid = ct.astype(f32) + normed_back(dh, gain, unit, inverse)
    dmid_ref[...] = dmid
    dmr = dmid.astype(bf16)
    acc_a[...] += dot_columns(o_ref[...], dmr)
    do_ref[...] = dot_rows(dmr, wa_ref[...]).astype(bf16)

    @pl.when(step == pl.num_programs(0) - 1)
    def _():
        gd_ref[...] = acc_d[...].astype(bf16)
        gm_ref[...] = acc_m[...].astype(bf16)
        ga_ref[...] = acc_a[...].astype(bf16)


def patched(step, steps, rows, value_ref, edge_ref):
    value = value_ref[...]
    edge = edge_ref[...]
    head = jnp.concatenate([edge[:HALF], value[HALF:]], axis=0)
    value = jnp.where(step == 0, head, value)
    tail = jnp.concatenate([value[: rows - HALF], edge[HALF:]], axis=0)
    return jnp.where(step == steps - 1, tail, value)


def qkv_grad_kernel(h_ref, dq_ref, dk_ref, dv_ref, ek_ref, ev_ref, g_ref, acc):
    step, steps = pl.program_id(0), pl.num_programs(0)
    rows, width = h_ref.shape

    @pl.when(step == 0)
    def _():
        acc[...] = jnp.zeros_like(acc)

    low = h_ref[...]
    acc[:, :width] += dot_columns(low, dq_ref[...])
    acc[:, width : 2 * width] += dot_columns(low, patched(step, steps, rows, dk_ref, ek_ref))
    acc[:, 2 * width :] += dot_columns(low, patched(step, steps, rows, dv_ref, ev_ref))

    @pl.when(step == steps - 1)
    def _():
        g_ref[...] = acc[...].astype(bf16)


def input_kernel(x_ref, gain_ref, w_ref, dmid_ref, dq_ref, dk_ref, dv_ref, ek_ref, ev_ref, dx_ref):
    step, steps = pl.program_id(0), pl.num_programs(0)
    rows, width = x_ref.shape

    dh = dot_rows(dq_ref[...], w_ref[:, :width])
    dh = dh + dot_rows(patched(step, steps, rows, dk_ref, ek_ref), w_ref[:, width : 2 * width])
    dh = dh + dot_rows(patched(step, steps, rows, dv_ref, ev_ref), w_ref[:, 2 * width :])
    unit, inverse = normed(x_ref[...].astype(f32))
    dx = dmid_ref[...] + normed_back(dh, gain_ref[0:1, :], unit, inverse)
    dx_ref[...] = dx.astype(bf16)


def shaped(shape, dtype):
    return jax.ShapeDtypeStruct(shape, dtype)


def tiles(rows, columns):
    return pl.BlockSpec((rows, columns), lambda i: (i, 0))


def pairs(rows, offset=0):
    return pl.BlockSpec((rows, LANES), lambda i: (0, i + offset))


def kept(*shape):
    return pl.BlockSpec(shape, lambda i: (0,) * len(shape), pipeline_mode=pl.Buffered(1))


def held(*shape):
    return pl.BlockSpec(shape, lambda i: (0,) * len(shape))


def call(kernel, grid, in_specs, out_specs, out_shape, scratch, flops, moved):
    return pl.pallas_call(
        kernel,
        grid=(grid,),
        in_specs=in_specs,
        out_specs=out_specs,
        out_shape=out_shape,
        scratch_shapes=scratch,
        compiler_params=pltpu.CompilerParams(
            vmem_limit_bytes=vmem_bytes, dimension_semantics=("arbitrary",)
        ),
        cost_estimate=pl.CostEstimate(
            flops=flops // 8, bytes_accessed=moved // 8, transcendentals=0
        ),
    )


def project(x, gains, weight, cos, sin):
    rows, width = x.shape
    tile = min(TILE, rows)
    return call(
        project_kernel,
        rows // tile,
        [tiles(tile, width), held(2, width), kept(*weight.shape), tiles(tile, LANES), tiles(tile, LANES)],
        [tiles(tile, width)] * 4,
        [shaped((rows, width), bf16)] * 4,
        [],
        2 * rows * width * 3 * width,
        rows * width * 10 + weight.size * 2,
    )(x, gains, weight, cos, sin)


def project_edges(x, gains, weight, cos, sin):
    rows, width = x.shape
    return call(
        project_edges_kernel,
        1,
        [held(rows, width), held(2, width), kept(*weight.shape), held(rows, LANES), held(rows, LANES)],
        [held(HALF, 2 * width)] * 2,
        [shaped((HALF, 2 * width), bf16)] * 2,
        [],
        4 * rows * width * width,
        rows * width * 6 + weight.size * 2,
    )(x, gains, weight, cos, sin)


def attend_scratch(rows):
    extended = rows + 2 * HALF
    return [
        pltpu.VMEM((extended, LANES), bf16),
        pltpu.VMEM((extended, LANES), bf16),
        pltpu.VMEM((rows // ROWS, ROWS + 2 * HALF, ROWS), f32),
    ]


def attend(meta, q, k, v, left, right):
    rows, width = q.shape
    steps = width // LANES
    return call(
        attend_kernel,
        steps,
        [pl.BlockSpec(memory_space=pltpu.SMEM)]
        + [pairs(rows)] * 3
        + [pairs(HALF), pairs(HALF, steps)] * 2,
        [pairs(rows), pl.BlockSpec((1, 2, rows), lambda i: (i, 0, 0))],
        [shaped((rows, width), bf16), shaped((steps, 2, rows), f32)],
        attend_scratch(rows),
        8 * rows * width * 256,
        rows * width * 8,
    )(meta, q, k, v, left, left, right, right)


def back_specs(rows, steps):
    return (
        [pl.BlockSpec(memory_space=pltpu.SMEM)]
        + [pairs(rows)] * 4
        + [pairs(HALF), pairs(HALF, steps)] * 2
        + [pl.BlockSpec((1, 2, rows), lambda i: (i, 0, 0)), held(rows, LANES), held(rows, LANES)]
    )


def back_scratch(rows):
    extended = rows + 2 * HALF
    return attend_scratch(rows) + [pltpu.VMEM((extended, LANES), f32)] * 2


def attend_back_edges(meta, q, k, v, do, left, right, lse, cos, sin):
    rows, width = q.shape
    steps = width // LANES
    span = 2 * (ROWS + 2 * HALF)
    return call(
        attend_back_edges_kernel,
        steps,
        back_specs(rows, steps),
        [pairs(2 * ROWS)] + [pairs(span)] * 2 + [pairs(2 * HALF)] * 2,
        [shaped((2 * ROWS, width), bf16)]
        + [shaped((span, width), f32)] * 2
        + [shaped((2 * HALF, width), bf16)] * 2,
        back_scratch(rows),
        20 * 2 * ROWS * width * 256,
        rows * width * 10,
    )(meta, q, k, v, do, left, left, right, right, lse, cos, sin)


def attend_back(meta, q, k, v, do, left, right, lse, cos, sin, edges):
    rows, width = q.shape
    steps = width // LANES
    span = 2 * (ROWS + 2 * HALF)
    return call(
        attend_back_kernel,
        steps,
        back_specs(rows, steps) + [pairs(2 * ROWS)] + [pairs(span)] * 2,
        [pairs(rows)] * 3,
        [shaped((rows, width), bf16)] * 3,
        back_scratch(rows),
        20 * rows * width * 256,
        rows * width * 14,
    )(meta, q, k, v, do, left, left, right, right, lse, cos, sin, *edges)


def middle(x, o, ct, gains, wa, wm, wd):
    rows, width = x.shape
    tile = min(TILE, rows)
    return call(
        middle_kernel,
        rows // tile,
        [tiles(tile, width)] * 3 + [held(2, width), kept(*wa.shape), kept(*wm.shape), kept(*wd.shape)],
        [tiles(tile, width)] * 3 + [held(*wd.shape), held(*wm.shape), held(*wa.shape)],
        [
            shaped((rows, width), bf16),
            shaped((rows, width), f32),
            shaped((rows, width), bf16),
            shaped(wd.shape, bf16),
            shaped(wm.shape, bf16),
            shaped(wa.shape, bf16),
        ],
        [pltpu.VMEM(wd.shape, f32), pltpu.VMEM(wm.shape, f32), pltpu.VMEM(wa.shape, f32)],
        6 * rows * (wa.size + wm.size + wd.size),
        rows * width * 14 + 4 * (wa.size + wm.size + wd.size),
    )(x, o, ct, gains, wa, wm, wd)


def qkv_gradient(h, dq, dk, dv, ek, ev):
    rows, width = h.shape
    tile = min(TILE, rows)
    return call(
        qkv_grad_kernel,
        rows // tile,
        [tiles(tile, width)] * 4 + [held(2 * HALF, width)] * 2,
        held(width, 3 * width),
        shaped((width, 3 * width), bf16),
        [pltpu.VMEM((width, 3 * width), f32)],
        6 * rows * width * width,
        rows * width * 8 + 6 * width * width,
    )(h, dq, dk, dv, ek, ev)


def input_gradient(x, gains, weight, dmid, dq, dk, dv, ek, ev):
    rows, width = x.shape
    tile = min(TILE, rows)
    return call(
        input_kernel,
        rows // tile,
        [tiles(tile, width), held(2, width), kept(*weight.shape)]
        + [tiles(tile, width)] * 4
        + [held(2 * HALF, width)] * 2,
        tiles(tile, width),
        shaped((rows, width), bf16),
        [],
        6 * rows * width * width,
        rows * width * 14 + 6 * width * width,
    )(x, gains, weight, dmid, dq, dk, dv, ek, ev)


def rope_tables(positions, head_size):
    half_size = head_size // 2
    exponent = jnp.arange(half_size, dtype=f32) * (2.0 / head_size)
    inverse = rope_theta ** (-exponent)
    inverse = jnp.tile(inverse, LANES // half_size)
    angles = positions.astype(f32)[:, None] * inverse[None, :]
    sign = jnp.where(jnp.arange(LANES) % head_size < half_size, -1.0, 1.0).astype(f32)
    return jnp.cos(angles), jnp.sin(angles) * sign


def adam_update(master, first_moment, second_moment, gradient, step_rate):
    gradient = gradient.astype(f32)
    new_first = beta_first * first_moment + (1.0 - beta_first) * gradient
    new_second = beta_second * second_moment + (1.0 - beta_second) * gradient * gradient
    first_hat = new_first / (1.0 - beta_first**ADAM_STEP)
    second_hat = new_second / (1.0 - beta_second**ADAM_STEP)
    new_master = master - step_rate * (
        decay_rate * master + first_hat / (jnp.sqrt(second_hat) + adam_epsilon)
    )
    return (new_first, new_second, new_master)


def edge_rows(value):
    return value[:HALF], value[value.shape[0] - HALF :]


def rope_back_wide(values, cos, sin):
    half = 32
    rows, width = values.shape
    parts = values.reshape(rows, width // (2 * half), 2, half)
    wide_cos = cos[:, None, : 2 * half].reshape(rows, 1, 2, half)
    wide_sin = sin[:, None, : 2 * half].reshape(rows, 1, 2, half)
    return (parts * wide_cos - parts[:, :, ::-1] * wide_sin).reshape(rows, width)


def per_device(
    tokens,
    positions,
    cotangent,
    qkv_weight,
    attn_weight,
    mlp_weight,
    down_weight,
    norm_gains,
    qkv_first,
    qkv_second,
    attn_first,
    attn_second,
    mlp_first,
    mlp_second,
    down_first,
    down_second,
    gains_first,
    gains_second,
):
    rows, width = tokens.shape
    device = lax.axis_index(("seq", "shard"))
    last_device = lax.axis_size(("seq", "shard")) - 1
    cos, sin = rope_tables(positions, width // HEADS)
    start = jnp.max(jnp.where(positions == 0, jnp.arange(rows, dtype=jnp.int32), 0))
    low = jnp.where(device > 0, -HALF, 0)
    high = jnp.where(device < last_device, rows + HALF, rows)
    meta = jnp.stack([start, low, high]).astype(jnp.int32)
    shards = lax.axis_size("shard")
    quarters = lax.axis_size("seq") // 2
    core = lax.axis_index("seq") % 2
    split = split_pays()
    half = qkv_weight.shape[1] // 2
    slot = qkv_weight.shape[0] // quarters
    rest = down_weight.shape[0] // quarters - slot
    wide = mlp_weight.shape[1] // 2
    down_at = wide + attn_weight.shape[1] // 2
    lows = [w.astype(bf16) for w in (qkv_weight, attn_weight, mlp_weight, down_weight)]
    if split:
        qkv_low, attn_low, mlp_low, down_low = lows
        part = quarter_rows(halves(qkv_low, core))
        gain_rows = jnp.pad(norm_gains.astype(bf16), ((0, 6), (0, half - norm_gains.shape[1])))
        qkv_part, arrived = over_shard(jnp.concatenate([part, gain_rows], axis=0))
        gains = qkv_part[:, slot : slot + 2, : norm_gains.shape[1]].astype(f32)
        gains = gains.transpose(1, 0, 2).reshape(2, -1)
        down_part = quarter_rows(halves(down_low, core))
        rest_part = jnp.concatenate(
            [quarter_rows(halves(w, core)) for w in (mlp_low, attn_low)]
            + pack_down(down_part[None], slot),
            axis=1,
        )
        rest_part, _ = over_shard(after(rest_part, *arrived[:1]))
        qkv_part = over_quarters(qkv_part[:, :slot])
        rest_part = after(rest_part, qkv_part)
        full_qkv = side_by_side(*by_core(core, qkv_part, swap(qkv_part, "seq", 1)))
    else:
        full_qkv, full_attn, full_mlp, full_down = (
            lax.all_gather(w, "shard", axis=0, tiled=True) for w in lows
        )
        gains = lax.all_gather(norm_gains.astype(bf16), "shard", axis=1, tiled=True).astype(f32)
    edge_x, edge_cos, edge_sin = (
        jnp.concatenate(edge_rows(value), axis=0) for value in (tokens, cos, sin)
    )
    kv_head, kv_tail = project_edges(edge_x, gains, full_qkv, edge_cos, edge_sin)
    left = to_right(kv_tail)
    right = to_left(kv_head)
    h, q, k, v = project(after(tokens, kv_head), gains, full_qkv, cos, sin)
    left = after(left, k)
    right = after(right, k)
    o, lse = attend(meta, q, k, v, left, right)
    if split:
        rest_part = over_quarters(rest_part, (o,))
    if split:
        first, second = by_core(core, rest_part, swap(rest_part, "seq", 1))
        full_mlp = side_by_side(first[:, :wide], second[:, :wide])
        full_attn = side_by_side(first[:, wide:down_at], second[:, wide:down_at])
        full_down = side_by_side(
            *(unpack_down(x[:, down_at:], shards * quarters, rest) for x in (first, second))
        )
    layer_output, dmid, do, down_grad, mlp_grad, attn_grad = middle(
        tokens, o, cotangent, gains, full_attn, full_mlp, full_down
    )
    if split:

        def packed(c):
            down = halves(down_grad, c).reshape(shards * quarters, slot + rest, -1)
            return jnp.concatenate(
                [halves(mlp_grad, c), halves(attn_grad, c)] + pack_down(down, slot), axis=1
            )

        rest_got = swap(packed(1 - core), "seq", 1)
    back_args = (meta, q, k, v, do, left, right, lse, cos, sin)
    *edges, halo_k, halo_v = attend_back_edges(*back_args)
    halo = side_by_side(halo_k, halo_v)
    from_right = to_left(halo[:HALF])
    from_left = to_right(halo[HALF:])
    if split:
        rest_half = keep_half(packed(core), after(rest_got, halo_k))
        do = after(do, rest_half)
        back_args = (meta, q, k, v, do, left, right, lse, cos, sin)
        rest_pieces = quarter_pieces(rest_half)
    dq, dk, dv = attend_back(*back_args, edges)
    arrived = jnp.concatenate([after(from_left, dq), after(from_right, dq)], axis=0).astype(f32)
    _, window_k, window_v = edges
    span = ROWS + 2 * HALF

    def own_edges(windows):
        return jnp.concatenate(
            [windows[HALF : 2 * HALF], windows[2 * span - 2 * HALF : 2 * span - HALF]], axis=0
        )

    edge_k = rope_back_wide(
        own_edges(window_k) + arrived[:, :width], edge_cos, edge_sin
    ).astype(bf16)
    edge_v = (own_edges(window_v) + arrived[:, width:]).astype(bf16)
    qkv_grad = qkv_gradient(h, dq, dk, dv, edge_k, edge_v)
    if split:
        rest_part = sum_after(rest_pieces, qkv_grad)
        qkv_got = swap(after(halves(qkv_grad, 1 - core), rest_part), "seq", 1)
        qkv_half = keep_half(halves(qkv_grad, core), qkv_got)
        dq = after(dq, qkv_half)
        qkv_pieces = quarter_pieces(qkv_half)
        rest_pieces = shard_pieces(rest_part)
    input_grad = input_gradient(tokens, gains, full_qkv, dmid, dq, dk, dv, edge_k, edge_v)
    if split:
        qkv_part = sum_after(qkv_pieces, input_grad)
        rest_part = sum_after(rest_pieces, qkv_part)
        qkv_part = sum_after(shard_pieces(qkv_part), rest_part)
        rest_half = owners_half(rest_part, (qkv_part,))
        rest_got = swap(rest_half, "seq", 1)
        qkv_half = owners_half(qkv_part, (rest_half,))
        qkv_got = swap(qkv_half, "seq", 1)
        first, second = by_core(core, rest_half, after(rest_got, qkv_half))
        mlp_total = side_by_side(first[:, :wide], second[:, :wide])
        attn_total = side_by_side(first[:, wide:down_at], second[:, wide:down_at])
        down_total = side_by_side(
            *(unpack_down(x[:, down_at:], quarters, rest) for x in (first, second))
        )
        qkv_total = side_by_side(*by_core(core, qkv_half, qkv_got))
    else:
        down_total, mlp_total, attn_total, qkv_total = (
            reduce_whole(g) for g in (down_grad, mlp_grad, attn_grad, qkv_grad)
        )
    gains_total = jnp.stack(
        [
            gain_grad(qkv_weight, qkv_total, norm_gains[0]),
            gain_grad(mlp_weight, mlp_total, norm_gains[1]),
        ]
    )
    qkv_new = adam_update(qkv_weight, qkv_first, qkv_second, qkv_total, rate_matrix)
    attn_new = adam_update(attn_weight, attn_first, attn_second, attn_total, rate_matrix)
    mlp_new = adam_update(mlp_weight, mlp_first, mlp_second, mlp_total, rate_matrix)
    down_new = adam_update(down_weight, down_first, down_second, down_total, rate_matrix)
    gains_new = adam_update(norm_gains, gains_first, gains_second, gains_total, rate_gains)
    return (layer_output, input_grad, *qkv_new, *attn_new, *mlp_new, *down_new, *gains_new)


def solution(mesh):
    tokens, rows, columns = P(("seq", "shard"), None), P("shard", None), P(None, "shard")
    matrices = (rows,) * 4
    return jax.shard_map(
        per_device,
        mesh=mesh,
        in_specs=(tokens, P(("seq", "shard")), tokens, *matrices, columns)
        + (rows,) * 8
        + (columns,) * 2,
        out_specs=(tokens, tokens) + (rows,) * 12 + (columns,) * 3,
        check_vma=False,
    )
```

```python
import functools
import math

import jax
import jax.numpy as jnp
from jax import lax
from jax.experimental import pallas as pl
from jax.experimental.pallas import tpu as pltpu
from jax.sharding import PartitionSpec as P

HEADS = 12
HALF = 64
ADAM_STEP = 5
LANES = 128
ROWS = 128
TILE = 256


norm_epsilon = 1e-05
rope_theta = 10000.0
beta_first = 0.9
beta_second = 0.98
adam_epsilon = 1e-06
decay_rate = 1e-05
rate_matrix = 0.04
rate_gains = 0.2
masked_score = -1e30
vmem_bytes = 60 * 1024 * 1024

f32 = jnp.float32
bf16 = jnp.bfloat16


def swap(value, axis, flip):
    count = lax.axis_size(axis)
    return lax.ppermute(value, axis, [(i, i ^ flip) for i in range(count)])


def after(value, *others):
    return lax.optimization_barrier((value, *others))[0]


def spread(part, axis, unit, index, count, dim, then=()):
    out = jnp.zeros(part.shape[:dim] + (count,) + part.shape[dim:], part.dtype)
    pieces = [part] + [after(swap(part, axis, unit * d), *then) for d in range(1, count)]
    for d, piece in enumerate(pieces):
        out = lax.dynamic_update_slice_in_dim(out, jnp.expand_dims(piece, dim), index ^ d, dim)
    return out, pieces[1:]


def places():
    core = lax.axis_index("seq") % 2
    return core, lax.axis_index("seq") // 2, lax.axis_index("shard")


def by_core(core, own, other):
    return jnp.where(core == 0, own, other), jnp.where(core == 0, other, own)


def split_pays():
    count, shards = lax.axis_size("seq"), lax.axis_size("shard")
    return count in (2, 4, 8) and shards in (1, 2, 4)


def halves(weight, core):
    width = weight.shape[1] // 2
    return lax.dynamic_slice_in_dim(weight, core * width, width, 1)


def quarter_rows(block):
    quarters = lax.axis_size("seq") // 2
    rows = block.shape[0] // quarters
    return lax.dynamic_slice_in_dim(block, (lax.axis_index("seq") // 2) * rows, rows, 0)


def over_shard(part):
    return spread(part, "shard", 1, lax.axis_index("shard"), lax.axis_size("shard"), 0)


def over_quarters(part, then=()):
    count = lax.axis_size("seq")
    part, _ = spread(part, "seq", 2, lax.axis_index("seq") // 2, count // 2, 1, then)
    return part.reshape(-1, part.shape[-1])


def pack_down(blocks, rows):
    rest = blocks.shape[1] - rows
    second = jnp.pad(blocks[:, rows:], ((0, 0), (0, rows - rest), (0, 0)))
    columns = blocks.shape[2]
    return [blocks[:, :rows].reshape(-1, columns), second.reshape(-1, columns)]


def unpack_down(packed, blocks, rest):
    columns = packed.shape[1] // 2
    packed = packed.reshape(blocks, -1, 2 * columns)
    whole = jnp.concatenate([packed[:, :, :columns], packed[:, :rest, columns:]], axis=1)
    return whole.reshape(-1, columns)


def side_by_side(first, second):
    return jnp.concatenate([first, second], axis=1)


def total_of(pieces):
    total = pieces[0].astype(f32)
    for piece in pieces[1:]:
        total = total + piece.astype(f32)
    return total.astype(bf16)


def keep_half(own, got):
    shards, quarters = lax.axis_size("shard"), lax.axis_size("seq") // 2
    return total_of([own, got]).reshape(shards, quarters, -1, own.shape[1])


def sum_after(parts, *others):
    return total_of(parts[:1] + [after(part, *others) for part in parts[1:]])


def pieces(value, axis, unit, index, count, dim):
    def at(place):
        return lax.dynamic_index_in_dim(value, place, dim, keepdims=False)

    return [at(index)] + [swap(at(index ^ d), axis, unit * d) for d in range(1, count)]


def quarter_pieces(half):
    return pieces(half, "seq", 2, lax.axis_index("seq") // 2, lax.axis_size("seq") // 2, 1)


def shard_pieces(half):
    return pieces(half, "shard", 1, lax.axis_index("shard"), lax.axis_size("shard"), 0)


def owners_half(part, then=()):
    count = lax.axis_size("seq")
    part, _ = spread(part, "seq", 2, lax.axis_index("seq") // 2, count // 2, 0, then)
    return part.reshape(-1, part.shape[-1])


def reduce_whole(grad):
    owned = lax.psum_scatter(grad, "shard", scatter_dimension=0, tiled=True)
    return lax.psum(owned.astype(f32), "seq")


def gain_grad(weight, gradient, gain):
    low = weight.astype(bf16).astype(f32)
    return jnp.sum(low * gradient.astype(f32), axis=1) / gain.astype(bf16).astype(f32)


def to_right(value):
    axes = ("seq", "shard")
    ends = lax.axis_size(axes) - 1
    return lax.ppermute(value, axes, [(i, i + 1) for i in range(ends)])


def to_left(value):
    axes = ("seq", "shard")
    ends = lax.axis_size(axes) - 1
    return lax.ppermute(value, axes, [(i + 1, i) for i in range(ends)])


def normed(hidden):
    centered = hidden - jnp.mean(hidden, axis=-1, keepdims=True)
    inverse = lax.rsqrt(jnp.mean(centered * centered, axis=-1, keepdims=True) + norm_epsilon)
    return centered * inverse, inverse


def normed_back(grad, gain, unit, inverse):
    inner = grad * gain
    mean = jnp.mean(inner, axis=-1, keepdims=True)
    slope = jnp.mean(inner * unit, axis=-1, keepdims=True)
    return inverse * (inner - mean - unit * slope)


def dot(a, b):
    return jnp.dot(a, b, preferred_element_type=f32)


def dot_rows(a, b):
    return lax.dot_general(a, b, (((1,), (1,)), ((), ())), preferred_element_type=f32)


def dot_columns(a, b):
    return lax.dot_general(a, b, (((0,), (0,)), ((), ())), preferred_element_type=f32)


def turned(values):
    lane = lax.broadcasted_iota(jnp.int32, values.shape, 1)
    up = pltpu.roll(values, LANES - 32, 1)
    down = pltpu.roll(values, 32, 1)
    return jnp.where(lane % 64 < 32, up, down)


def rope(values, cos, sin):
    return values * cos + turned(values) * sin


def rope_back(values, cos, sin):
    return values * cos - turned(values) * sin


def mask_bias(meta_ref, block, keys):
    first = block * ROWS
    shape = (keys, ROWS)
    key = lax.broadcasted_iota(jnp.int32, shape, 0) + (first - HALF)
    query = lax.broadcasted_iota(jnp.int32, shape, 1) + first
    start, low, high = meta_ref[0], meta_ref[1], meta_ref[2]
    apart = jnp.abs(query - key) > HALF
    other = (query >= start) != (key >= start)
    outside = (key < low) | (key >= high)
    return jnp.where(apart | other | outside, masked_score, 0.0).astype(f32)


def stacked(values):
    lane = lax.broadcasted_iota(jnp.int32, values.shape, 1)
    zero = jnp.zeros_like(values)
    return jnp.concatenate(
        [jnp.where(lane < 64, values, zero), jnp.where(lane < 64, zero, values)], axis=0
    )


def unstacked(values):
    depth = lax.broadcasted_iota(jnp.int32, (LANES, ROWS), 0)
    return jnp.where(depth < 64, values[:, :ROWS], values[:, ROWS:]).T


def window(block):
    return slice(block * ROWS, block * ROWS + ROWS + 2 * HALF)


def project_kernel(x_ref, gain_ref, w_ref, cos_ref, sin_ref, h_ref, q_ref, k_ref, v_ref):
    unit, _ = normed(x_ref[...].astype(f32))
    low = (unit * gain_ref[0:1, :]).astype(bf16)
    h_ref[...] = low
    width = low.shape[1]
    cos, sin = cos_ref[...], sin_ref[...]
    for ref, at, scale in ((q_ref, 0, 0.125), (k_ref, width, None)):
        out = dot(low, w_ref[:, at : at + width])
        for j in range(0, width, LANES):
            value = rope(out[:, j : j + LANES], cos, sin)
            if scale is not None:
                value = value * scale
            ref[:, j : j + LANES] = value.astype(bf16)
    v_ref[...] = dot(low, w_ref[:, 2 * width :]).astype(bf16)


def project_edges_kernel(x_ref, gain_ref, w_ref, cos_ref, sin_ref, head_ref, tail_ref):
    unit, _ = normed(x_ref[...].astype(f32))
    low = (unit * gain_ref[0:1, :]).astype(bf16)
    width = low.shape[1]
    cos, sin = cos_ref[...], sin_ref[...]
    keys = dot(low, w_ref[:, width : 2 * width])
    for j in range(0, width, LANES):
        value = rope(keys[:, j : j + LANES], cos, sin).astype(bf16)
        head_ref[:, j : j + LANES] = value[:HALF]
        tail_ref[:, j : j + LANES] = value[HALF:]
    values = dot(low, w_ref[:, 2 * width :]).astype(bf16)
    head_ref[:, width:] = values[:HALF]
    tail_ref[:, width:] = values[HALF:]


def fill(dst, left, middle, right):
    rows = middle.shape[0]
    dst[0:HALF, :] = left[...]
    dst[HALF : HALF + rows, :] = middle[...]
    dst[HALF + rows :, :] = right[...]


def flip(dst, src):
    for at in range(0, src.shape[0], LANES):
        dst[:, at : at + LANES] = src[at : at + LANES, :].T


def attend_kernel(
    meta_ref, q_ref, k_ref, v_ref, kl_ref, vl_ref, kr_ref, vr_ref, o_ref, lse_ref, kx, vx, bias, vt
):
    blocks = q_ref.shape[0] // ROWS

    @pl.when(pl.program_id(0) == 0)
    def _():
        for n in range(blocks):
            bias[n] = mask_bias(meta_ref, n, ROWS + 2 * HALF)

    fill(kx, kl_ref, k_ref, kr_ref)
    fill(vx, vl_ref, v_ref, vr_ref)
    flip(vt, vx)
    depth = lax.broadcasted_iota(jnp.int32, (LANES, ROWS), 0)
    for n in range(blocks):
        own = slice(n * ROWS, (n + 1) * ROWS)
        queries = stacked(q_ref[own, :])
        mask = bias[n]
        scores = dot_rows(kx[window(n), :], queries) + jnp.concatenate([mask, mask], axis=1)
        top = jnp.max(scores, axis=0, keepdims=True)
        weights = jnp.exp(scores - top)
        total = jnp.sum(weights, axis=0, keepdims=True)
        out = dot(vt[:, window(n)], weights.astype(bf16)) * (1.0 / total)
        o_ref[:, own] = jnp.where(depth < 64, out[:, :ROWS], out[:, ROWS:]).astype(bf16)
        lse = top + jnp.log(total)
        lse_ref[0, 0:1, own] = lse[:, :ROWS]
        lse_ref[0, 1:2, own] = lse[:, ROWS:]


def back_blocks(
    blocks, dq_at, q_ref, do_ref, kx, vx, bias, kt, lse_ref, cos_ref, sin_ref, dq_ref, dkx, dvx
):
    for n in blocks:
        own = slice(n * ROWS, (n + 1) * ROWS)
        queries = stacked(q_ref[own, :])
        grads = stacked(do_ref[own, :])
        keys = kx[window(n), :]
        mask = bias[n]
        lse = jnp.concatenate([lse_ref[0, 0:1, own], lse_ref[0, 1:2, own]], axis=1)
        scores = dot_rows(keys, queries) + jnp.concatenate([mask, mask], axis=1)
        probs = jnp.exp(scores - lse)
        grad_probs = dot_rows(vx[window(n), :], grads)
        inner = jnp.sum(probs * grad_probs, axis=0, keepdims=True)
        grad_scores = (probs * (grad_probs - inner)).astype(bf16)
        dvx[window(n), :] += dot(probs.astype(bf16), grads)
        dkx[window(n), :] += dot(grad_scores, queries)
        grad_query = unstacked(dot(kt[:, window(n)], grad_scores)) * 0.125
        at = dq_at(n) * ROWS
        dq_ref[at : at + ROWS, :] = rope_back(
            grad_query, cos_ref[own, :], sin_ref[own, :]
        ).astype(bf16)


def attend_back_edges_kernel(
    meta_ref, q_ref, k_ref, v_ref, do_ref, kl_ref, vl_ref, kr_ref, vr_ref, lse_ref, cos_ref, sin_ref,
    dq_ref, wk_ref, wv_ref, head_ref, tail_ref, ek_ref, ev_ref,
    kx, vx, bias, kt, dkx, dvx,
):
    rows = q_ref.shape[0]
    blocks = rows // ROWS
    span = ROWS + 2 * HALF

    @pl.when(pl.program_id(0) == 0)
    def _():
        for n in (0, blocks - 1):
            bias[n] = mask_bias(meta_ref, n, span)

    fill(kx, kl_ref, k_ref, kr_ref)
    fill(vx, vl_ref, v_ref, vr_ref)
    for n in (0, blocks - 1):
        flip(kt.at[:, window(n)], kx.at[window(n), :])
    for acc in (dkx, dvx):
        acc[window(0), :] = jnp.zeros((span, LANES), f32)
        acc[window(blocks - 1), :] = jnp.zeros((span, LANES), f32)
    back_blocks(
        (0, blocks - 1), lambda n: min(n, 1),
        q_ref, do_ref, kx, vx, bias, kt, lse_ref, cos_ref, sin_ref, dq_ref, dkx, dvx,
    )
    for ref, acc in ((wk_ref, dkx), (wv_ref, dvx)):
        ref[:span, :] = acc[window(0), :]
        ref[span:, :] = acc[window(blocks - 1), :]
    for at, acc, ref in ((0, dkx, ek_ref), (1, dvx, ev_ref)):
        head_ref[at] = acc[0:HALF, :].astype(bf16)
        tail_ref[at] = acc[HALF + rows :, :].astype(bf16)
        ref[0:HALF, :] = acc[HALF : 2 * HALF, :]
        ref[HALF:, :] = acc[rows : rows + HALF, :]


def attend_back_kernel(
    meta_ref, q_ref, k_ref, v_ref, do_ref, kl_ref, vl_ref, kr_ref, vr_ref, lse_ref, cos_ref, sin_ref,
    eq_ref, wk_ref, wv_ref,
    dq_ref, dk_ref, dv_ref,
    kx, vx, bias, kt, dkx, dvx,
):
    rows = q_ref.shape[0]
    blocks = rows // ROWS
    span = ROWS + 2 * HALF

    @pl.when(pl.program_id(0) == 0)
    def _():
        for n in range(1, blocks - 1):
            bias[n] = mask_bias(meta_ref, n, span)

    fill(kx, kl_ref, k_ref, kr_ref)
    fill(vx, vl_ref, v_ref, vr_ref)
    flip(kt, kx)
    last = window(blocks - 1)
    for acc, ref in ((dkx, wk_ref), (dvx, wv_ref)):
        acc[window(0), :] = ref[:span, :]
        acc[span : last.start, :] = jnp.zeros((last.start - span, LANES), f32)
        acc[last, :] = ref[span:, :]
    dq_ref[:ROWS, :] = eq_ref[:ROWS, :]
    dq_ref[rows - ROWS :, :] = eq_ref[ROWS:, :]
    back_blocks(
        range(1, blocks - 1), lambda n: n,
        q_ref, do_ref, kx, vx, bias, kt, lse_ref, cos_ref, sin_ref, dq_ref, dkx, dvx,
    )
    middle = slice(HALF, HALF + rows)
    dk_ref[...] = rope_back(dkx[middle, :], cos_ref[...], sin_ref[...]).astype(bf16)
    dv_ref[...] = dvx[middle, :].astype(bf16)


def pack_grads(ref, c, slots, acc_d, acc_m, acc_a):
    wide, narrow = acc_m.shape[1] // 2, acc_a.shape[1] // 2
    rows, down_rows = acc_m.shape[0] // slots, acc_d.shape[0] // slots
    ref[:, :wide] = acc_m[:, c * wide : (c + 1) * wide].astype(bf16)
    ref[:, wide : wide + narrow] = acc_a[:, c * narrow : (c + 1) * narrow].astype(bf16)
    fill_rows = jnp.zeros((2 * rows - down_rows, narrow), f32)
    for n in range(slots):
        own = slice(n * rows, (n + 1) * rows)
        block = acc_d[n * down_rows : (n + 1) * down_rows, c * narrow : (c + 1) * narrow]
        ref[own, wide + narrow : wide + 2 * narrow] = block[:rows].astype(bf16)
        rest = jnp.concatenate([block[rows:], fill_rows], axis=0)
        ref[own, wide + 2 * narrow :] = rest.astype(bf16)


def middle_kernel(
    slots, core_ref, x_ref, o_ref, ct_ref, gain_ref, wa_ref, wm_ref, wd_ref,
    out_ref, dmid_ref, do_ref, *refs,
):
    *grad_refs, acc_d, acc_m, acc_a = refs
    step = pl.program_id(0)

    @pl.when(step == 0)
    def _():
        acc_d[...] = jnp.zeros_like(acc_d)
        acc_m[...] = jnp.zeros_like(acc_m)
        acc_a[...] = jnp.zeros_like(acc_a)

    gain = gain_ref[1:2, :]
    hidden = wd_ref.shape[0]
    chunk = hidden // 3
    ct = ct_ref[...]
    mid = x_ref[...].astype(f32) + dot_columns(o_ref[...], wa_ref[...])
    unit, inverse = normed(mid)
    low = (unit * gain).astype(bf16)
    low_t = low.T
    out = mid
    dh = jnp.zeros_like(mid)
    for at in range(0, hidden, chunk):
        first, second = slice(at, at + chunk), slice(hidden + at, hidden + at + chunk)
        a1 = dot(low, wm_ref[:, first])
        a2 = dot(low, wm_ref[:, second])
        du = dot_rows(ct, wd_ref[first, :])
        phi = 0.5 * (1.0 + lax.erf(a1 * (1.0 / math.sqrt(2.0))))
        gate = a1 * phi
        u = (gate * a2).astype(bf16)
        slope = phi + a1 * (jnp.exp(-0.5 * a1 * a1) * (1.0 / math.sqrt(2.0 * math.pi)))
        da1 = (du * a2 * slope).astype(bf16)
        da2 = (du * gate).astype(bf16)
        out = out + dot(u, wd_ref[first, :])
        dh = dh + dot_rows(da1, wm_ref[:, first]) + dot_rows(da2, wm_ref[:, second])
        acc_d[first, :] += dot_columns(u, ct)
        acc_m[:, first] += dot(low_t, da1)
        acc_m[:, second] += dot(low_t, da2)
    out_ref[...] = out.astype(bf16)
    dmid = ct.astype(f32) + normed_back(dh, gain, unit, inverse)
    dmid_ref[...] = dmid
    dmr = dmid.astype(bf16)
    acc_a[...] += dot(o_ref[...], dmr)
    do_ref[...] = dot_rows(dmr, wa_ref[...]).astype(bf16)

    last = step == pl.num_programs(0) - 1
    if slots is None:

        @pl.when(last)
        def _():
            for ref, acc in zip(grad_refs, (acc_d, acc_m, acc_a)):
                ref[...] = acc[...].astype(bf16)

    else:
        own_ref, other_ref = grad_refs
        for c in (0, 1):

            @pl.when(last & (core_ref[0] == c))
            def _(c=c):
                pack_grads(own_ref, c, slots, acc_d, acc_m, acc_a)
                pack_grads(other_ref, 1 - c, slots, acc_d, acc_m, acc_a)


def patched(step, steps, rows, value_ref, edge_ref):
    value = value_ref[...]
    edge = edge_ref[...]
    head = jnp.concatenate([edge[:HALF], value[HALF:]], axis=0)
    value = jnp.where(step == 0, head, value)
    tail = jnp.concatenate([value[: rows - HALF], edge[HALF:]], axis=0)
    return jnp.where(step == steps - 1, tail, value)


def qkv_grad_kernel(
    h_ref, dq_ref, dk_ref, dv_ref, rk_ref, rv_ref, left_ref, right_ref, cos_ref, sin_ref,
    g_ref, ek_ref, ev_ref, acc,
):
    step, steps = pl.program_id(0), pl.num_programs(0)
    rows, width = h_ref.shape

    @pl.when(step == 0)
    def _():
        for at, side in ((0, left_ref), (HALF, right_ref)):
            own = slice(at, at + HALF)
            cos, sin = cos_ref[own, :], sin_ref[own, :]
            for j in range(0, width, LANES):
                lanes = slice(j, j + LANES)
                total = rk_ref[own, lanes] + side[0, :, lanes].astype(f32)
                ek_ref[own, lanes] = rope_back(total, cos, sin).astype(bf16)
            ev_ref[own, :] = (rv_ref[own, :] + side[1].astype(f32)).astype(bf16)

    @pl.when(step == 0)
    def _():
        acc[...] = jnp.zeros_like(acc)

    low = h_ref[...]
    acc[:, :width] += dot_columns(low, dq_ref[...])
    acc[:, width : 2 * width] += dot_columns(low, patched(step, steps, rows, dk_ref, ek_ref))
    acc[:, 2 * width :] += dot_columns(low, patched(step, steps, rows, dv_ref, ev_ref))

    @pl.when(step == steps - 1)
    def _():
        g_ref[...] = acc[...].astype(bf16)


def input_kernel(x_ref, gain_ref, w_ref, dmid_ref, dq_ref, dk_ref, dv_ref, ek_ref, ev_ref, dx_ref):
    step, steps = pl.program_id(0), pl.num_programs(0)
    rows, width = x_ref.shape

    dh = dot_rows(dq_ref[...], w_ref[:, :width])
    dh = dh + dot_rows(patched(step, steps, rows, dk_ref, ek_ref), w_ref[:, width : 2 * width])
    dh = dh + dot_rows(patched(step, steps, rows, dv_ref, ev_ref), w_ref[:, 2 * width :])
    unit, inverse = normed(x_ref[...].astype(f32))
    dx = dmid_ref[...] + normed_back(dh, gain_ref[0:1, :], unit, inverse)
    dx_ref[...] = dx.astype(bf16)


def shaped(shape, dtype):
    return jax.ShapeDtypeStruct(shape, dtype)


def tiles(rows, columns):
    return pl.BlockSpec((rows, columns), lambda i: (i, 0))


def pairs(rows, offset=0):
    return pl.BlockSpec((rows, LANES), lambda i: (0, i + offset))


def kept(*shape):
    return pl.BlockSpec(shape, lambda i: (0,) * len(shape), pipeline_mode=pl.Buffered(1))


def held(*shape):
    return pl.BlockSpec(shape, lambda i: (0,) * len(shape))


def call(kernel, grid, in_specs, out_specs, out_shape, scratch, flops, moved):
    return pl.pallas_call(
        kernel,
        grid=(grid,),
        in_specs=in_specs,
        out_specs=out_specs,
        out_shape=out_shape,
        scratch_shapes=scratch,
        compiler_params=pltpu.CompilerParams(
            vmem_limit_bytes=vmem_bytes, dimension_semantics=("arbitrary",)
        ),
        cost_estimate=pl.CostEstimate(
            flops=flops // 64, bytes_accessed=moved // 64, transcendentals=0
        ),
    )


def project(x, gains, weight, cos, sin):
    rows, width = x.shape
    tile = min(TILE, rows)
    return call(
        project_kernel,
        rows // tile,
        [tiles(tile, width), held(2, width), kept(*weight.shape), tiles(tile, LANES), tiles(tile, LANES)],
        [tiles(tile, width)] * 4,
        [shaped((rows, width), bf16)] * 4,
        [],
        2 * rows * width * 3 * width,
        rows * width * 10 + weight.size * 2,
    )(x, gains, weight, cos, sin)


def project_edges(x, gains, weight, cos, sin):
    rows, width = x.shape
    return call(
        project_edges_kernel,
        1,
        [held(rows, width), held(2, width), kept(*weight.shape), held(rows, LANES), held(rows, LANES)],
        [held(HALF, 2 * width)] * 2,
        [shaped((HALF, 2 * width), bf16)] * 2,
        [],
        4 * rows * width * width,
        rows * width * 6 + weight.size * 2,
    )(x, gains, weight, cos, sin)


def attend_scratch(rows):
    extended = rows + 2 * HALF
    return [
        pltpu.VMEM((extended, LANES), bf16),
        pltpu.VMEM((extended, LANES), bf16),
        pltpu.VMEM((rows // ROWS, ROWS + 2 * HALF, ROWS), f32),
        pltpu.VMEM((LANES, extended), bf16),
    ]


def attend(meta, q, k, v, left, right):
    rows, width = q.shape
    steps = width // LANES
    return call(
        attend_kernel,
        steps,
        [pl.BlockSpec(memory_space=pltpu.SMEM)]
        + [pairs(rows)] * 3
        + [pairs(HALF), pairs(HALF, steps)] * 2,
        [pl.BlockSpec((LANES, rows), lambda i: (i, 0)), pl.BlockSpec((1, 2, rows), lambda i: (i, 0, 0))],
        [shaped((width, rows), bf16), shaped((steps, 2, rows), f32)],
        attend_scratch(rows),
        8 * rows * width * 256,
        rows * width * 8,
    )(meta, q, k, v, left, left, right, right)


def back_specs(rows, steps):
    return (
        [pl.BlockSpec(memory_space=pltpu.SMEM)]
        + [pairs(rows)] * 4
        + [pairs(HALF), pairs(HALF, steps)] * 2
        + [pl.BlockSpec((1, 2, rows), lambda i: (i, 0, 0)), held(rows, LANES), held(rows, LANES)]
    )


def back_scratch(rows):
    extended = rows + 2 * HALF
    return attend_scratch(rows) + [pltpu.VMEM((extended, LANES), f32)] * 2


def attend_back_edges(meta, q, k, v, do, left, right, lse, cos, sin):
    rows, width = q.shape
    steps = width // LANES
    span = 2 * (ROWS + 2 * HALF)
    return call(
        attend_back_edges_kernel,
        steps,
        back_specs(rows, steps),
        [pairs(2 * ROWS)]
        + [pairs(span)] * 2
        + [pl.BlockSpec((2, HALF, LANES), lambda i: (0, 0, i))] * 2
        + [pairs(2 * HALF)] * 2,
        [shaped((2 * ROWS, width), bf16)]
        + [shaped((span, width), f32)] * 2
        + [shaped((2, HALF, width), bf16)] * 2
        + [shaped((2 * HALF, width), f32)] * 2,
        back_scratch(rows),
        20 * 2 * ROWS * width * 256,
        rows * width * 10,
    )(meta, q, k, v, do, left, left, right, right, lse, cos, sin)


def attend_back(meta, q, k, v, do, left, right, lse, cos, sin, edges):
    rows, width = q.shape
    steps = width // LANES
    span = 2 * (ROWS + 2 * HALF)
    return call(
        attend_back_kernel,
        steps,
        back_specs(rows, steps) + [pairs(2 * ROWS)] + [pairs(span)] * 2,
        [pairs(rows)] * 3,
        [shaped((rows, width), bf16)] * 3,
        back_scratch(rows),
        20 * rows * width * 256,
        rows * width * 14,
    )(meta, q, k, v, do, left, left, right, right, lse, cos, sin, *edges)


def middle(slots, core, x, o, ct, gains, wa, wm, wd):
    rows, width = x.shape
    tile = min(TILE, rows)
    if slots is None:
        grads = [wd.shape, wm.shape, wa.shape]
    else:
        grads = [(width, wm.shape[1] // 2 + 3 * (width // 2))] * 2
    return call(
        functools.partial(middle_kernel, slots),
        rows // tile,
        [
            pl.BlockSpec(memory_space=pltpu.SMEM),
            tiles(tile, width),
            pl.BlockSpec((width, tile), lambda i: (0, i)),
            tiles(tile, width),
            held(2, width),
            kept(*wa.shape),
            kept(*wm.shape),
            kept(*wd.shape),
        ],
        [tiles(tile, width)] * 3 + [held(*shape) for shape in grads],
        [
            shaped((rows, width), bf16),
            shaped((rows, width), f32),
            shaped((rows, width), bf16),
        ]
        + [shaped(shape, bf16) for shape in grads],
        [pltpu.VMEM(wd.shape, f32), pltpu.VMEM(wm.shape, f32), pltpu.VMEM(wa.shape, f32)],
        6 * rows * (wa.size + wm.size + wd.size),
        rows * width * 14 + 4 * (wa.size + wm.size + wd.size),
    )(core, x, o, ct, gains, wa, wm, wd)


def qkv_gradient(h, dq, dk, dv, ek, ev, left, right, cos, sin):
    rows, width = h.shape
    tile = min(TILE, rows)
    return call(
        qkv_grad_kernel,
        rows // tile,
        [tiles(tile, width)] * 4
        + [held(2 * HALF, width)] * 2
        + [held(2, HALF, width)] * 2
        + [held(2 * HALF, LANES)] * 2,
        [held(width, 3 * width)] + [held(2 * HALF, width)] * 2,
        [shaped((width, 3 * width), bf16)] + [shaped((2 * HALF, width), bf16)] * 2,
        [pltpu.VMEM((width, 3 * width), f32)],
        6 * rows * width * width,
        rows * width * 8 + 6 * width * width,
    )(h, dq, dk, dv, ek, ev, left, right, cos, sin)


def input_gradient(x, gains, weight, dmid, dq, dk, dv, ek, ev):
    rows, width = x.shape
    tile = min(TILE, rows)
    return call(
        input_kernel,
        rows // tile,
        [tiles(tile, width), held(2, width), kept(*weight.shape)]
        + [tiles(tile, width)] * 4
        + [held(2 * HALF, width)] * 2,
        tiles(tile, width),
        shaped((rows, width), bf16),
        [],
        6 * rows * width * width,
        rows * width * 14 + 6 * width * width,
    )(x, gains, weight, dmid, dq, dk, dv, ek, ev)


def rope_tables(positions, head_size):
    half_size = head_size // 2
    exponent = jnp.arange(half_size, dtype=f32) * (2.0 / head_size)
    inverse = rope_theta ** (-exponent)
    inverse = jnp.tile(inverse, LANES // half_size)
    angles = positions.astype(f32)[:, None] * inverse[None, :]
    sign = jnp.where(jnp.arange(LANES) % head_size < half_size, -1.0, 1.0).astype(f32)
    return jnp.cos(angles), jnp.sin(angles) * sign


def adam_update(master, first_moment, second_moment, gradient, step_rate):
    gradient = gradient.astype(f32)
    new_first = beta_first * first_moment + (1.0 - beta_first) * gradient
    new_second = beta_second * second_moment + (1.0 - beta_second) * gradient * gradient
    first_hat = new_first / (1.0 - beta_first**ADAM_STEP)
    second_hat = new_second / (1.0 - beta_second**ADAM_STEP)
    new_master = master - step_rate * (
        decay_rate * master + first_hat / (jnp.sqrt(second_hat) + adam_epsilon)
    )
    return (new_first, new_second, new_master)


def edge_rows(value):
    return value[:HALF], value[value.shape[0] - HALF :]


def per_device(
    tokens,
    positions,
    cotangent,
    qkv_weight,
    attn_weight,
    mlp_weight,
    down_weight,
    norm_gains,
    qkv_first,
    qkv_second,
    attn_first,
    attn_second,
    mlp_first,
    mlp_second,
    down_first,
    down_second,
    gains_first,
    gains_second,
):
    rows, width = tokens.shape
    device = lax.axis_index(("seq", "shard"))
    last_device = lax.axis_size(("seq", "shard")) - 1
    cos, sin = rope_tables(positions, width // HEADS)
    start = jnp.max(jnp.where(positions == 0, jnp.arange(rows, dtype=jnp.int32), 0))
    low = jnp.where(device > 0, -HALF, 0)
    high = jnp.where(device < last_device, rows + HALF, rows)
    meta = jnp.stack([start, low, high]).astype(jnp.int32)
    shards = lax.axis_size("shard")
    quarters = lax.axis_size("seq") // 2
    core = lax.axis_index("seq") % 2
    split = split_pays()
    half = qkv_weight.shape[1] // 2
    slot = qkv_weight.shape[0] // quarters
    rest = down_weight.shape[0] // quarters - slot
    wide = mlp_weight.shape[1] // 2
    down_at = wide + attn_weight.shape[1] // 2
    lows = [w.astype(bf16) for w in (qkv_weight, attn_weight, mlp_weight, down_weight)]
    if split:
        qkv_low, attn_low, mlp_low, down_low = lows
        part = quarter_rows(halves(qkv_low, core))
        gain_rows = jnp.pad(norm_gains.astype(bf16), ((0, 6), (0, half - norm_gains.shape[1])))
        qkv_part, arrived = over_shard(jnp.concatenate([part, gain_rows], axis=0))
        gains = qkv_part[:, slot : slot + 2, : norm_gains.shape[1]].astype(f32)
        gains = gains.transpose(1, 0, 2).reshape(2, -1)
        down_part = quarter_rows(halves(down_low, core))
        rest_part = jnp.concatenate(
            [quarter_rows(halves(w, core)) for w in (mlp_low, attn_low)]
            + pack_down(down_part[None], slot),
            axis=1,
        )
        rest_part, _ = over_shard(after(rest_part, *arrived[:1]))
        qkv_part = over_quarters(qkv_part[:, :slot])
        rest_part = after(rest_part, qkv_part)
        full_qkv = side_by_side(*by_core(core, qkv_part, swap(qkv_part, "seq", 1)))
    else:
        full_qkv, full_attn, full_mlp, full_down = (
            lax.all_gather(w, "shard", axis=0, tiled=True) for w in lows
        )
        gains = lax.all_gather(norm_gains.astype(bf16), "shard", axis=1, tiled=True).astype(f32)
    edge_x, edge_cos, edge_sin = (
        jnp.concatenate(edge_rows(value), axis=0) for value in (tokens, cos, sin)
    )
    kv_head, kv_tail = project_edges(edge_x, gains, full_qkv, edge_cos, edge_sin)
    left = to_right(kv_tail)
    right = to_left(kv_head)
    h, q, k, v = project(after(tokens, kv_head), gains, full_qkv, cos, sin)
    left = after(left, k)
    right = after(right, k)
    o, lse = attend(meta, q, k, v, left, right)
    if split:
        rest_part = over_quarters(rest_part, (o,))
    if split:
        first, second = by_core(core, rest_part, swap(rest_part, "seq", 1))
        full_mlp = side_by_side(first[:, :wide], second[:, :wide])
        full_attn = side_by_side(first[:, wide:down_at], second[:, wide:down_at])
        full_down = side_by_side(
            *(unpack_down(x[:, down_at:], shards * quarters, rest) for x in (first, second))
        )
    core_index = jnp.reshape(core, (1,)).astype(jnp.int32)
    layer_output, dmid, do, *rest_grads = middle(
        shards * quarters if split else None,
        core_index, tokens, o, cotangent, gains, full_attn, full_mlp, full_down,
    )
    if split:
        rest_own, rest_other = rest_grads
        rest_got = swap(rest_other, "seq", 1)
    back_args = (meta, q, k, v, do, left, right, lse, cos, sin)
    *edges, halo_head, halo_tail, raw_k, raw_v = attend_back_edges(*back_args)
    from_right = to_left(halo_head)
    from_left = to_right(halo_tail)
    if split:
        rest_half = keep_half(rest_own, after(rest_got, halo_head))
        do = after(do, rest_half)
        back_args = (meta, q, k, v, do, left, right, lse, cos, sin)
        rest_pieces = quarter_pieces(rest_half)
    dq, dk, dv = attend_back(*back_args, edges)
    qkv_grad, edge_k, edge_v = qkv_gradient(
        h, dq, dk, dv, raw_k, raw_v, after(from_left, dq), after(from_right, dq), edge_cos, edge_sin
    )
    if split:
        rest_part = sum_after(rest_pieces, qkv_grad)
        qkv_got = swap(after(halves(qkv_grad, 1 - core), rest_part), "seq", 1)
        qkv_half = keep_half(halves(qkv_grad, core), qkv_got)
        dq = after(dq, qkv_half)
        qkv_pieces = quarter_pieces(qkv_half)
        rest_pieces = shard_pieces(rest_part)
    input_grad = input_gradient(tokens, gains, full_qkv, dmid, dq, dk, dv, edge_k, edge_v)
    if split:
        qkv_part = sum_after(qkv_pieces, input_grad)
        rest_part = sum_after(rest_pieces, qkv_part)
        qkv_part = sum_after(shard_pieces(qkv_part), rest_part)
        rest_half = owners_half(rest_part, (qkv_part,))
        rest_got = swap(rest_half, "seq", 1)
        qkv_half = owners_half(qkv_part, (rest_half,))
        qkv_got = swap(qkv_half, "seq", 1)
        first, second = by_core(core, rest_half, after(rest_got, qkv_half))
        mlp_total = side_by_side(first[:, :wide], second[:, :wide])
        attn_total = side_by_side(first[:, wide:down_at], second[:, wide:down_at])
        down_total = side_by_side(
            *(unpack_down(x[:, down_at:], quarters, rest) for x in (first, second))
        )
    else:
        down_total, mlp_total, attn_total, qkv_total = (
            reduce_whole(g) for g in (*rest_grads, qkv_grad)
        )
    attn_new = adam_update(attn_weight, attn_first, attn_second, attn_total, rate_matrix)
    mlp_new = adam_update(mlp_weight, mlp_first, mlp_second, mlp_total, rate_matrix)
    down_new = adam_update(down_weight, down_first, down_second, down_total, rate_matrix)
    if split:
        qkv_got = after(qkv_got, attn_new[0], mlp_new[0], down_new[0])
        qkv_total = side_by_side(*by_core(core, qkv_half, qkv_got))
    qkv_new = adam_update(qkv_weight, qkv_first, qkv_second, qkv_total, rate_matrix)
    gains_total = jnp.stack(
        [
            gain_grad(qkv_weight, qkv_total, norm_gains[0]),
            gain_grad(mlp_weight, mlp_total, norm_gains[1]),
        ]
    )
    gains_new = adam_update(norm_gains, gains_first, gains_second, gains_total, rate_gains)
    return (layer_output, input_grad, *qkv_new, *attn_new, *mlp_new, *down_new, *gains_new)


def solution(mesh):
    tokens, rows, columns = P(("seq", "shard"), None), P("shard", None), P(None, "shard")
    matrices = (rows,) * 4
    return jax.shard_map(
        per_device,
        mesh=mesh,
        in_specs=(tokens, P(("seq", "shard")), tokens, *matrices, columns)
        + (rows,) * 8
        + (columns,) * 2,
        out_specs=(tokens, tokens) + (rows,) * 12 + (columns,) * 3,
        check_vma=False,
    )
```

```python
import functools
import math

import jax
import jax.numpy as jnp
from jax import lax
from jax.experimental import pallas as pl
from jax.experimental.pallas import tpu as pltpu
from jax.sharding import PartitionSpec as P

HEADS = 12
HALF = 64
ADAM_STEP = 5
LANES = 128
ROWS = 64
SPAN = ROWS + 2 * HALF
PAIR = 2 * ROWS
TILE = 256
WIDE_TILE = 640


norm_epsilon = 1e-05
rope_theta = 10000.0
beta_first = 0.9
beta_second = 0.98
adam_epsilon = 1e-06
decay_rate = 1e-05
rate_matrix = 0.04
rate_gains = 0.2
masked_score = -1e30
vmem_bytes = 60 * 1024 * 1024

f32 = jnp.float32
bf16 = jnp.bfloat16


def swap(value, axis, flip):
    count = lax.axis_size(axis)
    return lax.ppermute(value, axis, [(i, i ^ flip) for i in range(count)])


def after(value, *others):
    return lax.optimization_barrier((value, *others))[0]


def spread(part, axis, unit, index, count, dim, then=()):
    out = jnp.zeros(part.shape[:dim] + (count,) + part.shape[dim:], part.dtype)
    pieces = [part] + [after(swap(part, axis, unit * d), *then) for d in range(1, count)]
    for d, piece in enumerate(pieces):
        out = lax.dynamic_update_slice_in_dim(out, jnp.expand_dims(piece, dim), index ^ d, dim)
    return out, pieces[1:]


def places():
    core = lax.axis_index("seq") % 2
    return core, lax.axis_index("seq") // 2, lax.axis_index("shard")


def by_core(core, own, other):
    return jnp.where(core == 0, own, other), jnp.where(core == 0, other, own)


def split_pays():
    count, shards = lax.axis_size("seq"), lax.axis_size("shard")
    return count == 8 and shards == 4


def halves(weight, core):
    width = weight.shape[1] // 2
    return lax.dynamic_slice_in_dim(weight, core * width, width, 1)


def quarter_rows(block):
    quarters = lax.axis_size("seq") // 2
    rows = block.shape[0] // quarters
    return lax.dynamic_slice_in_dim(block, (lax.axis_index("seq") // 2) * rows, rows, 0)


def stack(part, axis, unit, then=()):
    count = lax.axis_size(axis) // unit
    others = [after(swap(part, axis, unit * d), *then) for d in range(1, count)]
    return [part] + others


def down_rows(quarter):
    return 72 * quarter + 8 * (quarter % 2)


def down_part(block, rows):
    quarter = lax.axis_index("seq") // 2
    padded = jnp.pad(block, ((0, 16), (0, 0)))
    part = lax.dynamic_slice_in_dim(padded, down_rows(quarter), 80, 0)
    return pack_down(part[None], rows)


def pack_down(blocks, rows):
    rest = blocks.shape[1] - rows
    second = jnp.pad(blocks[:, rows:], ((0, 0), (0, rows - rest), (0, 0)))
    columns = blocks.shape[2]
    return [blocks[:, :rows].reshape(-1, columns), second.reshape(-1, columns)]


def unpack_down(packed, blocks, rest):
    columns = packed.shape[1] // 2
    packed = packed.reshape(blocks, -1, 2 * columns)
    whole = jnp.concatenate([packed[:, :, :columns], packed[:, :rest, columns:]], axis=1)
    return whole.reshape(-1, columns)


def side_by_side(first, second):
    return jnp.concatenate([first, second], axis=1)


def total_of(pieces):
    total = pieces[0].astype(f32)
    for piece in pieces[1:]:
        total = total + piece.astype(f32)
    return total.astype(bf16)


def keep_half(own, got):
    shards, quarters = lax.axis_size("shard"), lax.axis_size("seq") // 2
    return total_of([own, got]).reshape(shards, quarters, -1, own.shape[1])


def sum_after(parts, *others):
    return total_of(parts[:1] + [after(part, *others) for part in parts[1:]])


def pieces(value, axis, unit, index, count, dim):
    def at(place):
        return lax.dynamic_index_in_dim(value, place, dim, keepdims=False)

    return [at(index)] + [swap(at(index ^ d), axis, unit * d) for d in range(1, count)]


def quarter_pieces(half):
    return pieces(half, "seq", 2, lax.axis_index("seq") // 2, lax.axis_size("seq") // 2, 1)


def shard_pieces(half):
    return pieces(half, "shard", 1, lax.axis_index("shard"), lax.axis_size("shard"), 0)


def owners_half(part, then=()):
    count = lax.axis_size("seq")
    part, _ = spread(part, "seq", 2, lax.axis_index("seq") // 2, count // 2, 0, then)
    return part.reshape(-1, part.shape[-1])


def reduce_whole(grad):
    owned = lax.psum_scatter(grad, "shard", scatter_dimension=0, tiled=True)
    return lax.psum(owned.astype(f32), "seq")


def gain_grad(weight, gradient, gain):
    low = weight.astype(bf16).astype(f32)
    return jnp.sum(low * gradient.astype(f32), axis=1) / gain.astype(bf16).astype(f32)


def to_right(value):
    axes = ("seq", "shard")
    ends = lax.axis_size(axes) - 1
    return lax.ppermute(value, axes, [(i, i + 1) for i in range(ends)])


def to_left(value):
    axes = ("seq", "shard")
    ends = lax.axis_size(axes) - 1
    return lax.ppermute(value, axes, [(i + 1, i) for i in range(ends)])


def normed(hidden):
    centered = hidden - jnp.mean(hidden, axis=-1, keepdims=True)
    inverse = lax.rsqrt(jnp.mean(centered * centered, axis=-1, keepdims=True) + norm_epsilon)
    return centered * inverse, inverse


def normed_back(grad, gain, unit, inverse):
    inner = grad * gain
    mean = jnp.mean(inner, axis=-1, keepdims=True)
    slope = jnp.mean(inner * unit, axis=-1, keepdims=True)
    return inverse * (inner - mean - unit * slope)


def dot(a, b):
    return jnp.dot(a, b, preferred_element_type=f32)


def dot_rows(a, b):
    return lax.dot_general(a, b, (((1,), (1,)), ((), ())), preferred_element_type=f32)


def dot_columns(a, b):
    return lax.dot_general(a, b, (((0,), (0,)), ((), ())), preferred_element_type=f32)


def turned(values):
    lane = lax.broadcasted_iota(jnp.int32, values.shape, 1)
    up = pltpu.roll(values, LANES - 32, 1)
    down = pltpu.roll(values, 32, 1)
    return jnp.where(lane % 64 < 32, up, down)


def rope(values, cos, sin):
    return values * cos + turned(values) * sin


def rope_back(values, cos, sin):
    return values * cos - turned(values) * sin


def mask_bias(meta_ref, block):
    first = block * ROWS
    shape = (SPAN, LANES)
    key = lax.broadcasted_iota(jnp.int32, shape, 0) + (first - HALF)
    query = lax.broadcasted_iota(jnp.int32, shape, 1) % ROWS + first
    start, low, high = meta_ref[0], meta_ref[1], meta_ref[2]
    apart = jnp.abs(query - key) > HALF
    other = (query >= start) != (key >= start)
    outside = (key < low) | (key >= high)
    return jnp.where(apart | other | outside, masked_score, 0.0).astype(f32)


def stacked(values):
    lane = lax.broadcasted_iota(jnp.int32, values.shape, 1)
    zero = jnp.zeros_like(values)
    return jnp.concatenate(
        [jnp.where(lane < 64, values, zero), jnp.where(lane < 64, zero, values)], axis=0
    )


def unstacked(even, odd):
    lane = lax.broadcasted_iota(jnp.int32, (64, LANES), 1)
    top = jnp.where(lane < ROWS, even[:64], pltpu.roll(odd[:64], ROWS, 1))
    bottom = jnp.where(lane < ROWS, pltpu.roll(even[64:], ROWS, 1), odd[64:])
    return jnp.concatenate([top, bottom], axis=0)


def window(block):
    return slice(block * ROWS, block * ROWS + SPAN)


def turned_window(kt, kt_odd, block):
    at = (block // 2) * PAIR
    return (kt_odd if block % 2 else kt)[:, at : at + SPAN]


def assemble(place_ref, shards, quarters, copy):
    for c in (0, 1):

        @pl.when(place_ref[0] == c)
        def _(c=c):
            for side in (0, 1):
                for dq in range(quarters):
                    for dz in range(shards):
                        copy(
                            side,
                            c ^ side,
                            dq * shards + dz,
                            jnp.bitwise_xor(place_ref[1], dq),
                            jnp.bitwise_xor(place_ref[2], dz),
                        )


def project_kernel(x_ref, gain_ref, w_ref, cos_ref, sin_ref, h_ref, q_ref, k_ref, v_ref):
    unit, _ = normed(x_ref[...].astype(f32))
    low = (unit * gain_ref[0:1, :]).astype(bf16)
    h_ref[...] = low
    width = low.shape[1]
    cos, sin = cos_ref[...], sin_ref[...]
    for ref, at, scale in ((q_ref, 0, 0.125), (k_ref, width, None)):
        out = dot(low, w_ref[:, at : at + width])
        for j in range(0, width, LANES):
            value = rope(out[:, j : j + LANES], cos, sin)
            if scale is not None:
                value = value * scale
            ref[:, j : j + LANES] = value.astype(bf16)
    v_ref[...] = dot(low, w_ref[:, 2 * width :]).astype(bf16)


def project_edges_kernel(
    split, place_ref, x_ref, gain_ref, cos_ref, sin_ref, *refs
):
    *parts, head_ref, tail_ref, w_ref = refs
    if split:
        shards, quarters = split
        rows = parts[0].shape[0] // (shards * quarters)
        half = parts[0].shape[1]

        def copy(side, column, part, quarter, shard):
            at = pl.multiple_of((shard * quarters + quarter) * rows, 16)
            w_ref[pl.ds(at, rows), column * half : (column + 1) * half] = parts[side][
                part * rows : (part + 1) * rows, :
            ]

        assemble(place_ref, shards, quarters, copy)
    else:
        w_ref[...] = parts[0][...]
    unit, _ = normed(x_ref[...].astype(f32))
    low = (unit * gain_ref[0:1, :]).astype(bf16)
    width = low.shape[1]
    cos, sin = cos_ref[...], sin_ref[...]
    keys = dot(low, w_ref[:, width : 2 * width])
    for j in range(0, width, LANES):
        value = rope(keys[:, j : j + LANES], cos, sin).astype(bf16)
        head_ref[:, j : j + LANES] = value[:HALF]
        tail_ref[:, j : j + LANES] = value[HALF:]
    values = dot(low, w_ref[:, 2 * width :]).astype(bf16)
    head_ref[:, width:] = values[:HALF]
    tail_ref[:, width:] = values[HALF:]


def fill(dst, left, middle, right):
    rows = middle.shape[0]
    dst[0:HALF, :] = left[...]
    dst[HALF : HALF + rows, :] = middle[...]
    dst[HALF + rows :, :] = right[...]


def flip(dst, src, start, stop, shift):
    for at in range(start, stop, LANES):
        end = min(at + LANES, stop)
        dst[:, at - shift : end - shift] = src[at:end, :].T


def attend_kernel(
    meta_ref, q_ref, k_ref, v_ref, kl_ref, vl_ref, kr_ref, vr_ref, *refs
):
    o_ref, lse_ref, kx, vx, bias, vt, vt_odd = refs[-7:]
    blocks = q_ref.shape[0] // ROWS

    @pl.when(pl.program_id(0) == 0)
    def _():
        for n in range(blocks):
            bias[n] = mask_bias(meta_ref, n)

    fill(kx, kl_ref, k_ref, kr_ref)
    fill(vx, vl_ref, v_ref, vr_ref)
    flip(vt, vx, 0, vx.shape[0], 0)
    flip(vt_odd, vx, ROWS, vx.shape[0], ROWS)
    outs = []
    for n in range(blocks):
        queries = stacked(q_ref[n * ROWS : (n + 1) * ROWS, :])
        scores = dot_rows(kx[window(n), :], queries) + bias[n]
        top = jnp.max(scores, axis=0, keepdims=True)
        weights = jnp.exp(scores - top)
        total = jnp.sum(weights, axis=0, keepdims=True)
        out = dot(turned_window(vt, vt_odd, n), weights.astype(bf16))
        outs.append(out * (1.0 / total))
        lse_ref[0, n : n + 1, :] = top + jnp.log(total)
        if n % 2:
            at = (n // 2) * PAIR
            o_ref[:, at : at + PAIR] = unstacked(*outs[-2:]).astype(bf16)


def back_blocks(
    halves, dq_at, q_ref, do_ref, kx, vx, bias, kt, kt_odd, lse_ref, cos_ref, sin_ref, dq_ref, dkx, dvx
):
    for m in halves:
        outs = []
        for n in (2 * m, 2 * m + 1):
            own = slice(n * ROWS, (n + 1) * ROWS)
            queries = stacked(q_ref[own, :])
            grads = stacked(do_ref[own, :])
            scores = dot_rows(kx[window(n), :], queries) + bias[n]
            probs = jnp.exp(scores - lse_ref[0, n : n + 1, :])
            grad_probs = dot_rows(vx[window(n), :], grads)
            inner = jnp.sum(probs * grad_probs, axis=0, keepdims=True)
            grad_scores = (probs * (grad_probs - inner)).astype(bf16)
            dvx[window(n), :] += dot(probs.astype(bf16), grads)
            dkx[window(n), :] += dot(grad_scores, queries)
            outs.append(dot(turned_window(kt, kt_odd, n), grad_scores))
        own = slice(m * PAIR, (m + 1) * PAIR)
        grad_query = unstacked(*outs).T * 0.125
        at = dq_at(m) * PAIR
        dq_ref[at : at + PAIR, :] = rope_back(
            grad_query, cos_ref[own, :], sin_ref[own, :]
        ).astype(bf16)


def attend_back_edges_kernel(
    meta_ref, q_ref, k_ref, v_ref, do_ref, kl_ref, vl_ref, kr_ref, vr_ref, lse_ref, cos_ref, sin_ref,
    dq_ref, wk_ref, wv_ref, head_ref, tail_ref, ek_ref, ev_ref,
    kx, vx, bias, kt, kt_odd, dkx, dvx,
):
    rows = q_ref.shape[0]
    blocks = rows // PAIR
    span = PAIR + 2 * HALF
    spans = (slice(0, span), slice(rows - PAIR, rows + 2 * HALF))

    @pl.when(pl.program_id(0) == 0)
    def _():
        for n in (0, 1, 2 * blocks - 2, 2 * blocks - 1):
            bias[n] = mask_bias(meta_ref, n)

    fill(kx, kl_ref, k_ref, kr_ref)
    fill(vx, vl_ref, v_ref, vr_ref)
    for own in spans:
        flip(kt, kx, own.start, own.stop, 0)
        flip(kt_odd, kx, own.start + ROWS, own.stop, ROWS)
        for acc in (dkx, dvx):
            acc[own, :] = jnp.zeros((span, LANES), f32)
    back_blocks(
        (0, blocks - 1), lambda n: min(n, 1),
        q_ref, do_ref, kx, vx, bias, kt, kt_odd, lse_ref, cos_ref, sin_ref, dq_ref, dkx, dvx,
    )
    for ref, acc in ((wk_ref, dkx), (wv_ref, dvx)):
        ref[:span, :] = acc[spans[0], :]
        ref[span:, :] = acc[spans[1], :]
    for at, acc, ref in ((0, dkx, ek_ref), (1, dvx, ev_ref)):
        head_ref[at] = acc[0:HALF, :].astype(bf16)
        tail_ref[at] = acc[HALF + rows :, :].astype(bf16)
        ref[0:HALF, :] = acc[HALF : 2 * HALF, :]
        ref[HALF:, :] = acc[rows : rows + HALF, :]


def attend_back_kernel(
    meta_ref, q_ref, k_ref, v_ref, do_ref, kl_ref, vl_ref, kr_ref, vr_ref, lse_ref, cos_ref, sin_ref,
    eq_ref, wk_ref, wv_ref,
    dq_ref, dk_ref, dv_ref,
    kx, vx, bias, kt, kt_odd, dkx, dvx,
):
    rows = q_ref.shape[0]
    blocks = rows // PAIR
    span = PAIR + 2 * HALF

    @pl.when(pl.program_id(0) == 0)
    def _():
        for n in range(2, 2 * blocks - 2):
            bias[n] = mask_bias(meta_ref, n)

    fill(kx, kl_ref, k_ref, kr_ref)
    fill(vx, vl_ref, v_ref, vr_ref)
    flip(kt, kx, 0, kx.shape[0], 0)
    flip(kt_odd, kx, ROWS, kx.shape[0], ROWS)
    last = slice(rows - PAIR, rows + 2 * HALF)
    for acc, ref in ((dkx, wk_ref), (dvx, wv_ref)):
        acc[:span, :] = ref[:span, :]
        acc[span : last.start, :] = jnp.zeros((last.start - span, LANES), f32)
        acc[last, :] = ref[span:, :]
    dq_ref[:PAIR, :] = eq_ref[:PAIR, :]
    dq_ref[rows - PAIR :, :] = eq_ref[PAIR:, :]
    back_blocks(
        range(1, blocks - 1), lambda n: n,
        q_ref, do_ref, kx, vx, bias, kt, kt_odd, lse_ref, cos_ref, sin_ref, dq_ref, dkx, dvx,
    )
    middle = slice(HALF, HALF + rows)
    dk_ref[...] = rope_back(dkx[middle, :], cos_ref[...], sin_ref[...]).astype(bf16)
    dv_ref[...] = dvx[middle, :].astype(bf16)


def pack_grads(ref, c, slots, acc_d, acc_m, acc_a):
    wide, narrow = acc_m.shape[1] // 2, acc_a.shape[1] // 2
    rows, down_rows = acc_m.shape[0] // slots, acc_d.shape[0] // slots
    ref[:, :wide] = acc_m[:, c * wide : (c + 1) * wide].astype(bf16)
    ref[:, wide : wide + narrow] = acc_a[:, c * narrow : (c + 1) * narrow].astype(bf16)
    fill_rows = jnp.zeros((2 * rows - down_rows, narrow), f32)
    for n in range(slots):
        own = slice(n * rows, (n + 1) * rows)
        block = acc_d[n * down_rows : (n + 1) * down_rows, c * narrow : (c + 1) * narrow]
        ref[own, wide + narrow : wide + 2 * narrow] = block[:rows].astype(bf16)
        rest = jnp.concatenate([block[rows:], fill_rows], axis=0)
        ref[own, wide + 2 * narrow :] = rest.astype(bf16)


def gather_middle(split, place_ref, step, parts, wa_ref, wm_ref, wd_ref):
    shards, quarters = split
    rows = parts[0].shape[0] // (shards * quarters)
    wide, narrow = wm_ref.shape[1] // 2, wa_ref.shape[1] // 2
    shard_rows = wd_ref.shape[0] // shards

    def copy(side, column, part, quarter, shard):
        own = slice(part * rows, (part + 1) * rows)
        ref = parts[side]
        lanes = slice(column * narrow, (column + 1) * narrow)
        at = pl.multiple_of((shard * quarters + quarter) * rows, 16)
        wm_ref[pl.ds(at, rows), column * wide : (column + 1) * wide] = ref[own, :wide]
        wa_ref[pl.ds(at, rows), lanes] = ref[own, wide : wide + narrow]
        at = shard * shard_rows + down_rows(quarter)
        first, second = wide + narrow, wide + 2 * narrow
        wd_ref[pl.ds(pl.multiple_of(at, 16), rows), lanes] = ref[own, first:second]
        rest = ref[own, second:]
        wd_ref[pl.ds(pl.multiple_of(at + rows, 16), 16), lanes] = rest[:16]

        @pl.when(quarter % 2 == 0)
        def _():
            wd_ref[pl.ds(pl.multiple_of(at + rows + 16, 16), 16), lanes] = rest[16:32]

    @pl.when(step == 0)
    def _():
        assemble(place_ref, shards, quarters, copy)


def middle_kernel(
    split, place_ref, x_ref, o_ref, ct_ref, gain_ref, *refs
):
    *refs, acc_d, acc_m, acc_a = refs
    step = pl.program_id(0)
    if split:
        own_part, other_part, out_ref, dmid_ref, do_ref, own_ref, other_ref, wa_ref, wm_ref, wd_ref = refs
        gather_middle(split, place_ref, step, (own_part, other_part), wa_ref, wm_ref, wd_ref)
    else:
        wa_ref, wm_ref, wd_ref, out_ref, dmid_ref, do_ref, *grad_refs = refs

    @pl.when(step == 0)
    def _():
        acc_d[...] = jnp.zeros_like(acc_d)
        acc_m[...] = jnp.zeros_like(acc_m)
        acc_a[...] = jnp.zeros_like(acc_a)

    gain = gain_ref[1:2, :]
    hidden = wd_ref.shape[0]
    chunk = hidden // 3
    ct = ct_ref[...]
    mid = x_ref[...].astype(f32) + dot_columns(o_ref[...], wa_ref[...])
    unit, inverse = normed(mid)
    low = (unit * gain).astype(bf16)
    low_t = low.T
    out = mid
    dh = jnp.zeros_like(mid)
    for at in range(0, hidden, chunk):
        first, second = slice(at, at + chunk), slice(hidden + at, hidden + at + chunk)
        a1 = dot(low, wm_ref[:, first])
        a2 = dot(low, wm_ref[:, second])
        du = dot_rows(ct, wd_ref[first, :])
        phi = 0.5 * (1.0 + lax.erf(a1 * (1.0 / math.sqrt(2.0))))
        gate = a1 * phi
        u = (gate * a2).astype(bf16)
        slope = phi + a1 * (jnp.exp(-0.5 * a1 * a1) * (1.0 / math.sqrt(2.0 * math.pi)))
        da1 = (du * a2 * slope).astype(bf16)
        da2 = (du * gate).astype(bf16)
        out = out + dot(u, wd_ref[first, :])
        dh = dh + dot_rows(da1, wm_ref[:, first]) + dot_rows(da2, wm_ref[:, second])
        acc_d[first, :] += dot_columns(u, ct)
        acc_m[:, first] += dot(low_t, da1)
        acc_m[:, second] += dot(low_t, da2)
    out_ref[...] = out.astype(bf16)
    dmid = ct.astype(f32) + normed_back(dh, gain, unit, inverse)
    dmr = dmid.astype(bf16)
    dmid_ref[...] = dmr
    acc_a[...] += dot(o_ref[...], dmr)
    do_ref[...] = dot_rows(dmr, wa_ref[...]).astype(bf16)

    last = step == pl.num_programs(0) - 1
    if not split:

        @pl.when(last)
        def _():
            for ref, acc in zip(grad_refs, (acc_d, acc_m, acc_a)):
                ref[...] = acc[...].astype(bf16)

    else:
        slots = split[0] * split[1]
        for c in (0, 1):

            @pl.when(last & (place_ref[0] == c))
            def _(c=c):
                pack_grads(own_ref, c, slots, acc_d, acc_m, acc_a)
                pack_grads(other_ref, 1 - c, slots, acc_d, acc_m, acc_a)


def patched(step, steps, rows, value_ref, edge_ref):
    value = value_ref[...]
    edge = edge_ref[...]
    head = jnp.concatenate([edge[:HALF], value[HALF:]], axis=0)
    value = jnp.where(step == 0, head, value)
    tail = jnp.concatenate([value[: rows - HALF], edge[HALF:]], axis=0)
    return jnp.where(step == steps - 1, tail, value)


def qkv_grad_kernel(
    split, place_ref,
    h_ref, dq_ref, dk_ref, dv_ref, rk_ref, rv_ref, left_ref, right_ref, cos_ref, sin_ref,
    ek_ref, ev_ref, *refs,
):
    *grad_refs, acc = refs
    step, steps = pl.program_id(0), pl.num_programs(0)
    rows, width = h_ref.shape

    @pl.when(step == 0)
    def _():
        for at, side in ((0, left_ref), (HALF, right_ref)):
            own = slice(at, at + HALF)
            cos, sin = cos_ref[own, :], sin_ref[own, :]
            for j in range(0, width, LANES):
                lanes = slice(j, j + LANES)
                total = rk_ref[own, lanes] + side[0, :, lanes].astype(f32)
                ek_ref[own, lanes] = rope_back(total, cos, sin).astype(bf16)
            ev_ref[own, :] = (rv_ref[own, :] + side[1].astype(f32)).astype(bf16)

    @pl.when(step == 0)
    def _():
        acc[...] = jnp.zeros_like(acc)

    low = h_ref[...]
    acc[:, :width] += dot_columns(low, dq_ref[...])
    acc[:, width : 2 * width] += dot_columns(low, patched(step, steps, rows, dk_ref, ek_ref))
    acc[:, 2 * width :] += dot_columns(low, patched(step, steps, rows, dv_ref, ev_ref))

    last = step == steps - 1
    if not split:

        @pl.when(last)
        def _():
            grad_refs[0][...] = acc[...].astype(bf16)

    else:
        half = acc.shape[1] // 2
        for c in (0, 1):

            @pl.when(last & (place_ref[0] == c))
            def _(c=c):
                for ref, side in zip(grad_refs, (c, 1 - c)):
                    ref[...] = acc[:, side * half : (side + 1) * half].astype(bf16)


def input_kernel(x_ref, gain_ref, w_ref, dmid_ref, dq_ref, dk_ref, dv_ref, ek_ref, ev_ref, dx_ref):
    step, steps = pl.program_id(0), pl.num_programs(0)
    rows, width = x_ref.shape

    dh = dot_rows(dq_ref[...], w_ref[:, :width])
    dh = dh + dot_rows(patched(step, steps, rows, dk_ref, ek_ref), w_ref[:, width : 2 * width])
    dh = dh + dot_rows(patched(step, steps, rows, dv_ref, ev_ref), w_ref[:, 2 * width :])
    unit, inverse = normed(x_ref[...].astype(f32))
    dx = dmid_ref[...].astype(f32) + normed_back(dh, gain_ref[0:1, :], unit, inverse)
    dx_ref[...] = dx.astype(bf16)


def shaped(shape, dtype):
    return jax.ShapeDtypeStruct(shape, dtype)


def tiles(rows, columns):
    return pl.BlockSpec((rows, columns), lambda i: (i, 0))


def pairs(rows, offset=0):
    return pl.BlockSpec((rows, LANES), lambda i: (0, i + offset))


def kept(*shape):
    return pl.BlockSpec(shape, lambda i: (0,) * len(shape), pipeline_mode=pl.Buffered(1))


def held(*shape):
    return pl.BlockSpec(shape, lambda i: (0,) * len(shape))


def call(
    kernel, grid, in_specs, out_specs, out_shape, scratch, flops, moved, aliases=None
):
    return pl.pallas_call(
        kernel,
        grid=(grid,),
        in_specs=in_specs,
        out_specs=out_specs,
        out_shape=out_shape,
        scratch_shapes=scratch,
        input_output_aliases=aliases or {},
        compiler_params=pltpu.CompilerParams(
            vmem_limit_bytes=vmem_bytes, dimension_semantics=("arbitrary",)
        ),
        cost_estimate=pl.CostEstimate(
            flops=flops // 64, bytes_accessed=moved // 64, transcendentals=0
        ),
    )


def project(x, gains, weight, cos, sin):
    rows, width = x.shape
    tile = min(TILE, rows)
    return call(
        project_kernel,
        rows // tile,
        [tiles(tile, width), held(2, width), kept(*weight.shape), tiles(tile, LANES), tiles(tile, LANES)],
        [tiles(tile, width)] * 4,
        [shaped((rows, width), bf16)] * 4,
        [],
        2 * rows * width * 3 * width,
        rows * width * 10 + weight.size * 2,
    )(x, gains, weight, cos, sin)


def project_edges(split, place, x, gains, cos, sin, *parts):
    rows, width = x.shape
    return call(
        functools.partial(project_edges_kernel, split),
        1,
        [pl.BlockSpec(memory_space=pltpu.SMEM), held(rows, width), held(2, width)]
        + [held(rows, LANES)] * 2
        + [held(*part.shape) for part in parts],
        [held(HALF, 2 * width)] * 2 + [held(width, 3 * width)],
        [shaped((HALF, 2 * width), bf16)] * 2 + [shaped((width, 3 * width), bf16)],
        [],
        4 * rows * width * width,
        rows * width * 6 + width * width * 12,
    )(place, x, gains, cos, sin, *parts)


def attend_scratch(rows):
    extended = rows + 2 * HALF
    return [
        pltpu.VMEM((extended, LANES), bf16),
        pltpu.VMEM((extended, LANES), bf16),
        pltpu.VMEM((rows // ROWS, SPAN, LANES), f32),
        pltpu.VMEM((LANES, extended), bf16),
        pltpu.VMEM((LANES, extended - ROWS), bf16),
    ]


def attend(meta, q, k, v, left, right, first, count, before=()):
    rows, width = q.shape
    steps = width // LANES

    def columns(height, offset=0):
        return pairs(height, first + offset)

    return call(
        attend_kernel,
        count,
        [pl.BlockSpec(memory_space=pltpu.SMEM)]
        + [columns(rows)] * 3
        + [columns(HALF), columns(HALF, steps)] * 2
        + [pl.BlockSpec(memory_space=pl.ANY)] * len(before),
        [
            pl.BlockSpec((LANES, rows), lambda i: (i + first, 0)),
            pl.BlockSpec((1, rows // ROWS, LANES), lambda i: (i + first, 0, 0)),
        ],
        [shaped((width, rows), bf16), shaped((steps, rows // ROWS, LANES), f32)],
        attend_scratch(rows),
        8 * rows * width * 256,
        rows * width * 8,
        {8 + at: at for at in range(len(before))},
    )(meta, q, k, v, left, left, right, right, *before)


def back_specs(rows, steps):
    return (
        [pl.BlockSpec(memory_space=pltpu.SMEM)]
        + [pairs(rows)] * 4
        + [pairs(HALF), pairs(HALF, steps)] * 2
        + [pl.BlockSpec((1, rows // ROWS, LANES), lambda i: (i, 0, 0)), held(rows, LANES), held(rows, LANES)]
    )


def back_scratch(rows):
    extended = rows + 2 * HALF
    return attend_scratch(rows) + [pltpu.VMEM((extended, LANES), f32)] * 2


def attend_back_edges(meta, q, k, v, do, left, right, lse, cos, sin):
    rows, width = q.shape
    steps = width // LANES
    span = 2 * (PAIR + 2 * HALF)
    return call(
        attend_back_edges_kernel,
        steps,
        back_specs(rows, steps),
        [pairs(2 * PAIR)]
        + [pairs(span)] * 2
        + [pl.BlockSpec((2, HALF, LANES), lambda i: (0, 0, i))] * 2
        + [pairs(2 * HALF)] * 2,
        [shaped((2 * PAIR, width), bf16)]
        + [shaped((span, width), f32)] * 2
        + [shaped((2, HALF, width), bf16)] * 2
        + [shaped((2 * HALF, width), f32)] * 2,
        back_scratch(rows),
        20 * 2 * PAIR * width * 256,
        rows * width * 10,
    )(meta, q, k, v, do, left, left, right, right, lse, cos, sin)


def attend_back(meta, q, k, v, do, left, right, lse, cos, sin, edges):
    rows, width = q.shape
    steps = width // LANES
    span = 2 * (PAIR + 2 * HALF)
    return call(
        attend_back_kernel,
        steps,
        back_specs(rows, steps) + [pairs(2 * PAIR)] + [pairs(span)] * 2,
        [pairs(rows)] * 3,
        [shaped((rows, width), bf16)] * 3,
        back_scratch(rows),
        20 * rows * width * 256,
        rows * width * 14,
    )(meta, q, k, v, do, left, left, right, right, lse, cos, sin, *edges)


def middle(split, place, x, o, ct, gains, shapes, *weights):
    rows, width = x.shape
    tile = WIDE_TILE if rows % WIDE_TILE == 0 else rows
    wa, wm, wd = shapes
    if split:
        grads = [(width, wm[1] // 2 + 3 * (width // 2))] * 2
    else:
        grads = [wd, wm, wa]
    return call(
        functools.partial(middle_kernel, split),
        rows // tile,
        [
            pl.BlockSpec(memory_space=pltpu.SMEM),
            tiles(tile, width),
            pl.BlockSpec((width, tile), lambda i: (0, i)),
            tiles(tile, width),
            held(2, width),
        ]
        + [kept(*w.shape) for w in weights],
        [tiles(tile, width)] * 3 + [kept(*shape) for shape in grads],
        [shaped((rows, width), bf16)] * 3 + [shaped(shape, bf16) for shape in grads],
        ([pltpu.VMEM(w, bf16) for w in shapes] if split else [])
        + [pltpu.VMEM(wd, f32), pltpu.VMEM(wm, f32), pltpu.VMEM(wa, f32)],
        6 * rows * width * width * 5,
        rows * width * 14 + 20 * width * width,
    )(place, x, o, ct, gains, *weights)


def qkv_gradient(split, place, h, dq, dk, dv, ek, ev, left, right, cos, sin):
    rows, width = h.shape
    tile = WIDE_TILE if rows % WIDE_TILE == 0 else rows
    grads = [(width, 3 * width // 2)] * 2 if split else [(width, 3 * width)]
    return call(
        functools.partial(qkv_grad_kernel, split),
        rows // tile,
        [pl.BlockSpec(memory_space=pltpu.SMEM)]
        + [tiles(tile, width)] * 4
        + [held(2 * HALF, width)] * 2
        + [held(2, HALF, width)] * 2
        + [held(2 * HALF, LANES)] * 2,
        [held(2 * HALF, width)] * 2 + [held(*shape) for shape in grads],
        [shaped((2 * HALF, width), bf16)] * 2 + [shaped(shape, bf16) for shape in grads],
        [pltpu.VMEM((width, 3 * width), f32)],
        6 * rows * width * width,
        rows * width * 8 + 6 * width * width,
    )(place, h, dq, dk, dv, ek, ev, left, right, cos, sin)


def input_gradient(x, gains, weight, dmid, dq, dk, dv, ek, ev):
    rows, width = x.shape
    tile = min(TILE, rows)
    return call(
        input_kernel,
        rows // tile,
        [tiles(tile, width), held(2, width), kept(*weight.shape)]
        + [tiles(tile, width)] * 4
        + [held(2 * HALF, width)] * 2,
        tiles(tile, width),
        shaped((rows, width), bf16),
        [],
        6 * rows * width * width,
        rows * width * 14 + 6 * width * width,
    )(x, gains, weight, dmid, dq, dk, dv, ek, ev)


def rope_tables(positions, head_size):
    half_size = head_size // 2
    exponent = jnp.arange(half_size, dtype=f32) * (2.0 / head_size)
    inverse = rope_theta ** (-exponent)
    inverse = jnp.tile(inverse, LANES // half_size)
    angles = positions.astype(f32)[:, None] * inverse[None, :]
    sign = jnp.where(jnp.arange(LANES) % head_size < half_size, -1.0, 1.0).astype(f32)
    return jnp.cos(angles), jnp.sin(angles) * sign


def adam_update(master, first_moment, second_moment, gradient, step_rate):
    gradient = gradient.astype(f32)
    new_first = beta_first * first_moment + (1.0 - beta_first) * gradient
    new_second = beta_second * second_moment + (1.0 - beta_second) * gradient * gradient
    first_hat = new_first / (1.0 - beta_first**ADAM_STEP)
    second_hat = new_second / (1.0 - beta_second**ADAM_STEP)
    new_master = master - step_rate * (
        decay_rate * master + first_hat / (jnp.sqrt(second_hat) + adam_epsilon)
    )
    return (new_first, new_second, new_master)


def edge_rows(value):
    return value[:HALF], value[value.shape[0] - HALF :]


def per_device(
    tokens,
    positions,
    cotangent,
    qkv_weight,
    attn_weight,
    mlp_weight,
    down_weight,
    norm_gains,
    qkv_first,
    qkv_second,
    attn_first,
    attn_second,
    mlp_first,
    mlp_second,
    down_first,
    down_second,
    gains_first,
    gains_second,
):
    rows, width = tokens.shape
    device = lax.axis_index(("seq", "shard"))
    last_device = lax.axis_size(("seq", "shard")) - 1
    cos, sin = rope_tables(positions, width // HEADS)
    start = jnp.max(jnp.where(positions == 0, jnp.arange(rows, dtype=jnp.int32), 0))
    low = jnp.where(device > 0, -HALF, 0)
    high = jnp.where(device < last_device, rows + HALF, rows)
    meta = jnp.stack([start, low, high]).astype(jnp.int32)
    shards = lax.axis_size("shard")
    quarters = lax.axis_size("seq") // 2
    core = lax.axis_index("seq") % 2
    split = (shards, quarters) if split_pays() else None
    place = jnp.stack([core, lax.axis_index("seq") // 2, lax.axis_index("shard")])
    place = place.astype(jnp.int32)
    half = qkv_weight.shape[1] // 2
    slot = qkv_weight.shape[0] // quarters
    rest = down_weight.shape[0] // quarters - slot
    wide = mlp_weight.shape[1] // 2
    down_at = wide + attn_weight.shape[1] // 2
    lows = [w.astype(bf16) for w in (qkv_weight, attn_weight, mlp_weight, down_weight)]
    if split:
        qkv_low, attn_low, mlp_low, down_low = lows
        part = quarter_rows(halves(qkv_low, core))
        gain_rows = jnp.pad(norm_gains.astype(bf16), ((0, 6), (0, half - norm_gains.shape[1])))
        qkv_stack = stack(jnp.concatenate([part, gain_rows], axis=0), "shard", 1)
        gains = jnp.zeros((shards, 2, norm_gains.shape[1]), bf16)
        for d, piece in enumerate(qkv_stack):
            piece = piece[None, slot : slot + 2, : norm_gains.shape[1]]
            gains = lax.dynamic_update_slice_in_dim(gains, piece, lax.axis_index("shard") ^ d, 0)
        gains = gains.astype(f32).transpose(1, 0, 2).reshape(2, -1)
        rest_part = jnp.concatenate(
            [quarter_rows(halves(w, core)) for w in (mlp_low, attn_low)]
            + down_part(halves(down_low, core), slot),
            axis=1,
        )
        rest_part = jnp.concatenate(
            stack(after(rest_part, qkv_stack[1]), "shard", 1), axis=0
        )
        qkv_part = jnp.concatenate([piece[:slot] for piece in qkv_stack], axis=0)
        qkv_part = jnp.concatenate(stack(qkv_part, "seq", 2), axis=0)
        qkv_part = after(qkv_part, rest_part)
        rest_part = after(rest_part, qkv_part)
        qkv_parts = qkv_part, swap(qkv_part, "seq", 1)
    else:
        full_qkv, full_attn, full_mlp, full_down = (
            lax.all_gather(w, "shard", axis=0, tiled=True) for w in lows
        )
        gains = lax.all_gather(norm_gains.astype(bf16), "shard", axis=1, tiled=True).astype(f32)
        qkv_parts = (full_qkv,)
    edge_x, edge_cos, edge_sin = (
        jnp.concatenate(edge_rows(value), axis=0) for value in (tokens, cos, sin)
    )
    kv_head, kv_tail, full_qkv = project_edges(
        split, place, edge_x, gains, edge_cos, edge_sin, *qkv_parts
    )
    left = to_right(kv_tail)
    right = to_left(kv_head)
    h, q, k, v = project(after(tokens, kv_head), gains, full_qkv, cos, sin)
    left = after(left, k)
    right = after(right, k)
    pair_count = width // LANES
    before = attend(meta, q, k, v, left, right, 0, pair_count // 2)
    if split:
        rest_part = jnp.concatenate(stack(rest_part, "seq", 2, (before[0],)), axis=0)
        rest_weights = rest_part, swap(rest_part, "seq", 1)
        q = after(q, rest_part)
    else:
        rest_weights = full_attn, full_mlp, full_down
    o, lse = attend(
        meta, q, k, v, left, right, pair_count // 2, pair_count - pair_count // 2, before
    )
    shapes = (
        (width, attn_weight.shape[1]),
        (width, mlp_weight.shape[1]),
        (shards * down_weight.shape[0], width),
    )
    layer_output, dmid, do, *rest_grads = middle(
        split, place, tokens, o, cotangent, gains, shapes, *rest_weights
    )
    if split:
        rest_own, rest_other = rest_grads
        rest_got = swap(rest_other, "seq", 1)
    back_args = (meta, q, k, v, do, left, right, lse, cos, sin)
    *edges, halo_head, halo_tail, raw_k, raw_v = attend_back_edges(*back_args)
    from_right = to_left(halo_head)
    from_left = to_right(halo_tail)
    if split:
        rest_half = keep_half(rest_own, after(rest_got, halo_head))
        do = after(do, rest_half)
        back_args = (meta, q, k, v, do, left, right, lse, cos, sin)
        rest_pieces = quarter_pieces(rest_half)
    dq, dk, dv = attend_back(*back_args, edges)
    edge_k, edge_v, *qkv_grads = qkv_gradient(
        split, place, h, dq, dk, dv, raw_k, raw_v, after(from_left, dq), after(from_right, dq), edge_cos, edge_sin
    )
    if split:
        qkv_own, qkv_other = qkv_grads
        rest_part = sum_after(rest_pieces, qkv_own)
        qkv_got = swap(after(qkv_other, rest_part), "seq", 1)
        qkv_half = keep_half(qkv_own, qkv_got)
        dq = after(dq, qkv_half)
        qkv_pieces = quarter_pieces(qkv_half)
        rest_pieces = shard_pieces(rest_part)
    input_grad = input_gradient(tokens, gains, full_qkv, dmid, dq, dk, dv, edge_k, edge_v)
    if split:
        qkv_part = sum_after(qkv_pieces, input_grad)
        rest_part = sum_after(rest_pieces, qkv_part)
        qkv_part = sum_after(shard_pieces(qkv_part), rest_part)
        rest_half = owners_half(rest_part, (qkv_part,))
        rest_got = swap(rest_half, "seq", 1)
        qkv_half = owners_half(qkv_part, (rest_half,))
        qkv_got = swap(qkv_half, "seq", 1)
        first, second = by_core(core, rest_half, after(rest_got, qkv_half))
        mlp_total = side_by_side(first[:, :wide], second[:, :wide])
        attn_total = side_by_side(first[:, wide:down_at], second[:, wide:down_at])
        down_total = side_by_side(
            *(unpack_down(x[:, down_at:], quarters, rest) for x in (first, second))
        )
    else:
        down_total, mlp_total, attn_total, qkv_total = (
            reduce_whole(g) for g in (*rest_grads, *qkv_grads)
        )
    attn_new = adam_update(attn_weight, attn_first, attn_second, attn_total, rate_matrix)
    mlp_new = adam_update(mlp_weight, mlp_first, mlp_second, mlp_total, rate_matrix)
    down_new = adam_update(down_weight, down_first, down_second, down_total, rate_matrix)
    if split:
        qkv_got = after(qkv_got, attn_new[0], mlp_new[0], down_new[0])
        qkv_total = side_by_side(*by_core(core, qkv_half, qkv_got))
    qkv_new = adam_update(qkv_weight, qkv_first, qkv_second, qkv_total, rate_matrix)
    gains_total = jnp.stack(
        [
            gain_grad(qkv_weight, qkv_total, norm_gains[0]),
            gain_grad(mlp_weight, mlp_total, norm_gains[1]),
        ]
    )
    gains_new = adam_update(norm_gains, gains_first, gains_second, gains_total, rate_gains)
    return (layer_output, input_grad, *qkv_new, *attn_new, *mlp_new, *down_new, *gains_new)


def solution(mesh):
    tokens, rows, columns = P(("seq", "shard"), None), P("shard", None), P(None, "shard")
    matrices = (rows,) * 4
    return jax.shard_map(
        per_device,
        mesh=mesh,
        in_specs=(tokens, P(("seq", "shard")), tokens, *matrices, columns)
        + (rows,) * 8
        + (columns,) * 2,
        out_specs=(tokens, tokens) + (rows,) * 12 + (columns,) * 3,
        check_vma=False,
    )
```

```python
import functools
import math

import jax
import jax.numpy as jnp
from jax import lax
from jax.experimental import pallas as pl
from jax.experimental.pallas import tpu as pltpu
from jax.sharding import PartitionSpec as P

HEADS = 12
HALF = 64
ADAM_STEP = 5
LANES = 128
ROWS = 128
SPAN = ROWS + 2 * HALF
TILE = 256
WIDE_TILE = 640
GROUP = 2


norm_epsilon = 1e-05
rope_theta = 10000.0
beta_first = 0.9
beta_second = 0.98
adam_epsilon = 1e-06
decay_rate = 1e-05
rate_matrix = 0.04
rate_gains = 0.2
masked_score = -1e30
vmem_bytes = 60 * 1024 * 1024

f32 = jnp.float32
bf16 = jnp.bfloat16


def swap(value, axis, flip):
    count = lax.axis_size(axis)
    return lax.ppermute(value, axis, [(i, i ^ flip) for i in range(count)])


def after(value, *others):
    return lax.optimization_barrier((value, *others))[0]


def spread(part, axis, unit, index, count, dim, then=()):
    out = jnp.zeros(part.shape[:dim] + (count,) + part.shape[dim:], part.dtype)
    pieces = [part] + [after(swap(part, axis, unit * d), *then) for d in range(1, count)]
    for d, piece in enumerate(pieces):
        out = lax.dynamic_update_slice_in_dim(out, jnp.expand_dims(piece, dim), index ^ d, dim)
    return out, pieces[1:]


def places():
    core = lax.axis_index("seq") % 2
    return core, lax.axis_index("seq") // 2, lax.axis_index("shard")


def by_core(core, own, other):
    return jnp.where(core == 0, own, other), jnp.where(core == 0, other, own)


def split_pays():
    count, shards = lax.axis_size("seq"), lax.axis_size("shard")
    return count == 8 and shards == 4


def halves(weight, core):
    width = weight.shape[1] // 2
    return lax.dynamic_slice_in_dim(weight, core * width, width, 1)


def quarter_rows(block):
    quarters = lax.axis_size("seq") // 2
    rows = block.shape[0] // quarters
    return lax.dynamic_slice_in_dim(block, (lax.axis_index("seq") // 2) * rows, rows, 0)


def stack(part, axis, unit, then=()):
    count = lax.axis_size(axis) // unit
    others = [after(swap(part, axis, unit * d), *then) for d in range(1, count)]
    return [part] + others


def down_rows(quarter):
    return 72 * quarter + 8 * (quarter % 2)


def down_part(block, rows):
    quarter = lax.axis_index("seq") // 2
    padded = jnp.pad(block, ((0, 16), (0, 0)))
    part = lax.dynamic_slice_in_dim(padded, down_rows(quarter), 80, 0)
    return pack_down(part[None], rows)


def pack_down(blocks, rows):
    rest = blocks.shape[1] - rows
    second = jnp.pad(blocks[:, rows:], ((0, 0), (0, rows - rest), (0, 0)))
    columns = blocks.shape[2]
    return [blocks[:, :rows].reshape(-1, columns), second.reshape(-1, columns)]


def unpack_down(packed, blocks, rest):
    columns = packed.shape[1] // 2
    packed = packed.reshape(blocks, -1, 2 * columns)
    whole = jnp.concatenate([packed[:, :, :columns], packed[:, :rest, columns:]], axis=1)
    return whole.reshape(-1, columns)


def side_by_side(first, second):
    return jnp.concatenate([first, second], axis=1)


def total_of(pieces):
    total = pieces[0].astype(f32)
    for piece in pieces[1:]:
        total = total + piece.astype(f32)
    return total.astype(bf16)


def keep_half(own, got):
    shards, quarters = lax.axis_size("shard"), lax.axis_size("seq") // 2
    return total_of([own, got]).reshape(shards, quarters, -1, own.shape[1])


def sum_after(parts, *others):
    return total_of(parts[:1] + [after(part, *others) for part in parts[1:]])


def pieces(value, axis, unit, index, count, dim):
    def at(place):
        return lax.dynamic_index_in_dim(value, place, dim, keepdims=False)

    return [at(index)] + [swap(at(index ^ d), axis, unit * d) for d in range(1, count)]


def quarter_pieces(half):
    return pieces(half, "seq", 2, lax.axis_index("seq") // 2, lax.axis_size("seq") // 2, 1)


def shard_pieces(half):
    return pieces(half, "shard", 1, lax.axis_index("shard"), lax.axis_size("shard"), 0)


def owners_half(part, then=()):
    count = lax.axis_size("seq")
    part, _ = spread(part, "seq", 2, lax.axis_index("seq") // 2, count // 2, 0, then)
    return part.reshape(-1, part.shape[-1])


def reduce_whole(grad):
    owned = lax.psum_scatter(grad, "shard", scatter_dimension=0, tiled=True)
    return lax.psum(owned.astype(f32), "seq")


def gain_grad(weight, gradient, gain):
    low = weight.astype(bf16).astype(f32)
    return jnp.sum(low * gradient.astype(f32), axis=1) / gain.astype(bf16).astype(f32)


def to_right(value):
    axes = ("seq", "shard")
    ends = lax.axis_size(axes) - 1
    return lax.ppermute(value, axes, [(i, i + 1) for i in range(ends)])


def to_left(value):
    axes = ("seq", "shard")
    ends = lax.axis_size(axes) - 1
    return lax.ppermute(value, axes, [(i + 1, i) for i in range(ends)])


def normed(hidden):
    centered = hidden - jnp.mean(hidden, axis=-1, keepdims=True)
    inverse = lax.rsqrt(jnp.mean(centered * centered, axis=-1, keepdims=True) + norm_epsilon)
    return centered * inverse, inverse


def normed_back(grad, gain, unit, inverse):
    inner = grad * gain
    mean = jnp.mean(inner, axis=-1, keepdims=True)
    slope = jnp.mean(inner * unit, axis=-1, keepdims=True)
    return inverse * (inner - mean - unit * slope)


def dot(a, b):
    return jnp.dot(a, b, preferred_element_type=f32)


def dot_rows(a, b):
    return lax.dot_general(a, b, (((1,), (1,)), ((), ())), preferred_element_type=f32)


def dot_columns(a, b):
    return lax.dot_general(a, b, (((0,), (0,)), ((), ())), preferred_element_type=f32)


def turned(values):
    lane = lax.broadcasted_iota(jnp.int32, values.shape, 1)
    up = pltpu.roll(values, LANES - 32, 1)
    down = pltpu.roll(values, 32, 1)
    return jnp.where(lane % 64 < 32, up, down)


def rope(values, cos, sin):
    return values * cos + turned(values) * sin


def rope_back(values, cos, sin):
    return values * cos - turned(values) * sin


def mask_bias(meta_ref, block):
    first = block * ROWS
    shape = (SPAN, ROWS)
    key = lax.broadcasted_iota(jnp.int32, shape, 0) + (first - HALF)
    query = lax.broadcasted_iota(jnp.int32, shape, 1) + first
    start, low, high = meta_ref[0], meta_ref[1], meta_ref[2]
    apart = jnp.abs(query - key) > HALF
    other = (query >= start) != (key >= start)
    outside = (key < low) | (key >= high)
    return jnp.where(apart | other | outside, masked_score, 0.0).astype(f32)


def stacked(values):
    lane = lax.broadcasted_iota(jnp.int32, values.shape, 1)
    zero = jnp.zeros_like(values)
    return jnp.concatenate(
        [jnp.where(lane < 64, values, zero), jnp.where(lane < 64, zero, values)], axis=0
    )


def unstacked(values):
    depth = lax.broadcasted_iota(jnp.int32, (LANES, ROWS), 0)
    return jnp.where(depth < 64, values[:, :ROWS], values[:, ROWS:])


def window(block):
    return slice(block * ROWS, block * ROWS + SPAN)


def assemble(place_ref, shards, quarters, copy):
    for c in (0, 1):

        @pl.when(place_ref[0] == c)
        def _(c=c):
            for side in (0, 1):
                for dq in range(quarters):
                    for dz in range(shards):
                        copy(
                            side,
                            c ^ side,
                            dq * shards + dz,
                            jnp.bitwise_xor(place_ref[1], dq),
                            jnp.bitwise_xor(place_ref[2], dz),
                        )


def project_kernel(x_ref, gain_ref, w_ref, cos_ref, sin_ref, h_ref, q_ref, k_ref, v_ref):
    unit, _ = normed(x_ref[...].astype(f32))
    low = (unit * gain_ref[0:1, :]).astype(bf16)
    h_ref[...] = low
    width = low.shape[1]
    cos, sin = cos_ref[...], sin_ref[...]
    for ref, at, scale in ((q_ref, 0, 0.125), (k_ref, width, None)):
        out = dot(low, w_ref[:, at : at + width])
        for j in range(0, width, LANES):
            value = rope(out[:, j : j + LANES], cos, sin)
            if scale is not None:
                value = value * scale
            ref[:, j : j + LANES] = value.astype(bf16)
    v_ref[...] = dot(low, w_ref[:, 2 * width :]).astype(bf16)


def project_edges_kernel(
    split, place_ref, x_ref, gain_ref, cos_ref, sin_ref, *refs
):
    *parts, head_ref, tail_ref, w_ref = refs
    if split:
        shards, quarters = split
        rows = parts[0].shape[0] // (shards * quarters)
        half = parts[0].shape[1]

        def copy(side, column, part, quarter, shard):
            at = pl.multiple_of((shard * quarters + quarter) * rows, 16)
            w_ref[pl.ds(at, rows), column * half : (column + 1) * half] = parts[side][
                part * rows : (part + 1) * rows, :
            ]

        assemble(place_ref, shards, quarters, copy)
    else:
        w_ref[...] = parts[0][...]
    unit, _ = normed(x_ref[...].astype(f32))
    low = (unit * gain_ref[0:1, :]).astype(bf16)
    width = low.shape[1]
    cos, sin = cos_ref[...], sin_ref[...]
    keys = dot(low, w_ref[:, width : 2 * width])
    for j in range(0, width, LANES):
        value = rope(keys[:, j : j + LANES], cos, sin).astype(bf16)
        head_ref[:, j : j + LANES] = value[:HALF]
        tail_ref[:, j : j + LANES] = value[HALF:]
    values = dot(low, w_ref[:, 2 * width :]).astype(bf16)
    head_ref[:, width:] = values[:HALF]
    tail_ref[:, width:] = values[HALF:]


def fill(dst, left, middle, right):
    rows = middle.shape[0]
    dst[0:HALF, :] = left[...]
    dst[HALF : HALF + rows, :] = middle[...]
    dst[HALF + rows :, :] = right[...]


def flip(dst, src, start, stop):
    for at in range(start, stop, LANES):
        dst[:, at : at + LANES] = src[at : at + LANES, :].T


def attend_kernel(
    meta_ref, q_ref, k_ref, v_ref, kl_ref, vl_ref, kr_ref, vr_ref, *refs
):
    o_ref, lse_ref, kx, vx, bias, vt = refs[-6:]
    blocks = q_ref.shape[0] // ROWS

    @pl.when(pl.program_id(0) == 0)
    def _():
        for n in range(blocks):
            bias[n] = mask_bias(meta_ref, n)

    fill(kx, kl_ref, k_ref, kr_ref)
    fill(vx, vl_ref, v_ref, vr_ref)
    flip(vt, vx, 0, vx.shape[0])
    for first in range(0, blocks, GROUP):
        group = range(first, min(first + GROUP, blocks))
        scores = []
        for n in group:
            queries = stacked(q_ref[n * ROWS : (n + 1) * ROWS, :])
            mask = bias[n]
            score = dot_rows(kx[window(n), :], queries)
            scores.append(score + jnp.concatenate([mask, mask], axis=1))
        tops = [jnp.max(score, axis=0, keepdims=True) for score in scores]
        weights = [jnp.exp(score - top) for score, top in zip(scores, tops)]
        totals = [jnp.sum(weight, axis=0, keepdims=True) for weight in weights]
        outs = [dot(vt[:, window(n)], weight.astype(bf16)) for n, weight in zip(group, weights)]
        for n, out, top, total in zip(group, outs, tops, totals):
            own = slice(n * ROWS, (n + 1) * ROWS)
            o_ref[:, own] = unstacked(out * (1.0 / total)).astype(bf16)
            lse_ref[0, n : n + 1, :] = top + jnp.log(total)


def back_blocks(
    blocks, dq_at, q_ref, do_ref, kx, vx, bias, kt, lse_ref, cos_ref, sin_ref, dq_ref, dkx, dvx
):
    for first in range(0, len(blocks), GROUP):
        group = blocks[first : first + GROUP]
        rows = [slice(n * ROWS, (n + 1) * ROWS) for n in group]
        queries = [stacked(q_ref[own, :]) for own in rows]
        grads = [stacked(do_ref[own, :]) for own in rows]
        scores = [dot_rows(kx[window(n), :], query) for n, query in zip(group, queries)]
        grad_probs = [dot_rows(vx[window(n), :], grad) for n, grad in zip(group, grads)]
        probs = []
        for n, score in zip(group, scores):
            mask = bias[n]
            mask = jnp.concatenate([mask, mask], axis=1)
            probs.append(jnp.exp(score + mask - lse_ref[0, n : n + 1, :]))
        inners = [jnp.sum(p * g, axis=0, keepdims=True) for p, g in zip(probs, grad_probs)]
        grad_scores = [
            (p * (g - inner)).astype(bf16) for p, g, inner in zip(probs, grad_probs, inners)
        ]
        grad_queries = [dot(kt[:, window(n)], ds) for n, ds in zip(group, grad_scores)]
        grad_values = [dot(p.astype(bf16), grad) for p, grad in zip(probs, grads)]
        grad_keys = [dot(ds, query) for ds, query in zip(grad_scores, queries)]
        for n, grad_value, grad_key in zip(group, grad_values, grad_keys):
            dvx[window(n), :] += grad_value
            dkx[window(n), :] += grad_key
        for n, own, grad_query in zip(group, rows, grad_queries):
            at = dq_at(n) * ROWS
            dq_ref[at : at + ROWS, :] = rope_back(
                unstacked(grad_query).T * 0.125, cos_ref[own, :], sin_ref[own, :]
            ).astype(bf16)


def attend_back_edges_kernel(
    meta_ref, q_ref, k_ref, v_ref, do_ref, kl_ref, vl_ref, kr_ref, vr_ref, lse_ref, cos_ref, sin_ref,
    dq_ref, wk_ref, wv_ref, head_ref, tail_ref, ek_ref, ev_ref,
    kx, vx, bias, kt, dkx, dvx,
):
    rows = q_ref.shape[0]
    blocks = rows // ROWS
    span = SPAN
    spans = (slice(0, span), slice(rows - ROWS, rows + 2 * HALF))

    @pl.when(pl.program_id(0) == 0)
    def _():
        for n in (0, blocks - 1):
            bias[n] = mask_bias(meta_ref, n)

    inside = span - HALF
    for x, left, own, right in ((kx, kl_ref, k_ref, kr_ref), (vx, vl_ref, v_ref, vr_ref)):
        x[0:HALF, :] = left[...]
        x[HALF:span, :] = own[:inside, :]
        x[HALF + rows - inside : HALF + rows, :] = own[rows - inside :, :]
        x[HALF + rows :, :] = right[...]
    for own in spans:
        flip(kt, kx, own.start, own.stop)
        for acc in (dkx, dvx):
            acc[own, :] = jnp.zeros((span, LANES), f32)
    back_blocks(
        (0, blocks - 1), lambda n: min(n, 1),
        q_ref, do_ref, kx, vx, bias, kt, lse_ref, cos_ref, sin_ref, dq_ref, dkx, dvx,
    )
    for ref, acc in ((wk_ref, dkx), (wv_ref, dvx)):
        ref[:span, :] = acc[spans[0], :]
        ref[span:, :] = acc[spans[1], :]
    for at, acc, ref in ((0, dkx, ek_ref), (1, dvx, ev_ref)):
        head_ref[at] = acc[0:HALF, :].astype(bf16)
        tail_ref[at] = acc[HALF + rows :, :].astype(bf16)
        ref[0:HALF, :] = acc[HALF : 2 * HALF, :]
        ref[HALF:, :] = acc[rows : rows + HALF, :]


def attend_back_kernel(
    meta_ref, q_ref, k_ref, v_ref, do_ref, kl_ref, vl_ref, kr_ref, vr_ref, lse_ref, cos_ref, sin_ref,
    eq_ref, wk_ref, wv_ref,
    dq_ref, dk_ref, dv_ref,
    kx, vx, bias, kt, dkx, dvx,
):
    rows = q_ref.shape[0]
    blocks = rows // ROWS
    span = SPAN

    @pl.when(pl.program_id(0) == 0)
    def _():
        for n in range(1, blocks - 1):
            bias[n] = mask_bias(meta_ref, n)

    fill(kx, kl_ref, k_ref, kr_ref)
    fill(vx, vl_ref, v_ref, vr_ref)
    flip(kt, kx, 0, kx.shape[0])
    last = slice(rows - ROWS, rows + 2 * HALF)
    for acc, ref in ((dkx, wk_ref), (dvx, wv_ref)):
        acc[:span, :] = ref[:span, :]
        acc[span : last.start, :] = jnp.zeros((last.start - span, LANES), f32)
        acc[last, :] = ref[span:, :]
    dq_ref[:ROWS, :] = eq_ref[:ROWS, :]
    dq_ref[rows - ROWS :, :] = eq_ref[ROWS:, :]
    back_blocks(
        range(1, blocks - 1), lambda n: n,
        q_ref, do_ref, kx, vx, bias, kt, lse_ref, cos_ref, sin_ref, dq_ref, dkx, dvx,
    )
    middle = slice(HALF, HALF + rows)
    dk_ref[...] = rope_back(dkx[middle, :], cos_ref[...], sin_ref[...]).astype(bf16)
    dv_ref[...] = dvx[middle, :].astype(bf16)


def pack_grads(ref, c, slots, acc_d, acc_m, acc_a):
    wide, narrow = acc_m.shape[1] // 2, acc_a.shape[1] // 2
    rows, down_rows = acc_m.shape[0] // slots, acc_d.shape[0] // slots
    ref[:, :wide] = acc_m[:, c * wide : (c + 1) * wide].astype(bf16)
    ref[:, wide : wide + narrow] = acc_a[:, c * narrow : (c + 1) * narrow].astype(bf16)
    fill_rows = jnp.zeros((2 * rows - down_rows, narrow), f32)
    for n in range(slots):
        own = slice(n * rows, (n + 1) * rows)
        block = acc_d[n * down_rows : (n + 1) * down_rows, c * narrow : (c + 1) * narrow]
        ref[own, wide + narrow : wide + 2 * narrow] = block[:rows].astype(bf16)
        rest = jnp.concatenate([block[rows:], fill_rows], axis=0)
        ref[own, wide + 2 * narrow :] = rest.astype(bf16)


def gather_middle(split, place_ref, step, parts, wa_ref, wm_ref, wd_ref):
    shards, quarters = split
    rows = parts[0].shape[0] // (shards * quarters)
    wide, narrow = wm_ref.shape[1] // 2, wa_ref.shape[1] // 2
    shard_rows = wd_ref.shape[0] // shards

    def copy(side, column, part, quarter, shard):
        own = slice(part * rows, (part + 1) * rows)
        ref = parts[side]
        lanes = slice(column * narrow, (column + 1) * narrow)
        at = pl.multiple_of((shard * quarters + quarter) * rows, 16)
        wm_ref[pl.ds(at, rows), column * wide : (column + 1) * wide] = ref[own, :wide]
        wa_ref[pl.ds(at, rows), lanes] = ref[own, wide : wide + narrow]
        at = shard * shard_rows + down_rows(quarter)
        first, second = wide + narrow, wide + 2 * narrow
        wd_ref[pl.ds(pl.multiple_of(at, 16), rows), lanes] = ref[own, first:second]
        rest = ref[own, second:]
        wd_ref[pl.ds(pl.multiple_of(at + rows, 16), 16), lanes] = rest[:16]

        @pl.when(quarter % 2 == 0)
        def _():
            wd_ref[pl.ds(pl.multiple_of(at + rows + 16, 16), 16), lanes] = rest[16:32]

    @pl.when(step == 0)
    def _():
        assemble(place_ref, shards, quarters, copy)


def middle_kernel(
    split, place_ref, x_ref, o_ref, ct_ref, gain_ref, *refs
):
    *refs, acc_d, acc_m, acc_a = refs
    step = pl.program_id(0)
    if split:
        own_part, other_part, out_ref, dmid_ref, do_ref, own_ref, other_ref, wa_ref, wm_ref, wd_ref = refs
        gather_middle(split, place_ref, step, (own_part, other_part), wa_ref, wm_ref, wd_ref)
    else:
        wa_ref, wm_ref, wd_ref, out_ref, dmid_ref, do_ref, *grad_refs = refs

    @pl.when(step == 0)
    def _():
        acc_d[...] = jnp.zeros_like(acc_d)
        acc_m[...] = jnp.zeros_like(acc_m)
        acc_a[...] = jnp.zeros_like(acc_a)

    gain = gain_ref[1:2, :]
    hidden = wd_ref.shape[0]
    chunk = hidden // 3
    ct = ct_ref[...]
    mid = x_ref[...].astype(f32) + dot_columns(o_ref[...], wa_ref[...])
    unit, inverse = normed(mid)
    low = (unit * gain).astype(bf16)
    low_t = low.T
    out = mid
    dh = jnp.zeros_like(mid)

    def ahead(at):
        first, second = slice(at, at + chunk), slice(hidden + at, hidden + at + chunk)
        products = dot(low, wm_ref[:, first]), dot(low, wm_ref[:, second])
        return first, second, *products, dot_rows(ct, wd_ref[first, :])

    begun = ahead(0)
    for at in range(0, hidden, chunk):
        first, second, a1, a2, du = begun
        if at + chunk < hidden:
            begun = ahead(at + chunk)
        phi = 0.5 * (1.0 + lax.erf(a1 * (1.0 / math.sqrt(2.0))))
        gate = a1 * phi
        u = (gate * a2).astype(bf16)
        slope = phi + a1 * (jnp.exp(-0.5 * a1 * a1) * (1.0 / math.sqrt(2.0 * math.pi)))
        da1 = (du * a2 * slope).astype(bf16)
        da2 = (du * gate).astype(bf16)
        out = out + dot(u, wd_ref[first, :])
        dh = dh + dot_rows(da1, wm_ref[:, first]) + dot_rows(da2, wm_ref[:, second])
        acc_d[first, :] += dot_columns(u, ct)
        acc_m[:, first] += dot(low_t, da1)
        acc_m[:, second] += dot(low_t, da2)
    out_ref[...] = out.astype(bf16)
    dmid = ct.astype(f32) + normed_back(dh, gain, unit, inverse)
    dmr = dmid.astype(bf16)
    dmid_ref[...] = dmr
    acc_a[...] += dot(o_ref[...], dmr)
    do_ref[...] = dot_rows(dmr, wa_ref[...]).astype(bf16)

    last = step == pl.num_programs(0) - 1
    if not split:

        @pl.when(last)
        def _():
            for ref, acc in zip(grad_refs, (acc_d, acc_m, acc_a)):
                ref[...] = acc[...].astype(bf16)

    else:
        slots = split[0] * split[1]
        for c in (0, 1):

            @pl.when(last & (place_ref[0] == c))
            def _(c=c):
                pack_grads(own_ref, c, slots, acc_d, acc_m, acc_a)
                pack_grads(other_ref, 1 - c, slots, acc_d, acc_m, acc_a)


def patched(step, steps, rows, value_ref, edge_ref):
    value = value_ref[...]
    edge = edge_ref[...]
    head = jnp.concatenate([edge[:HALF], value[HALF:]], axis=0)
    value = jnp.where(step == 0, head, value)
    tail = jnp.concatenate([value[: rows - HALF], edge[HALF:]], axis=0)
    return jnp.where(step == steps - 1, tail, value)


def qkv_grad_kernel(
    split, place_ref,
    h_ref, dq_ref, dk_ref, dv_ref, rk_ref, rv_ref, left_ref, right_ref, cos_ref, sin_ref,
    ek_ref, ev_ref, *refs,
):
    *grad_refs, acc = refs
    step, steps = pl.program_id(0), pl.num_programs(0)
    rows, width = h_ref.shape

    @pl.when(step == 0)
    def _():
        for at, side in ((0, left_ref), (HALF, right_ref)):
            own = slice(at, at + HALF)
            cos, sin = cos_ref[own, :], sin_ref[own, :]
            for j in range(0, width, LANES):
                lanes = slice(j, j + LANES)
                total = rk_ref[own, lanes] + side[0, :, lanes].astype(f32)
                ek_ref[own, lanes] = rope_back(total, cos, sin).astype(bf16)
            ev_ref[own, :] = (rv_ref[own, :] + side[1].astype(f32)).astype(bf16)

    @pl.when(step == 0)
    def _():
        acc[...] = jnp.zeros_like(acc)

    low = h_ref[...]
    acc[:, :width] += dot_columns(low, dq_ref[...])
    acc[:, width : 2 * width] += dot_columns(low, patched(step, steps, rows, dk_ref, ek_ref))
    acc[:, 2 * width :] += dot_columns(low, patched(step, steps, rows, dv_ref, ev_ref))

    last = step == steps - 1
    if not split:

        @pl.when(last)
        def _():
            grad_refs[0][...] = acc[...].astype(bf16)

    else:
        half = acc.shape[1] // 2
        for c in (0, 1):

            @pl.when(last & (place_ref[0] == c))
            def _(c=c):
                for ref, side in zip(grad_refs, (c, 1 - c)):
                    ref[...] = acc[:, side * half : (side + 1) * half].astype(bf16)


def input_kernel(x_ref, gain_ref, w_ref, dmid_ref, dq_ref, dk_ref, dv_ref, ek_ref, ev_ref, dx_ref):
    step, steps = pl.program_id(0), pl.num_programs(0)
    rows, width = x_ref.shape

    dh = dot_rows(dq_ref[...], w_ref[:, :width])
    dh = dh + dot_rows(patched(step, steps, rows, dk_ref, ek_ref), w_ref[:, width : 2 * width])
    dh = dh + dot_rows(patched(step, steps, rows, dv_ref, ev_ref), w_ref[:, 2 * width :])
    unit, inverse = normed(x_ref[...].astype(f32))
    dx = dmid_ref[...].astype(f32) + normed_back(dh, gain_ref[0:1, :], unit, inverse)
    dx_ref[...] = dx.astype(bf16)


def shaped(shape, dtype):
    return jax.ShapeDtypeStruct(shape, dtype)


def tiles(rows, columns):
    return pl.BlockSpec((rows, columns), lambda i: (i, 0))


def pairs(rows, offset=0):
    return pl.BlockSpec((rows, LANES), lambda i: (0, i + offset))


def kept(*shape):
    return pl.BlockSpec(shape, lambda i: (0,) * len(shape), pipeline_mode=pl.Buffered(1))


def held(*shape):
    return pl.BlockSpec(shape, lambda i: (0,) * len(shape))


def call(
    kernel, grid, in_specs, out_specs, out_shape, scratch, flops, moved, aliases=None
):
    return pl.pallas_call(
        kernel,
        grid=(grid,),
        in_specs=in_specs,
        out_specs=out_specs,
        out_shape=out_shape,
        scratch_shapes=scratch,
        input_output_aliases=aliases or {},
        compiler_params=pltpu.CompilerParams(
            vmem_limit_bytes=vmem_bytes, dimension_semantics=("arbitrary",)
        ),
        cost_estimate=pl.CostEstimate(
            flops=flops // 64, bytes_accessed=moved // 64, transcendentals=0
        ),
    )


def project(x, gains, weight, cos, sin):
    rows, width = x.shape
    tile = min(TILE, rows)
    return call(
        project_kernel,
        rows // tile,
        [tiles(tile, width), held(2, width), kept(*weight.shape), tiles(tile, LANES), tiles(tile, LANES)],
        [tiles(tile, width)] * 4,
        [shaped((rows, width), bf16)] * 4,
        [],
        2 * rows * width * 3 * width,
        rows * width * 10 + weight.size * 2,
    )(x, gains, weight, cos, sin)


def project_edges(split, place, x, gains, cos, sin, *parts):
    rows, width = x.shape
    return call(
        functools.partial(project_edges_kernel, split),
        1,
        [pl.BlockSpec(memory_space=pltpu.SMEM), held(rows, width), held(2, width)]
        + [held(rows, LANES)] * 2
        + [held(*part.shape) for part in parts],
        [held(HALF, 2 * width)] * 2 + [held(width, 3 * width)],
        [shaped((HALF, 2 * width), bf16)] * 2 + [shaped((width, 3 * width), bf16)],
        [],
        4 * rows * width * width,
        rows * width * 6 + width * width * 12,
    )(place, x, gains, cos, sin, *parts)


def attend_scratch(rows):
    extended = rows + 2 * HALF
    return [
        pltpu.VMEM((extended, LANES), bf16),
        pltpu.VMEM((extended, LANES), bf16),
        pltpu.VMEM((rows // ROWS, SPAN, ROWS), f32),
        pltpu.VMEM((LANES, extended), bf16),
    ]


def attend(meta, q, k, v, left, right, first, count, before=()):
    rows, width = q.shape
    steps = width // LANES

    def columns(height, offset=0):
        return pairs(height, first + offset)

    return call(
        attend_kernel,
        count,
        [pl.BlockSpec(memory_space=pltpu.SMEM)]
        + [columns(rows)] * 3
        + [columns(HALF), columns(HALF, steps)] * 2
        + [pl.BlockSpec(memory_space=pl.ANY)] * len(before),
        [
            pl.BlockSpec((LANES, rows), lambda i: (i + first, 0)),
            pl.BlockSpec((1, rows // ROWS, 2 * ROWS), lambda i: (i + first, 0, 0)),
        ],
        [shaped((width, rows), bf16), shaped((steps, rows // ROWS, 2 * ROWS), f32)],
        attend_scratch(rows),
        8 * rows * width * 256,
        rows * width * 8,
        {8 + at: at for at in range(len(before))},
    )(meta, q, k, v, left, left, right, right, *before)


def back_specs(rows, steps):
    return (
        [pl.BlockSpec(memory_space=pltpu.SMEM)]
        + [pairs(rows)] * 4
        + [pairs(HALF), pairs(HALF, steps)] * 2
        + [pl.BlockSpec((1, rows // ROWS, 2 * ROWS), lambda i: (i, 0, 0)), held(rows, LANES), held(rows, LANES)]
    )


def back_scratch(rows):
    extended = rows + 2 * HALF
    return attend_scratch(rows) + [pltpu.VMEM((extended, LANES), f32)] * 2


def attend_back_edges(meta, q, k, v, do, left, right, lse, cos, sin):
    rows, width = q.shape
    steps = width // LANES
    span = 2 * SPAN
    return call(
        attend_back_edges_kernel,
        steps,
        back_specs(rows, steps),
        [pairs(2 * ROWS)]
        + [pairs(span)] * 2
        + [pl.BlockSpec((2, HALF, LANES), lambda i: (0, 0, i))] * 2
        + [pairs(2 * HALF)] * 2,
        [shaped((2 * ROWS, width), bf16)]
        + [shaped((span, width), f32)] * 2
        + [shaped((2, HALF, width), bf16)] * 2
        + [shaped((2 * HALF, width), f32)] * 2,
        back_scratch(rows),
        20 * 2 * ROWS * width * 256,
        rows * width * 10,
    )(meta, q, k, v, do, left, left, right, right, lse, cos, sin)


def attend_back(meta, q, k, v, do, left, right, lse, cos, sin, edges):
    rows, width = q.shape
    steps = width // LANES
    span = 2 * SPAN
    return call(
        attend_back_kernel,
        steps,
        back_specs(rows, steps) + [pairs(2 * ROWS)] + [pairs(span)] * 2,
        [pairs(rows)] * 3,
        [shaped((rows, width), bf16)] * 3,
        back_scratch(rows),
        20 * rows * width * 256,
        rows * width * 14,
    )(meta, q, k, v, do, left, left, right, right, lse, cos, sin, *edges)


def middle(split, place, x, o, ct, gains, shapes, *weights):
    rows, width = x.shape
    tile = WIDE_TILE if rows % WIDE_TILE == 0 else rows
    wa, wm, wd = shapes
    if split:
        grads = [(width, wm[1] // 2 + 3 * (width // 2))] * 2
    else:
        grads = [wd, wm, wa]
    return call(
        functools.partial(middle_kernel, split),
        rows // tile,
        [
            pl.BlockSpec(memory_space=pltpu.SMEM),
            tiles(tile, width),
            pl.BlockSpec((width, tile), lambda i: (0, i)),
            tiles(tile, width),
            held(2, width),
        ]
        + [kept(*w.shape) for w in weights],
        [tiles(tile, width)] * 3 + [kept(*shape) for shape in grads],
        [shaped((rows, width), bf16)] * 3 + [shaped(shape, bf16) for shape in grads],
        ([pltpu.VMEM(w, bf16) for w in shapes] if split else [])
        + [pltpu.VMEM(wd, f32), pltpu.VMEM(wm, f32), pltpu.VMEM(wa, f32)],
        6 * rows * width * width * 5,
        rows * width * 14 + 20 * width * width,
    )(place, x, o, ct, gains, *weights)


def qkv_gradient(split, place, h, dq, dk, dv, ek, ev, left, right, cos, sin):
    rows, width = h.shape
    tile = min(TILE, rows)
    grads = [(width, 3 * width // 2)] * 2 if split else [(width, 3 * width)]
    return call(
        functools.partial(qkv_grad_kernel, split),
        rows // tile,
        [pl.BlockSpec(memory_space=pltpu.SMEM)]
        + [tiles(tile, width)] * 4
        + [held(2 * HALF, width)] * 2
        + [held(2, HALF, width)] * 2
        + [held(2 * HALF, LANES)] * 2,
        [held(2 * HALF, width)] * 2 + [held(*shape) for shape in grads],
        [shaped((2 * HALF, width), bf16)] * 2 + [shaped(shape, bf16) for shape in grads],
        [pltpu.VMEM((width, 3 * width), f32)],
        6 * rows * width * width,
        rows * width * 8 + 6 * width * width,
    )(place, h, dq, dk, dv, ek, ev, left, right, cos, sin)


def input_gradient(x, gains, weight, dmid, dq, dk, dv, ek, ev):
    rows, width = x.shape
    tile = min(TILE, rows)
    return call(
        input_kernel,
        rows // tile,
        [tiles(tile, width), held(2, width), kept(*weight.shape)]
        + [tiles(tile, width)] * 4
        + [held(2 * HALF, width)] * 2,
        tiles(tile, width),
        shaped((rows, width), bf16),
        [],
        6 * rows * width * width,
        rows * width * 14 + 6 * width * width,
    )(x, gains, weight, dmid, dq, dk, dv, ek, ev)


def rope_tables(positions, head_size):
    half_size = head_size // 2
    exponent = jnp.arange(half_size, dtype=f32) * (2.0 / head_size)
    inverse = rope_theta ** (-exponent)
    inverse = jnp.tile(inverse, LANES // half_size)
    angles = positions.astype(f32)[:, None] * inverse[None, :]
    sign = jnp.where(jnp.arange(LANES) % head_size < half_size, -1.0, 1.0).astype(f32)
    return jnp.cos(angles), jnp.sin(angles) * sign


def adam_update(master, first_moment, second_moment, gradient, step_rate):
    gradient = gradient.astype(f32)
    new_first = beta_first * first_moment + (1.0 - beta_first) * gradient
    new_second = beta_second * second_moment + (1.0 - beta_second) * gradient * gradient
    first_hat = new_first / (1.0 - beta_first**ADAM_STEP)
    second_hat = new_second / (1.0 - beta_second**ADAM_STEP)
    new_master = master - step_rate * (
        decay_rate * master + first_hat / (jnp.sqrt(second_hat) + adam_epsilon)
    )
    return (new_first, new_second, new_master)


def edge_rows(value):
    return value[:HALF], value[value.shape[0] - HALF :]


def per_device(
    tokens,
    positions,
    cotangent,
    qkv_weight,
    attn_weight,
    mlp_weight,
    down_weight,
    norm_gains,
    qkv_first,
    qkv_second,
    attn_first,
    attn_second,
    mlp_first,
    mlp_second,
    down_first,
    down_second,
    gains_first,
    gains_second,
):
    rows, width = tokens.shape
    device = lax.axis_index(("seq", "shard"))
    last_device = lax.axis_size(("seq", "shard")) - 1
    cos, sin = rope_tables(positions, width // HEADS)
    start = jnp.max(jnp.where(positions == 0, jnp.arange(rows, dtype=jnp.int32), 0))
    low = jnp.where(device > 0, -HALF, 0)
    high = jnp.where(device < last_device, rows + HALF, rows)
    meta = jnp.stack([start, low, high]).astype(jnp.int32)
    edge_x, edge_cos, edge_sin = (
        jnp.concatenate(edge_rows(value), axis=0) for value in (tokens, cos, sin)
    )
    shards = lax.axis_size("shard")
    quarters = lax.axis_size("seq") // 2
    core = lax.axis_index("seq") % 2
    split = (shards, quarters) if split_pays() else None
    place = jnp.stack([core, lax.axis_index("seq") // 2, lax.axis_index("shard")])
    place = place.astype(jnp.int32)
    half = qkv_weight.shape[1] // 2
    slot = qkv_weight.shape[0] // quarters
    rest = down_weight.shape[0] // quarters - slot
    wide = mlp_weight.shape[1] // 2
    down_at = wide + attn_weight.shape[1] // 2
    lows = [w.astype(bf16) for w in (qkv_weight, attn_weight, mlp_weight, down_weight)]
    if split:
        qkv_low, attn_low, mlp_low, down_low = lows
        part = quarter_rows(halves(qkv_low, core))
        gain_rows = jnp.pad(norm_gains.astype(bf16), ((0, 6), (0, half - norm_gains.shape[1])))
        qkv_stack = stack(jnp.concatenate([part, gain_rows], axis=0), "shard", 1)
        gains = jnp.zeros((shards, 2, norm_gains.shape[1]), bf16)
        for d, piece in enumerate(qkv_stack):
            piece = piece[None, slot : slot + 2, : norm_gains.shape[1]]
            gains = lax.dynamic_update_slice_in_dim(gains, piece, lax.axis_index("shard") ^ d, 0)
        gains = gains.astype(f32).transpose(1, 0, 2).reshape(2, -1)
        rest_part = jnp.concatenate(
            [quarter_rows(halves(w, core)) for w in (mlp_low, attn_low)]
            + down_part(halves(down_low, core), slot),
            axis=1,
        )
        rest_part = jnp.concatenate(
            stack(after(rest_part, qkv_stack[1]), "shard", 1), axis=0
        )
        qkv_part = jnp.concatenate([piece[:slot] for piece in qkv_stack], axis=0)
        qkv_part = jnp.concatenate(stack(qkv_part, "seq", 2), axis=0)
        qkv_part = after(qkv_part, rest_part, gains, meta, place, edge_x, edge_cos, edge_sin)
        rest_part = after(rest_part, qkv_part)
        qkv_parts = qkv_part, swap(qkv_part, "seq", 1)
    else:
        full_qkv, full_attn, full_mlp, full_down = (
            lax.all_gather(w, "shard", axis=0, tiled=True) for w in lows
        )
        gains = lax.all_gather(norm_gains.astype(bf16), "shard", axis=1, tiled=True).astype(f32)
        qkv_parts = (full_qkv,)
    kv_head, kv_tail, full_qkv = project_edges(
        split, place, edge_x, gains, edge_cos, edge_sin, *qkv_parts
    )
    left = to_right(kv_tail)
    right = to_left(kv_head)
    h, q, k, v = project(after(tokens, kv_head), gains, full_qkv, cos, sin)
    left = after(left, k)
    right = after(right, k)
    pair_count = width // LANES
    before = attend(meta, q, k, v, left, right, 0, pair_count // 2)
    if split:
        rest_part = jnp.concatenate(stack(rest_part, "seq", 2, (before[0],)), axis=0)
        rest_weights = rest_part, swap(rest_part, "seq", 1)
        q = after(q, rest_part)
    else:
        rest_weights = full_attn, full_mlp, full_down
    o, lse = attend(
        meta, q, k, v, left, right, pair_count // 2, pair_count - pair_count // 2, before
    )
    shapes = (
        (width, attn_weight.shape[1]),
        (width, mlp_weight.shape[1]),
        (shards * down_weight.shape[0], width),
    )
    layer_output, dmid, do, *rest_grads = middle(
        split, place, tokens, o, cotangent, gains, shapes, *rest_weights
    )
    if split:
        rest_own, rest_other = rest_grads
        rest_got = swap(rest_other, "seq", 1)
    back_args = (meta, q, k, v, do, left, right, lse, cos, sin)
    *edges, halo_head, halo_tail, raw_k, raw_v = attend_back_edges(*back_args)
    from_right = to_left(halo_head)
    from_left = to_right(halo_tail)
    if split:
        rest_half = keep_half(rest_own, after(rest_got, halo_head))
        do = after(do, rest_half)
        back_args = (meta, q, k, v, do, left, right, lse, cos, sin)
        rest_pieces = quarter_pieces(rest_half)
    dq, dk, dv = attend_back(*back_args, edges)
    edge_k, edge_v, *qkv_grads = qkv_gradient(
        split, place, h, dq, dk, dv, raw_k, raw_v, after(from_left, dq), after(from_right, dq), edge_cos, edge_sin
    )
    if split:
        qkv_own, qkv_other = qkv_grads
        rest_part = sum_after(rest_pieces, qkv_own)
        qkv_got = swap(after(qkv_other, rest_part), "seq", 1)
        qkv_half = keep_half(qkv_own, qkv_got)
        dq = after(dq, qkv_half)
        qkv_pieces = quarter_pieces(qkv_half)
        rest_pieces = shard_pieces(rest_part)
    input_grad = input_gradient(tokens, gains, full_qkv, dmid, dq, dk, dv, edge_k, edge_v)
    if split:
        qkv_part = sum_after(qkv_pieces, input_grad)
        rest_part = sum_after(rest_pieces, qkv_part)
        qkv_part = sum_after(shard_pieces(qkv_part), rest_part)
        rest_half = owners_half(rest_part, (qkv_part,))
        rest_got = swap(rest_half, "seq", 1)
        qkv_half = owners_half(qkv_part, (rest_half,))
        qkv_got = swap(qkv_half, "seq", 1)
        first, second = by_core(core, rest_half, after(rest_got, qkv_half))
        mlp_total = side_by_side(first[:, :wide], second[:, :wide])
        attn_total = side_by_side(first[:, wide:down_at], second[:, wide:down_at])
        down_total = side_by_side(
            *(unpack_down(x[:, down_at:], quarters, rest) for x in (first, second))
        )
    else:
        down_total, mlp_total, attn_total, qkv_total = (
            reduce_whole(g) for g in (*rest_grads, *qkv_grads)
        )
    attn_new = adam_update(attn_weight, attn_first, attn_second, attn_total, rate_matrix)
    mlp_new = adam_update(mlp_weight, mlp_first, mlp_second, mlp_total, rate_matrix)
    down_new = adam_update(down_weight, down_first, down_second, down_total, rate_matrix)
    if split:
        qkv_got = after(qkv_got, attn_new[0], mlp_new[0], down_new[0])
        qkv_total = side_by_side(*by_core(core, qkv_half, qkv_got))
    qkv_new = adam_update(qkv_weight, qkv_first, qkv_second, qkv_total, rate_matrix)
    gains_total = jnp.stack(
        [
            gain_grad(qkv_weight, qkv_total, norm_gains[0]),
            gain_grad(mlp_weight, mlp_total, norm_gains[1]),
        ]
    )
    gains_new = adam_update(norm_gains, gains_first, gains_second, gains_total, rate_gains)
    return (layer_output, input_grad, *qkv_new, *attn_new, *mlp_new, *down_new, *gains_new)


def solution(mesh):
    tokens, rows, columns = P(("seq", "shard"), None), P("shard", None), P(None, "shard")
    matrices = (rows,) * 4
    return jax.shard_map(
        per_device,
        mesh=mesh,
        in_specs=(tokens, P(("seq", "shard")), tokens, *matrices, columns)
        + (rows,) * 8
        + (columns,) * 2,
        out_specs=(tokens, tokens) + (rows,) * 12 + (columns,) * 3,
        check_vma=False,
    )
```

```python
import functools
import math

import jax
import jax.numpy as jnp
from jax import lax
from jax.experimental import pallas as pl
from jax.experimental.pallas import tpu as pltpu
from jax.sharding import PartitionSpec as P

HEADS = 12
HALF = 64
ADAM_STEP = 5
LANES = 128
ROWS = 128
SPAN = ROWS + 2 * HALF
TILE = 256
WIDE_TILE = 640
GROUP = 2


norm_epsilon = 1e-05
rope_theta = 10000.0
beta_first = 0.9
beta_second = 0.98
adam_epsilon = 1e-06
decay_rate = 1e-05
rate_matrix = 0.04
rate_gains = 0.2
masked_score = -1e30
vmem_bytes = 60 * 1024 * 1024

f32 = jnp.float32
bf16 = jnp.bfloat16


def swap(value, axis, flip):
    count = lax.axis_size(axis)
    return lax.ppermute(value, axis, [(i, i ^ flip) for i in range(count)])


def after(value, *others):
    return lax.optimization_barrier((value, *others))[0]


def spread(part, axis, unit, index, count, dim, then=()):
    out = jnp.zeros(part.shape[:dim] + (count,) + part.shape[dim:], part.dtype)
    pieces = [part] + [after(swap(part, axis, unit * d), *then) for d in range(1, count)]
    for d, piece in enumerate(pieces):
        out = lax.dynamic_update_slice_in_dim(out, jnp.expand_dims(piece, dim), index ^ d, dim)
    return out, pieces[1:]


def places():
    core = lax.axis_index("seq") % 2
    return core, lax.axis_index("seq") // 2, lax.axis_index("shard")


def by_core(core, own, other):
    return jnp.where(core == 0, own, other), jnp.where(core == 0, other, own)


def split_pays():
    count, shards = lax.axis_size("seq"), lax.axis_size("shard")
    return count == 8 and shards == 4


def own_block(weight, start, rows):
    width = weight.shape[1] // 2
    core = lax.axis_index("seq") % 2
    return lax.dynamic_slice(weight, (start, core * width), (rows, width)).astype(bf16)


def stack(part, axis, unit, then=()):
    count = lax.axis_size(axis) // unit
    others = [after(swap(part, axis, unit * d), *then) for d in range(1, count)]
    return [part] + others


def doubled(part, flip):
    return jnp.concatenate([part, swap(part, "shard", flip)], axis=0)


def down_rows(quarter):
    return 72 * quarter + 8 * (quarter % 2)


def down_part(weight, rows):
    start = down_rows(lax.axis_index("seq") // 2)
    last = jnp.minimum(start + 64, weight.shape[0] - 16)
    block = jnp.concatenate([own_block(weight, start, 64), own_block(weight, last, 16)], axis=0)
    return pack_down(block[None], rows)


def pack_down(blocks, rows):
    rest = blocks.shape[1] - rows
    second = jnp.pad(blocks[:, rows:], ((0, 0), (0, rows - rest), (0, 0)))
    columns = blocks.shape[2]
    return [blocks[:, :rows].reshape(-1, columns), second.reshape(-1, columns)]


def unpack_down(packed, blocks, rest):
    columns = packed.shape[1] // 2
    packed = packed.reshape(blocks, -1, 2 * columns)
    whole = jnp.concatenate([packed[:, :, :columns], packed[:, :rest, columns:]], axis=1)
    return whole.reshape(-1, columns)


def side_by_side(first, second):
    return jnp.concatenate([first, second], axis=1)


def total_of(pieces):
    total = pieces[0].astype(f32)
    for piece in pieces[1:]:
        total = total + piece.astype(f32)
    return total.astype(bf16)


def keep_half(own, got):
    shards, quarters = lax.axis_size("shard"), lax.axis_size("seq") // 2
    return total_of([own, got]).reshape(shards, quarters, -1, own.shape[1])


def sum_after(parts, *others):
    return total_of(parts[:1] + [after(part, *others) for part in parts[1:]])


def pieces(value, axis, unit, index, count, dim):
    def at(place):
        return lax.dynamic_index_in_dim(value, place, dim, keepdims=False)

    return [at(index)] + [swap(at(index ^ d), axis, unit * d) for d in range(1, count)]


def quarter_pieces(half):
    return pieces(half, "seq", 2, lax.axis_index("seq") // 2, lax.axis_size("seq") // 2, 1)


def shard_pieces(half):
    return pieces(half, "shard", 1, lax.axis_index("shard"), lax.axis_size("shard"), 0)


def halve(value, bit):
    side = lax.axis_index("shard") & bit
    kept_half = lax.dynamic_slice_in_dim(value, side, bit, 0)
    return kept_half, swap(lax.dynamic_slice_in_dim(value, side ^ bit, bit, 0), "shard", bit)


def owners_half(part, then=()):
    count = lax.axis_size("seq")
    part, _ = spread(part, "seq", 2, lax.axis_index("seq") // 2, count // 2, 0, then)
    return part.reshape(-1, part.shape[-1])


def reduce_whole(grad):
    owned = lax.psum_scatter(grad, "shard", scatter_dimension=0, tiled=True)
    return lax.psum(owned.astype(f32), "seq")


def gain_grad(weight, gradient, gain):
    low = weight.astype(bf16).astype(f32)
    return jnp.sum(low * gradient.astype(f32), axis=1) / gain.astype(bf16).astype(f32)


def to_right(value):
    axes = ("seq", "shard")
    ends = lax.axis_size(axes) - 1
    return lax.ppermute(value, axes, [(i, i + 1) for i in range(ends)])


def to_left(value):
    axes = ("seq", "shard")
    ends = lax.axis_size(axes) - 1
    return lax.ppermute(value, axes, [(i + 1, i) for i in range(ends)])


def normed(hidden):
    centered = hidden - jnp.mean(hidden, axis=-1, keepdims=True)
    inverse = lax.rsqrt(jnp.mean(centered * centered, axis=-1, keepdims=True) + norm_epsilon)
    return centered * inverse, inverse


def normed_back(grad, gain, unit, inverse):
    inner = grad * gain
    mean = jnp.mean(inner, axis=-1, keepdims=True)
    slope = jnp.mean(inner * unit, axis=-1, keepdims=True)
    return inverse * (inner - mean - unit * slope)


def dot(a, b):
    return jnp.dot(a, b, preferred_element_type=f32)


def dot_rows(a, b):
    return lax.dot_general(a, b, (((1,), (1,)), ((), ())), preferred_element_type=f32)


def dot_columns(a, b):
    return lax.dot_general(a, b, (((0,), (0,)), ((), ())), preferred_element_type=f32)


def turned(values):
    lane = lax.broadcasted_iota(jnp.int32, values.shape, 1)
    up = pltpu.roll(values, LANES - 32, 1)
    down = pltpu.roll(values, 32, 1)
    return jnp.where(lane % 64 < 32, up, down)


def rope(values, cos, sin):
    return values * cos + turned(values) * sin


def rope_back(values, cos, sin):
    return values * cos - turned(values) * sin


def mask_bias(meta_ref, block):
    first = block * ROWS
    shape = (SPAN, ROWS)
    key = lax.broadcasted_iota(jnp.int32, shape, 0) + (first - HALF)
    query = lax.broadcasted_iota(jnp.int32, shape, 1) + first
    start, low, high = meta_ref[0], meta_ref[1], meta_ref[2]
    apart = jnp.abs(query - key) > HALF
    other = (query >= start) != (key >= start)
    outside = (key < low) | (key >= high)
    return jnp.where(apart | other | outside, masked_score, 0.0).astype(f32)


def stacked(values):
    lane = lax.broadcasted_iota(jnp.int32, values.shape, 1)
    zero = jnp.zeros_like(values)
    return jnp.concatenate(
        [jnp.where(lane < 64, values, zero), jnp.where(lane < 64, zero, values)], axis=0
    )


def unstacked(values):
    depth = lax.broadcasted_iota(jnp.int32, (LANES, ROWS), 0)
    return jnp.where(depth < 64, values[:, :ROWS], values[:, ROWS:])


def window(block):
    return slice(block * ROWS, block * ROWS + SPAN)


def assemble(place_ref, shards, quarters, copy):
    for c in (0, 1):

        @pl.when(place_ref[0] == c)
        def _(c=c):
            for side in (0, 1):
                for dq in range(quarters):
                    for dz in range(shards):
                        copy(
                            side,
                            c ^ side,
                            dq * shards + dz,
                            jnp.bitwise_xor(place_ref[1], dq),
                            jnp.bitwise_xor(place_ref[2], dz),
                        )


def project_kernel(x_ref, gain_ref, w_ref, cos_ref, sin_ref, h_ref, q_ref, k_ref, v_ref):
    unit, _ = normed(x_ref[...].astype(f32))
    low = (unit * gain_ref[0:1, :]).astype(bf16)
    h_ref[...] = low
    width = low.shape[1]
    cos, sin = cos_ref[...], sin_ref[...]
    for ref, at, scale in ((q_ref, 0, 0.125), (k_ref, width, None)):
        out = dot(low, w_ref[:, at : at + width])
        for j in range(0, width, LANES):
            value = rope(out[:, j : j + LANES], cos, sin)
            if scale is not None:
                value = value * scale
            ref[:, j : j + LANES] = value.astype(bf16)
    v_ref[...] = dot(low, w_ref[:, 2 * width :]).astype(bf16)


def project_edges_kernel(
    split, place_ref, x_ref, gain_ref, cos_ref, sin_ref, *refs
):
    *parts, head_ref, tail_ref, w_ref = refs
    if split:
        shards, quarters = split
        rows = parts[0].shape[0] // (shards * quarters)
        half = parts[0].shape[1]

        def copy(side, column, part, quarter, shard):
            at = pl.multiple_of((shard * quarters + quarter) * rows, 16)
            w_ref[pl.ds(at, rows), column * half : (column + 1) * half] = parts[side][
                part * rows : (part + 1) * rows, :
            ]

        assemble(place_ref, shards, quarters, copy)
    else:
        w_ref[...] = parts[0][...]
    unit, _ = normed(x_ref[...].astype(f32))
    low = (unit * gain_ref[0:1, :]).astype(bf16)
    width = low.shape[1]
    cos, sin = cos_ref[...], sin_ref[...]
    keys = dot(low, w_ref[:, width : 2 * width])
    for j in range(0, width, LANES):
        value = rope(keys[:, j : j + LANES], cos, sin).astype(bf16)
        head_ref[:, j : j + LANES] = value[:HALF]
        tail_ref[:, j : j + LANES] = value[HALF:]
    values = dot(low, w_ref[:, 2 * width :]).astype(bf16)
    head_ref[:, width:] = values[:HALF]
    tail_ref[:, width:] = values[HALF:]


def fill(dst, left, middle, right):
    rows = middle.shape[0]
    dst[0:HALF, :] = left[...]
    dst[HALF : HALF + rows, :] = middle[...]
    dst[HALF + rows :, :] = right[...]


def flip(dst, src, start, stop):
    for at in range(start, stop, LANES):
        dst[:, at : at + LANES] = src[at : at + LANES, :].T


def attend_kernel(
    meta_ref, q_ref, k_ref, v_ref, kl_ref, vl_ref, kr_ref, vr_ref, *refs
):
    o_ref, lse_ref, kx, vx, bias, vt = refs[-6:]
    blocks = q_ref.shape[0] // ROWS

    @pl.when(pl.program_id(0) == 0)
    def _():
        for n in range(blocks):
            bias[n] = mask_bias(meta_ref, n)

    fill(kx, kl_ref, k_ref, kr_ref)
    fill(vx, vl_ref, v_ref, vr_ref)
    flip(vt, vx, 0, vx.shape[0])
    for first in range(0, blocks, GROUP):
        group = range(first, min(first + GROUP, blocks))
        scores = []
        for n in group:
            queries = stacked(q_ref[n * ROWS : (n + 1) * ROWS, :])
            mask = bias[n]
            score = dot_rows(kx[window(n), :], queries)
            scores.append(score + jnp.concatenate([mask, mask], axis=1))
        tops = [jnp.max(score, axis=0, keepdims=True) for score in scores]
        weights = [jnp.exp(score - top) for score, top in zip(scores, tops)]
        totals = [jnp.sum(weight, axis=0, keepdims=True) for weight in weights]
        outs = [dot(vt[:, window(n)], weight.astype(bf16)) for n, weight in zip(group, weights)]
        for n, out, top, total in zip(group, outs, tops, totals):
            own = slice(n * ROWS, (n + 1) * ROWS)
            o_ref[:, own] = unstacked(out * (1.0 / total)).astype(bf16)
            lse_ref[0, n : n + 1, :] = top + jnp.log(total)


def back_blocks(
    blocks, dq_at, q_ref, do_ref, kx, vx, bias, kt, lse_ref, cos_ref, sin_ref, dq_ref, dkx, dvx
):
    for first in range(0, len(blocks), GROUP):
        group = blocks[first : first + GROUP]
        rows = [slice(n * ROWS, (n + 1) * ROWS) for n in group]
        queries = [stacked(q_ref[own, :]) for own in rows]
        grads = [stacked(do_ref[own, :]) for own in rows]
        scores = [dot_rows(kx[window(n), :], query) for n, query in zip(group, queries)]
        grad_probs = [dot_rows(vx[window(n), :], grad) for n, grad in zip(group, grads)]
        probs = []
        for n, score in zip(group, scores):
            mask = bias[n]
            mask = jnp.concatenate([mask, mask], axis=1)
            probs.append(jnp.exp(score + mask - lse_ref[0, n : n + 1, :]))
        inners = [jnp.sum(p * g, axis=0, keepdims=True) for p, g in zip(probs, grad_probs)]
        grad_scores = [
            (p * (g - inner)).astype(bf16) for p, g, inner in zip(probs, grad_probs, inners)
        ]
        grad_queries = [dot(kt[:, window(n)], ds) for n, ds in zip(group, grad_scores)]
        grad_values = [dot(p.astype(bf16), grad) for p, grad in zip(probs, grads)]
        grad_keys = [dot(ds, query) for ds, query in zip(grad_scores, queries)]
        for n, grad_value, grad_key in zip(group, grad_values, grad_keys):
            dvx[window(n), :] += grad_value
            dkx[window(n), :] += grad_key
        for n, own, grad_query in zip(group, rows, grad_queries):
            at = dq_at(n) * ROWS
            dq_ref[at : at + ROWS, :] = rope_back(
                unstacked(grad_query).T * 0.125, cos_ref[own, :], sin_ref[own, :]
            ).astype(bf16)


def attend_back_edges_kernel(
    meta_ref, q_ref, k_ref, v_ref, do_ref, kl_ref, vl_ref, kr_ref, vr_ref, lse_ref, cos_ref, sin_ref,
    dq_ref, wk_ref, wv_ref, head_ref, tail_ref, ek_ref, ev_ref,
    kx, vx, bias, kt, dkx, dvx,
):
    rows = q_ref.shape[0]
    blocks = rows // ROWS
    span = SPAN
    spans = (slice(0, span), slice(rows - ROWS, rows + 2 * HALF))

    @pl.when(pl.program_id(0) == 0)
    def _():
        for n in (0, blocks - 1):
            bias[n] = mask_bias(meta_ref, n)

    inside = span - HALF
    for x, left, own, right in ((kx, kl_ref, k_ref, kr_ref), (vx, vl_ref, v_ref, vr_ref)):
        x[0:HALF, :] = left[...]
        x[HALF:span, :] = own[:inside, :]
        x[HALF + rows - inside : HALF + rows, :] = own[rows - inside :, :]
        x[HALF + rows :, :] = right[...]
    for own in spans:
        flip(kt, kx, own.start, own.stop)
        for acc in (dkx, dvx):
            acc[own, :] = jnp.zeros((span, LANES), f32)
    back_blocks(
        (0, blocks - 1), lambda n: min(n, 1),
        q_ref, do_ref, kx, vx, bias, kt, lse_ref, cos_ref, sin_ref, dq_ref, dkx, dvx,
    )
    for ref, acc in ((wk_ref, dkx), (wv_ref, dvx)):
        ref[:span, :] = acc[spans[0], :]
        ref[span:, :] = acc[spans[1], :]
    for at, acc, ref in ((0, dkx, ek_ref), (1, dvx, ev_ref)):
        head_ref[at] = acc[0:HALF, :].astype(bf16)
        tail_ref[at] = acc[HALF + rows :, :].astype(bf16)
        ref[0:HALF, :] = acc[HALF : 2 * HALF, :]
        ref[HALF:, :] = acc[rows : rows + HALF, :]


def attend_back_kernel(
    meta_ref, q_ref, k_ref, v_ref, do_ref, kl_ref, vl_ref, kr_ref, vr_ref, lse_ref, cos_ref, sin_ref,
    eq_ref, wk_ref, wv_ref,
    dq_ref, dk_ref, dv_ref,
    kx, vx, bias, kt, dkx, dvx,
):
    rows = q_ref.shape[0]
    blocks = rows // ROWS
    span = SPAN

    @pl.when(pl.program_id(0) == 0)
    def _():
        for n in range(1, blocks - 1):
            bias[n] = mask_bias(meta_ref, n)

    fill(kx, kl_ref, k_ref, kr_ref)
    fill(vx, vl_ref, v_ref, vr_ref)
    flip(kt, kx, 0, kx.shape[0])
    last = slice(rows - ROWS, rows + 2 * HALF)
    for acc, ref in ((dkx, wk_ref), (dvx, wv_ref)):
        acc[:span, :] = ref[:span, :]
        acc[span : last.start, :] = jnp.zeros((last.start - span, LANES), f32)
        acc[last, :] = ref[span:, :]
    dq_ref[:ROWS, :] = eq_ref[:ROWS, :]
    dq_ref[rows - ROWS :, :] = eq_ref[ROWS:, :]
    back_blocks(
        range(1, blocks - 1), lambda n: n,
        q_ref, do_ref, kx, vx, bias, kt, lse_ref, cos_ref, sin_ref, dq_ref, dkx, dvx,
    )
    middle = slice(HALF, HALF + rows)
    dk_ref[...] = rope_back(dkx[middle, :], cos_ref[...], sin_ref[...]).astype(bf16)
    dv_ref[...] = dvx[middle, :].astype(bf16)


def pack_grads(ref, c, slots, acc_d, acc_m, acc_a):
    wide, narrow = acc_m.shape[1] // 2, acc_a.shape[1] // 2
    rows, down_rows = acc_m.shape[0] // slots, acc_d.shape[0] // slots
    ref[:, :wide] = acc_m[:, c * wide : (c + 1) * wide].astype(bf16)
    ref[:, wide : wide + narrow] = acc_a[:, c * narrow : (c + 1) * narrow].astype(bf16)
    fill_rows = jnp.zeros((2 * rows - down_rows, narrow), f32)
    for n in range(slots):
        own = slice(n * rows, (n + 1) * rows)
        block = acc_d[n * down_rows : (n + 1) * down_rows, c * narrow : (c + 1) * narrow]
        ref[own, wide + narrow : wide + 2 * narrow] = block[:rows].astype(bf16)
        rest = jnp.concatenate([block[rows:], fill_rows], axis=0)
        ref[own, wide + 2 * narrow :] = rest.astype(bf16)


def gather_middle(split, place_ref, step, parts, wa_ref, wm_ref, wd_ref):
    shards, quarters = split
    rows = parts[0].shape[0] // (shards * quarters)
    wide, narrow = wm_ref.shape[1] // 2, wa_ref.shape[1] // 2
    shard_rows = wd_ref.shape[0] // shards

    def copy(side, column, part, quarter, shard):
        own = slice(part * rows, (part + 1) * rows)
        ref = parts[side]
        lanes = slice(column * narrow, (column + 1) * narrow)
        at = pl.multiple_of((shard * quarters + quarter) * rows, 16)
        wm_ref[pl.ds(at, rows), column * wide : (column + 1) * wide] = ref[own, :wide]
        wa_ref[pl.ds(at, rows), lanes] = ref[own, wide : wide + narrow]
        at = shard * shard_rows + down_rows(quarter)
        first, second = wide + narrow, wide + 2 * narrow
        wd_ref[pl.ds(pl.multiple_of(at, 16), rows), lanes] = ref[own, first:second]
        rest = ref[own, second:]
        wd_ref[pl.ds(pl.multiple_of(at + rows, 16), 16), lanes] = rest[:16]

        @pl.when(quarter % 2 == 0)
        def _():
            wd_ref[pl.ds(pl.multiple_of(at + rows + 16, 16), 16), lanes] = rest[16:32]

    @pl.when(step == 0)
    def _():
        assemble(place_ref, shards, quarters, copy)


def middle_kernel(
    split, place_ref, x_ref, o_ref, ct_ref, gain_ref, *refs
):
    *refs, acc_d, acc_m, acc_a = refs
    step = pl.program_id(0)
    if split:
        own_part, other_part, out_ref, dmid_ref, do_ref, own_ref, other_ref, wa_ref, wm_ref, wd_ref = refs
        gather_middle(split, place_ref, step, (own_part, other_part), wa_ref, wm_ref, wd_ref)
    else:
        wa_ref, wm_ref, wd_ref, out_ref, dmid_ref, do_ref, *grad_refs = refs

    @pl.when(step == 0)
    def _():
        acc_d[...] = jnp.zeros_like(acc_d)
        acc_m[...] = jnp.zeros_like(acc_m)
        acc_a[...] = jnp.zeros_like(acc_a)

    gain = gain_ref[1:2, :]
    hidden = wd_ref.shape[0]
    chunk = hidden // 3
    ct = ct_ref[...]
    mid = x_ref[...].astype(f32) + dot_columns(o_ref[...], wa_ref[...])
    unit, inverse = normed(mid)
    low = (unit * gain).astype(bf16)
    low_t = low.T
    out = mid
    dh = jnp.zeros_like(mid)

    def ahead(at):
        first, second = slice(at, at + chunk), slice(hidden + at, hidden + at + chunk)
        products = dot(low, wm_ref[:, first]), dot(low, wm_ref[:, second])
        return first, second, *products, dot_rows(ct, wd_ref[first, :])

    begun = ahead(0)
    for at in range(0, hidden, chunk):
        first, second, a1, a2, du = begun
        if at + chunk < hidden:
            begun = ahead(at + chunk)
        phi = 0.5 * (1.0 + lax.erf(a1 * (1.0 / math.sqrt(2.0))))
        gate = a1 * phi
        u = (gate * a2).astype(bf16)
        slope = phi + a1 * (jnp.exp(-0.5 * a1 * a1) * (1.0 / math.sqrt(2.0 * math.pi)))
        da1 = (du * a2 * slope).astype(bf16)
        da2 = (du * gate).astype(bf16)
        out = out + dot(u, wd_ref[first, :])
        dh = dh + dot_rows(da1, wm_ref[:, first]) + dot_rows(da2, wm_ref[:, second])
        acc_d[first, :] += dot_columns(u, ct)
        acc_m[:, first] += dot(low_t, da1)
        acc_m[:, second] += dot(low_t, da2)
    out_ref[...] = out.astype(bf16)
    dmid = ct.astype(f32) + normed_back(dh, gain, unit, inverse)
    dmr = dmid.astype(bf16)
    dmid_ref[...] = dmr
    acc_a[...] += dot(o_ref[...], dmr)
    do_ref[...] = dot_rows(dmr, wa_ref[...]).astype(bf16)

    last = step == pl.num_programs(0) - 1
    if not split:

        @pl.when(last)
        def _():
            for ref, acc in zip(grad_refs, (acc_d, acc_m, acc_a)):
                ref[...] = acc[...].astype(bf16)

    else:
        slots = split[0] * split[1]
        for c in (0, 1):

            @pl.when(last & (place_ref[0] == c))
            def _(c=c):
                pack_grads(own_ref, c, slots, acc_d, acc_m, acc_a)
                pack_grads(other_ref, 1 - c, slots, acc_d, acc_m, acc_a)


def patched(step, steps, rows, value_ref, edge_ref):
    value = value_ref[...]
    edge = edge_ref[...]
    head = jnp.concatenate([edge[:HALF], value[HALF:]], axis=0)
    value = jnp.where(step == 0, head, value)
    tail = jnp.concatenate([value[: rows - HALF], edge[HALF:]], axis=0)
    return jnp.where(step == steps - 1, tail, value)


def qkv_grad_kernel(
    split, place_ref,
    h_ref, dq_ref, dk_ref, dv_ref, rk_ref, rv_ref, left_ref, right_ref, cos_ref, sin_ref,
    ek_ref, ev_ref, *refs,
):
    *grad_refs, acc = refs
    step, steps = pl.program_id(0), pl.num_programs(0)
    rows, width = h_ref.shape

    @pl.when(step == 0)
    def _():
        for at, side in ((0, left_ref), (HALF, right_ref)):
            own = slice(at, at + HALF)
            cos, sin = cos_ref[own, :], sin_ref[own, :]
            for j in range(0, width, LANES):
                lanes = slice(j, j + LANES)
                total = rk_ref[own, lanes] + side[0, :, lanes].astype(f32)
                ek_ref[own, lanes] = rope_back(total, cos, sin).astype(bf16)
            ev_ref[own, :] = (rv_ref[own, :] + side[1].astype(f32)).astype(bf16)

    @pl.when(step == 0)
    def _():
        acc[...] = jnp.zeros_like(acc)

    low = h_ref[...]
    acc[:, :width] += dot_columns(low, dq_ref[...])
    acc[:, width : 2 * width] += dot_columns(low, patched(step, steps, rows, dk_ref, ek_ref))
    acc[:, 2 * width :] += dot_columns(low, patched(step, steps, rows, dv_ref, ev_ref))

    last = step == steps - 1
    if not split:

        @pl.when(last)
        def _():
            grad_refs[0][...] = acc[...].astype(bf16)

    else:
        half = acc.shape[1] // 2
        for c in (0, 1):

            @pl.when(last & (place_ref[0] == c))
            def _(c=c):
                for ref, side in zip(grad_refs, (c, 1 - c)):
                    ref[...] = acc[:, side * half : (side + 1) * half].astype(bf16)


def input_kernel(x_ref, gain_ref, w_ref, dmid_ref, dq_ref, dk_ref, dv_ref, ek_ref, ev_ref, dx_ref):
    step, steps = pl.program_id(0), pl.num_programs(0)
    rows, width = x_ref.shape

    dh = dot_rows(dq_ref[...], w_ref[:, :width])
    dh = dh + dot_rows(patched(step, steps, rows, dk_ref, ek_ref), w_ref[:, width : 2 * width])
    dh = dh + dot_rows(patched(step, steps, rows, dv_ref, ev_ref), w_ref[:, 2 * width :])
    unit, inverse = normed(x_ref[...].astype(f32))
    dx = dmid_ref[...].astype(f32) + normed_back(dh, gain_ref[0:1, :], unit, inverse)
    dx_ref[...] = dx.astype(bf16)


def shaped(shape, dtype):
    return jax.ShapeDtypeStruct(shape, dtype)


def tiles(rows, columns):
    return pl.BlockSpec((rows, columns), lambda i: (i, 0))


def pairs(rows, offset=0):
    return pl.BlockSpec((rows, LANES), lambda i: (0, i + offset))


def kept(*shape):
    return pl.BlockSpec(shape, lambda i: (0,) * len(shape), pipeline_mode=pl.Buffered(1))


def held(*shape):
    return pl.BlockSpec(shape, lambda i: (0,) * len(shape))


def call(
    kernel, grid, in_specs, out_specs, out_shape, scratch, flops, moved, aliases=None
):
    return pl.pallas_call(
        kernel,
        grid=(grid,),
        in_specs=in_specs,
        out_specs=out_specs,
        out_shape=out_shape,
        scratch_shapes=scratch,
        input_output_aliases=aliases or {},
        compiler_params=pltpu.CompilerParams(
            vmem_limit_bytes=vmem_bytes, dimension_semantics=("arbitrary",)
        ),
        cost_estimate=pl.CostEstimate(
            flops=flops // 64, bytes_accessed=moved // 64, transcendentals=0
        ),
    )


def project(x, gains, weight, cos, sin):
    rows, width = x.shape
    tile = min(TILE, rows)
    return call(
        project_kernel,
        rows // tile,
        [tiles(tile, width), held(2, width), kept(*weight.shape), tiles(tile, LANES), tiles(tile, LANES)],
        [tiles(tile, width)] * 4,
        [shaped((rows, width), bf16)] * 4,
        [],
        2 * rows * width * 3 * width,
        rows * width * 10 + weight.size * 2,
    )(x, gains, weight, cos, sin)


def project_edges(split, place, x, gains, cos, sin, *parts):
    rows, width = x.shape
    return call(
        functools.partial(project_edges_kernel, split),
        1,
        [pl.BlockSpec(memory_space=pltpu.SMEM), held(rows, width), held(2, width)]
        + [held(rows, LANES)] * 2
        + [held(*part.shape) for part in parts],
        [held(HALF, 2 * width)] * 2 + [held(width, 3 * width)],
        [shaped((HALF, 2 * width), bf16)] * 2 + [shaped((width, 3 * width), bf16)],
        [],
        4 * rows * width * width,
        rows * width * 6 + width * width * 12,
    )(place, x, gains, cos, sin, *parts)


def attend_scratch(rows):
    extended = rows + 2 * HALF
    return [
        pltpu.VMEM((extended, LANES), bf16),
        pltpu.VMEM((extended, LANES), bf16),
        pltpu.VMEM((rows // ROWS, SPAN, ROWS), f32),
        pltpu.VMEM((LANES, extended), bf16),
    ]


def attend(meta, q, k, v, left, right, first, count, before=()):
    rows, width = q.shape
    steps = width // LANES

    def columns(height, offset=0):
        return pairs(height, first + offset)

    return call(
        attend_kernel,
        count,
        [pl.BlockSpec(memory_space=pltpu.SMEM)]
        + [columns(rows)] * 3
        + [columns(HALF), columns(HALF, steps)] * 2
        + [pl.BlockSpec(memory_space=pl.ANY)] * len(before),
        [
            pl.BlockSpec((LANES, rows), lambda i: (i + first, 0)),
            pl.BlockSpec((1, rows // ROWS, 2 * ROWS), lambda i: (i + first, 0, 0)),
        ],
        [shaped((width, rows), bf16), shaped((steps, rows // ROWS, 2 * ROWS), f32)],
        attend_scratch(rows),
        8 * rows * width * 256,
        rows * width * 8,
        {8 + at: at for at in range(len(before))},
    )(meta, q, k, v, left, left, right, right, *before)


def back_specs(rows, steps):
    return (
        [pl.BlockSpec(memory_space=pltpu.SMEM)]
        + [pairs(rows)] * 4
        + [pairs(HALF), pairs(HALF, steps)] * 2
        + [pl.BlockSpec((1, rows // ROWS, 2 * ROWS), lambda i: (i, 0, 0)), held(rows, LANES), held(rows, LANES)]
    )


def back_scratch(rows):
    extended = rows + 2 * HALF
    return attend_scratch(rows) + [pltpu.VMEM((extended, LANES), f32)] * 2


def attend_back_edges(meta, q, k, v, do, left, right, lse, cos, sin):
    rows, width = q.shape
    steps = width // LANES
    span = 2 * SPAN
    return call(
        attend_back_edges_kernel,
        steps,
        back_specs(rows, steps),
        [pairs(2 * ROWS)]
        + [pairs(span)] * 2
        + [pl.BlockSpec((2, HALF, LANES), lambda i: (0, 0, i))] * 2
        + [pairs(2 * HALF)] * 2,
        [shaped((2 * ROWS, width), bf16)]
        + [shaped((span, width), f32)] * 2
        + [shaped((2, HALF, width), bf16)] * 2
        + [shaped((2 * HALF, width), f32)] * 2,
        back_scratch(rows),
        20 * 2 * ROWS * width * 256,
        rows * width * 10,
    )(meta, q, k, v, do, left, left, right, right, lse, cos, sin)


def attend_back(meta, q, k, v, do, left, right, lse, cos, sin, edges):
    rows, width = q.shape
    steps = width // LANES
    span = 2 * SPAN
    return call(
        attend_back_kernel,
        steps,
        back_specs(rows, steps) + [pairs(2 * ROWS)] + [pairs(span)] * 2,
        [pairs(rows)] * 3,
        [shaped((rows, width), bf16)] * 3,
        back_scratch(rows),
        20 * rows * width * 256,
        rows * width * 14,
    )(meta, q, k, v, do, left, left, right, right, lse, cos, sin, *edges)


def middle(split, place, x, o, ct, gains, shapes, *weights):
    rows, width = x.shape
    tile = WIDE_TILE if rows % WIDE_TILE == 0 else rows
    wa, wm, wd = shapes
    if split:
        grads = [(width, wm[1] // 2 + 3 * (width // 2))] * 2
    else:
        grads = [wd, wm, wa]
    return call(
        functools.partial(middle_kernel, split),
        rows // tile,
        [
            pl.BlockSpec(memory_space=pltpu.SMEM),
            tiles(tile, width),
            pl.BlockSpec((width, tile), lambda i: (0, i)),
            tiles(tile, width),
            held(2, width),
        ]
        + [kept(*w.shape) for w in weights],
        [tiles(tile, width)] * 3 + [kept(*shape) for shape in grads],
        [shaped((rows, width), bf16)] * 3 + [shaped(shape, bf16) for shape in grads],
        ([pltpu.VMEM(w, bf16) for w in shapes] if split else [])
        + [pltpu.VMEM(wd, f32), pltpu.VMEM(wm, f32), pltpu.VMEM(wa, f32)],
        6 * rows * width * width * 5,
        rows * width * 14 + 20 * width * width,
    )(place, x, o, ct, gains, *weights)


def qkv_gradient(split, place, h, dq, dk, dv, ek, ev, left, right, cos, sin):
    rows, width = h.shape
    tile = min(TILE, rows)
    grads = [(width, 3 * width // 2)] * 2 if split else [(width, 3 * width)]
    return call(
        functools.partial(qkv_grad_kernel, split),
        rows // tile,
        [pl.BlockSpec(memory_space=pltpu.SMEM)]
        + [tiles(tile, width)] * 4
        + [held(2 * HALF, width)] * 2
        + [held(2, HALF, width)] * 2
        + [held(2 * HALF, LANES)] * 2,
        [held(2 * HALF, width)] * 2 + [held(*shape) for shape in grads],
        [shaped((2 * HALF, width), bf16)] * 2 + [shaped(shape, bf16) for shape in grads],
        [pltpu.VMEM((width, 3 * width), f32)],
        6 * rows * width * width,
        rows * width * 8 + 6 * width * width,
    )(place, h, dq, dk, dv, ek, ev, left, right, cos, sin)


def input_gradient(x, gains, weight, dmid, dq, dk, dv, ek, ev):
    rows, width = x.shape
    tile = min(TILE, rows)
    return call(
        input_kernel,
        rows // tile,
        [tiles(tile, width), held(2, width), kept(*weight.shape)]
        + [tiles(tile, width)] * 4
        + [held(2 * HALF, width)] * 2,
        tiles(tile, width),
        shaped((rows, width), bf16),
        [],
        6 * rows * width * width,
        rows * width * 14 + 6 * width * width,
    )(x, gains, weight, dmid, dq, dk, dv, ek, ev)


def rope_tables(positions, head_size):
    half_size = head_size // 2
    exponent = jnp.arange(half_size, dtype=f32) * (2.0 / head_size)
    inverse = rope_theta ** (-exponent)
    inverse = jnp.tile(inverse, LANES // half_size)
    angles = positions.astype(f32)[:, None] * inverse[None, :]
    sign = jnp.where(jnp.arange(LANES) % head_size < half_size, -1.0, 1.0).astype(f32)
    return jnp.cos(angles), jnp.sin(angles) * sign


def adam_update(master, first_moment, second_moment, gradient, step_rate):
    gradient = gradient.astype(f32)
    new_first = beta_first * first_moment + (1.0 - beta_first) * gradient
    new_second = beta_second * second_moment + (1.0 - beta_second) * gradient * gradient
    first_hat = new_first / (1.0 - beta_first**ADAM_STEP)
    second_hat = new_second / (1.0 - beta_second**ADAM_STEP)
    new_master = master - step_rate * (
        decay_rate * master + first_hat / (jnp.sqrt(second_hat) + adam_epsilon)
    )
    return (new_first, new_second, new_master)


def edge_rows(value):
    return value[:HALF], value[value.shape[0] - HALF :]


def per_device(
    tokens,
    positions,
    cotangent,
    qkv_weight,
    attn_weight,
    mlp_weight,
    down_weight,
    norm_gains,
    qkv_first,
    qkv_second,
    attn_first,
    attn_second,
    mlp_first,
    mlp_second,
    down_first,
    down_second,
    gains_first,
    gains_second,
):
    rows, width = tokens.shape
    device = lax.axis_index(("seq", "shard"))
    last_device = lax.axis_size(("seq", "shard")) - 1
    shards = lax.axis_size("shard")
    quarters = lax.axis_size("seq") // 2
    core = lax.axis_index("seq") % 2
    split = (shards, quarters) if split_pays() else None
    place = jnp.stack([core, lax.axis_index("seq") // 2, lax.axis_index("shard")])
    place = place.astype(jnp.int32)
    half = qkv_weight.shape[1] // 2
    slot = qkv_weight.shape[0] // quarters
    rest = down_weight.shape[0] // quarters - slot
    wide = mlp_weight.shape[1] // 2
    down_at = wide + attn_weight.shape[1] // 2
    quarter = lax.axis_index("seq") // 2
    edge_x = jnp.concatenate(edge_rows(tokens), axis=0)
    if split:
        part = own_block(qkv_weight, quarter * slot, slot)
        gain_rows = jnp.pad(norm_gains.astype(bf16), ((0, 6), (0, half - norm_gains.shape[1])))
        qkv_stack = stack(jnp.concatenate([part, gain_rows], axis=0), "shard", 1)
        rest_part = jnp.concatenate(
            [own_block(w, quarter * slot, slot) for w in (mlp_weight, attn_weight)]
            + down_part(down_weight, slot),
            axis=1,
        )
        qkv_part = jnp.concatenate([piece[:slot] for piece in qkv_stack], axis=0)
        rest_part = doubled(rest_part, 1)
        qkv_part = after(qkv_part, rest_part)
        rest_part = doubled(rest_part, 2)
        qkv_pieces = stack(qkv_part, "seq", 2)
        positions, edge_x = after((positions, edge_x), qkv_part)
        gains = jnp.zeros((shards, 2, norm_gains.shape[1]), bf16)
        for d, piece in enumerate(qkv_stack):
            piece = piece[None, slot : slot + 2, : norm_gains.shape[1]]
            gains = lax.dynamic_update_slice_in_dim(gains, piece, lax.axis_index("shard") ^ d, 0)
        gains = gains.astype(f32).transpose(1, 0, 2).reshape(2, -1)
    else:
        lows = [w.astype(bf16) for w in (qkv_weight, attn_weight, mlp_weight, down_weight)]
        full_qkv, full_attn, full_mlp, full_down = (
            lax.all_gather(w, "shard", axis=0, tiled=True) for w in lows
        )
        gains = lax.all_gather(norm_gains.astype(bf16), "shard", axis=1, tiled=True).astype(f32)
        qkv_parts = (full_qkv,)
    cos, sin = rope_tables(positions, width // HEADS)
    start = jnp.max(jnp.where(positions == 0, jnp.arange(rows, dtype=jnp.int32), 0))
    low = jnp.where(device > 0, -HALF, 0)
    high = jnp.where(device < last_device, rows + HALF, rows)
    meta = jnp.stack([start, low, high]).astype(jnp.int32)
    edge_cos, edge_sin = (jnp.concatenate(edge_rows(value), axis=0) for value in (cos, sin))
    if split:
        qkv_pieces = after(qkv_pieces, rest_part, gains, meta, place, edge_x, edge_cos, edge_sin)
        qkv_part = jnp.concatenate(qkv_pieces, axis=0)
        rest_part = after(rest_part, qkv_part)
        qkv_parts = qkv_part, swap(qkv_part, "seq", 1)
    kv_head, kv_tail, full_qkv = project_edges(
        split, place, edge_x, gains, edge_cos, edge_sin, *qkv_parts
    )
    left = to_right(kv_tail)
    right = to_left(kv_head)
    h, q, k, v = project(after(tokens, kv_head), gains, full_qkv, cos, sin)
    left = after(left, k)
    right = after(right, k)
    pair_count = width // LANES
    before = attend(meta, q, k, v, left, right, 0, pair_count // 2)
    if split:
        rest_part = jnp.concatenate(stack(rest_part, "seq", 2, (before[0],)), axis=0)
        rest_weights = rest_part, swap(rest_part, "seq", 1)
        q = after(q, rest_part)
    else:
        rest_weights = full_attn, full_mlp, full_down
    o, lse = attend(
        meta, q, k, v, left, right, pair_count // 2, pair_count - pair_count // 2, before
    )
    shapes = (
        (width, attn_weight.shape[1]),
        (width, mlp_weight.shape[1]),
        (shards * down_weight.shape[0], width),
    )
    layer_output, dmid, do, *rest_grads = middle(
        split, place, tokens, o, cotangent, gains, shapes, *rest_weights
    )
    if split:
        rest_own, rest_other = rest_grads
        rest_got = swap(rest_other, "seq", 1)
    back_args = (meta, q, k, v, do, left, right, lse, cos, sin)
    *edges, halo_head, halo_tail, raw_k, raw_v = attend_back_edges(*back_args)
    from_right = to_left(halo_head)
    from_left = to_right(halo_tail)
    if split:
        rest_half = keep_half(rest_own, after(rest_got, halo_head))
        do = after(do, rest_half)
        back_args = (meta, q, k, v, do, left, right, lse, cos, sin)
        rest_pieces = quarter_pieces(rest_half)
    dq, dk, dv = attend_back(*back_args, edges)
    edge_k, edge_v, *qkv_grads = qkv_gradient(
        split, place, h, dq, dk, dv, raw_k, raw_v, after(from_left, dq), after(from_right, dq), edge_cos, edge_sin
    )
    if split:
        qkv_own, qkv_other = qkv_grads
        rest_part = sum_after(rest_pieces, qkv_own)
        qkv_got = swap(after(qkv_other, rest_part), "seq", 1)
        qkv_half = keep_half(qkv_own, qkv_got)
        dq = after(dq, qkv_half)
        qkv_pieces = quarter_pieces(qkv_half)
        rest_pieces = halve(rest_part, 2)
    input_grad = input_gradient(tokens, gains, full_qkv, dmid, dq, dk, dv, edge_k, edge_v)
    if split:
        qkv_part = sum_after(qkv_pieces, input_grad)
        rest_part = sum_after(list(rest_pieces), qkv_part)
        rest_pieces = halve(rest_part, 1)
        rest_part = sum_after(list(rest_pieces), qkv_part)[0]
        qkv_part = sum_after(shard_pieces(qkv_part), rest_part)
        rest_half = owners_half(rest_part, (qkv_part,))
        rest_got = swap(rest_half, "seq", 1)
        qkv_half = owners_half(qkv_part, (rest_half,))
        qkv_got = swap(qkv_half, "seq", 1)
        first, second = by_core(core, rest_half, after(rest_got, qkv_half))
        mlp_total = side_by_side(first[:, :wide], second[:, :wide])
        attn_total = side_by_side(first[:, wide:down_at], second[:, wide:down_at])
        down_total = side_by_side(
            *(unpack_down(x[:, down_at:], quarters, rest) for x in (first, second))
        )
    else:
        down_total, mlp_total, attn_total, qkv_total = (
            reduce_whole(g) for g in (*rest_grads, *qkv_grads)
        )
    attn_new = adam_update(attn_weight, attn_first, attn_second, attn_total, rate_matrix)
    mlp_new = adam_update(mlp_weight, mlp_first, mlp_second, mlp_total, rate_matrix)
    down_new = adam_update(down_weight, down_first, down_second, down_total, rate_matrix)
    if split:
        qkv_got = after(qkv_got, attn_new[0], mlp_new[0], down_new[0])
        qkv_total = side_by_side(*by_core(core, qkv_half, qkv_got))
    qkv_new = adam_update(qkv_weight, qkv_first, qkv_second, qkv_total, rate_matrix)
    gains_total = jnp.stack(
        [
            gain_grad(qkv_weight, qkv_total, norm_gains[0]),
            gain_grad(mlp_weight, mlp_total, norm_gains[1]),
        ]
    )
    gains_new = adam_update(norm_gains, gains_first, gains_second, gains_total, rate_gains)
    return (layer_output, input_grad, *qkv_new, *attn_new, *mlp_new, *down_new, *gains_new)


def solution(mesh):
    tokens, rows, columns = P(("seq", "shard"), None), P("shard", None), P(None, "shard")
    matrices = (rows,) * 4
    return jax.shard_map(
        per_device,
        mesh=mesh,
        in_specs=(tokens, P(("seq", "shard")), tokens, *matrices, columns)
        + (rows,) * 8
        + (columns,) * 2,
        out_specs=(tokens, tokens) + (rows,) * 12 + (columns,) * 3,
        check_vma=False,
    )
```

```python
import functools
import math

import jax
import jax.numpy as jnp
from jax import lax
from jax.experimental import pallas as pl
from jax.experimental.pallas import tpu as pltpu
from jax.sharding import PartitionSpec as P

HEADS = 12
HALF = 64
ADAM_STEP = 5
LANES = 128
ROWS = 128
SPAN = ROWS + 2 * HALF
TILE = 256
WIDE_TILE = 640
GROUP = 4


norm_epsilon = 1e-05
rope_theta = 10000.0
beta_first = 0.9
beta_second = 0.98
adam_epsilon = 1e-06
decay_rate = 1e-05
rate_matrix = 0.04
rate_gains = 0.2
masked_score = -1e30
vmem_bytes = 60 * 1024 * 1024

f32 = jnp.float32
bf16 = jnp.bfloat16


def swap(value, axis, flip):
    count = lax.axis_size(axis)
    return lax.ppermute(value, axis, [(i, i ^ flip) for i in range(count)])


def after(value, *others):
    return lax.optimization_barrier((value, *others))[0]


def spread(part, axis, unit, index, count, dim, then=()):
    out = jnp.zeros(part.shape[:dim] + (count,) + part.shape[dim:], part.dtype)
    pieces = [part] + [after(swap(part, axis, unit * d), *then) for d in range(1, count)]
    for d, piece in enumerate(pieces):
        out = lax.dynamic_update_slice_in_dim(out, jnp.expand_dims(piece, dim), index ^ d, dim)
    return out, pieces[1:]


def places():
    core = lax.axis_index("seq") % 2
    return core, lax.axis_index("seq") // 2, lax.axis_index("shard")


def by_core(core, own, other):
    return jnp.where(core == 0, own, other), jnp.where(core == 0, other, own)


def split_pays():
    count, shards = lax.axis_size("seq"), lax.axis_size("shard")
    return count == 8 and shards == 4


def own_block(weight, start, rows):
    width = weight.shape[1] // 2
    core = lax.axis_index("seq") % 2
    return lax.dynamic_slice(weight, (start, core * width), (rows, width)).astype(bf16)


def stack(part, axis, unit, then=()):
    count = lax.axis_size(axis) // unit
    others = [after(swap(part, axis, unit * d), *then) for d in range(1, count)]
    return [part] + others


def doubled(part, flip):
    return jnp.concatenate([part, swap(part, "shard", flip)], axis=0)


def down_rows(quarter):
    return 72 * quarter + 8 * (quarter % 2)


def down_part(weight, rows):
    start = down_rows(lax.axis_index("seq") // 2)
    last = jnp.minimum(start + 64, weight.shape[0] - 16)
    block = jnp.concatenate([own_block(weight, start, 64), own_block(weight, last, 16)], axis=0)
    return pack_down(block[None], rows)


def pack_down(blocks, rows):
    rest = blocks.shape[1] - rows
    second = jnp.pad(blocks[:, rows:], ((0, 0), (0, rows - rest), (0, 0)))
    columns = blocks.shape[2]
    return [blocks[:, :rows].reshape(-1, columns), second.reshape(-1, columns)]


def unpack_down(packed, blocks, rest):
    columns = packed.shape[1] // 2
    packed = packed.reshape(blocks, -1, 2 * columns)
    whole = jnp.concatenate([packed[:, :, :columns], packed[:, :rest, columns:]], axis=1)
    return whole.reshape(-1, columns)


def side_by_side(first, second):
    return jnp.concatenate([first, second], axis=1)


def total_of(pieces):
    total = pieces[0].astype(f32)
    for piece in pieces[1:]:
        total = total + piece.astype(f32)
    return total.astype(bf16)


def keep_half(own, got):
    shards, quarters = lax.axis_size("shard"), lax.axis_size("seq") // 2
    return total_of([own, got]).reshape(shards, quarters, -1, own.shape[1])


def sum_after(parts, *others):
    return total_of(parts[:1] + [after(part, *others) for part in parts[1:]])


def pieces(value, axis, unit, index, count, dim):
    def at(place):
        return lax.dynamic_index_in_dim(value, place, dim, keepdims=False)

    return [at(index)] + [swap(at(index ^ d), axis, unit * d) for d in range(1, count)]


def quarter_pieces(half):
    return pieces(half, "seq", 2, lax.axis_index("seq") // 2, lax.axis_size("seq") // 2, 1)


def shard_pieces(half):
    return pieces(half, "shard", 1, lax.axis_index("shard"), lax.axis_size("shard"), 0)


def halve(value, bit):
    side = lax.axis_index("shard") & bit
    kept_half = lax.dynamic_slice_in_dim(value, side, bit, 0)
    return kept_half, swap(lax.dynamic_slice_in_dim(value, side ^ bit, bit, 0), "shard", bit)


def owners_half(part, then=()):
    count = lax.axis_size("seq")
    part, _ = spread(part, "seq", 2, lax.axis_index("seq") // 2, count // 2, 0, then)
    return part.reshape(-1, part.shape[-1])


def reduce_whole(grad):
    owned = lax.psum_scatter(grad, "shard", scatter_dimension=0, tiled=True)
    return lax.psum(owned.astype(f32), "seq")


def gain_grad(weight, gradient, gain):
    low = weight.astype(bf16).astype(f32)
    return jnp.sum(low * gradient.astype(f32), axis=1) / gain.astype(bf16).astype(f32)


def to_right(value):
    axes = ("seq", "shard")
    ends = lax.axis_size(axes) - 1
    return lax.ppermute(value, axes, [(i, i + 1) for i in range(ends)])


def to_left(value):
    axes = ("seq", "shard")
    ends = lax.axis_size(axes) - 1
    return lax.ppermute(value, axes, [(i + 1, i) for i in range(ends)])


def normed(hidden):
    centered = hidden - jnp.mean(hidden, axis=-1, keepdims=True)
    inverse = lax.rsqrt(jnp.mean(centered * centered, axis=-1, keepdims=True) + norm_epsilon)
    return centered * inverse, inverse


def normed_back(grad, gain, unit, inverse):
    inner = grad * gain
    mean = jnp.mean(inner, axis=-1, keepdims=True)
    slope = jnp.mean(inner * unit, axis=-1, keepdims=True)
    return inverse * (inner - mean - unit * slope)


def dot(a, b):
    return jnp.dot(a, b, preferred_element_type=f32)


def dot_rows(a, b):
    return lax.dot_general(a, b, (((1,), (1,)), ((), ())), preferred_element_type=f32)


def dot_columns(a, b):
    return lax.dot_general(a, b, (((0,), (0,)), ((), ())), preferred_element_type=f32)


def turned(values):
    lane = lax.broadcasted_iota(jnp.int32, values.shape, 1)
    up = pltpu.roll(values, LANES - 32, 1)
    down = pltpu.roll(values, 32, 1)
    return jnp.where(lane % 64 < 32, up, down)


def rope(values, cos, sin):
    return values * cos + turned(values) * sin


def rope_back(values, cos, sin):
    return values * cos - turned(values) * sin


def mask_bias(meta_ref, block):
    first = block * ROWS
    shape = (SPAN, ROWS)
    key = lax.broadcasted_iota(jnp.int32, shape, 0) + (first - HALF)
    query = lax.broadcasted_iota(jnp.int32, shape, 1) + first
    start, low, high = meta_ref[0], meta_ref[1], meta_ref[2]
    apart = jnp.abs(query - key) > HALF
    other = (query >= start) != (key >= start)
    outside = (key < low) | (key >= high)
    return jnp.where(apart | other | outside, masked_score, 0.0).astype(f32)


def stacked(values):
    lane = lax.broadcasted_iota(jnp.int32, values.shape, 1)
    zero = jnp.zeros_like(values)
    return jnp.concatenate(
        [jnp.where(lane < 64, values, zero), jnp.where(lane < 64, zero, values)], axis=0
    )


def unstacked(values):
    depth = lax.broadcasted_iota(jnp.int32, (LANES, ROWS), 0)
    return jnp.where(depth < 64, values[:, :ROWS], values[:, ROWS:])


def window(block):
    return slice(block * ROWS, block * ROWS + SPAN)


def assemble(place_ref, shards, quarters, copy):
    for c in (0, 1):

        @pl.when(place_ref[0] == c)
        def _(c=c):
            for side in (0, 1):
                for dq in range(quarters):
                    for dz in range(shards):
                        copy(
                            side,
                            c ^ side,
                            dq * shards + dz,
                            jnp.bitwise_xor(place_ref[1], dq),
                            jnp.bitwise_xor(place_ref[2], dz),
                        )


def project_kernel(x_ref, gain_ref, w_ref, cos_ref, sin_ref, h_ref, q_ref, k_ref, v_ref):
    unit, _ = normed(x_ref[...].astype(f32))
    low = (unit * gain_ref[0:1, :]).astype(bf16)
    h_ref[...] = low
    width = low.shape[1]
    cos, sin = cos_ref[...], sin_ref[...]
    for ref, at, scale in ((q_ref, 0, 0.125), (k_ref, width, None)):
        out = dot(low, w_ref[:, at : at + width])
        for j in range(0, width, LANES):
            value = rope(out[:, j : j + LANES], cos, sin)
            if scale is not None:
                value = value * scale
            ref[:, j : j + LANES] = value.astype(bf16)
    v_ref[...] = dot(low, w_ref[:, 2 * width :]).astype(bf16)


def project_edges_kernel(
    split, place_ref, x_ref, gain_ref, cos_ref, sin_ref, *refs
):
    *parts, head_ref, tail_ref, w_ref = refs
    if split:
        shards, quarters = split
        rows = parts[0].shape[0] // (shards * quarters)
        half = parts[0].shape[1]

        def copy(side, column, part, quarter, shard):
            at = pl.multiple_of((shard * quarters + quarter) * rows, 16)
            w_ref[pl.ds(at, rows), column * half : (column + 1) * half] = parts[side][
                part * rows : (part + 1) * rows, :
            ]

        assemble(place_ref, shards, quarters, copy)
    else:
        w_ref[...] = parts[0][...]
    unit, _ = normed(x_ref[...].astype(f32))
    low = (unit * gain_ref[0:1, :]).astype(bf16)
    width = low.shape[1]
    cos, sin = cos_ref[...], sin_ref[...]
    keys = dot(low, w_ref[:, width : 2 * width])
    for j in range(0, width, LANES):
        value = rope(keys[:, j : j + LANES], cos, sin).astype(bf16)
        head_ref[:, j : j + LANES] = value[:HALF]
        tail_ref[:, j : j + LANES] = value[HALF:]
    values = dot(low, w_ref[:, 2 * width :]).astype(bf16)
    head_ref[:, width:] = values[:HALF]
    tail_ref[:, width:] = values[HALF:]


def fill(dst, left, middle, right):
    rows = middle.shape[0]
    dst[0:HALF, :] = left[...]
    dst[HALF : HALF + rows, :] = middle[...]
    dst[HALF + rows :, :] = right[...]


def flip(dst, src, start, stop):
    for at in range(start, stop, LANES):
        dst[:, at : at + LANES] = src[at : at + LANES, :].T


def attend_kernel(
    meta_ref, q_ref, k_ref, v_ref, kl_ref, vl_ref, kr_ref, vr_ref, *refs
):
    o_ref, lse_ref, kx, vx, bias, vt = refs[-6:]
    blocks = q_ref.shape[0] // ROWS

    @pl.when(pl.program_id(0) == 0)
    def _():
        for n in range(blocks):
            bias[n] = mask_bias(meta_ref, n)

    fill(kx, kl_ref, k_ref, kr_ref)
    fill(vx, vl_ref, v_ref, vr_ref)
    flip(vt, vx, 0, vx.shape[0])
    for first in range(0, blocks, GROUP):
        group = range(first, min(first + GROUP, blocks))
        scores = []
        for n in group:
            queries = stacked(q_ref[n * ROWS : (n + 1) * ROWS, :])
            mask = bias[n]
            score = dot_rows(kx[window(n), :], queries)
            scores.append(score + jnp.concatenate([mask, mask], axis=1))
        tops = [jnp.max(score, axis=0, keepdims=True) for score in scores]
        weights = [jnp.exp(score - top) for score, top in zip(scores, tops)]
        totals = [jnp.sum(weight, axis=0, keepdims=True) for weight in weights]
        outs = [dot(vt[:, window(n)], weight.astype(bf16)) for n, weight in zip(group, weights)]
        for n, out, top, total in zip(group, outs, tops, totals):
            own = slice(n * ROWS, (n + 1) * ROWS)
            o_ref[:, own] = unstacked(out * (1.0 / total)).astype(bf16)
            lse_ref[0, n : n + 1, :] = top + jnp.log(total)


def back_blocks(
    blocks, dq_at, q_ref, do_ref, kx, vx, bias, kt, lse_ref, cos_ref, sin_ref, dq_ref, dkx, dvx
):
    for first in range(0, len(blocks), GROUP):
        group = blocks[first : first + GROUP]
        rows = [slice(n * ROWS, (n + 1) * ROWS) for n in group]
        queries = [stacked(q_ref[own, :]) for own in rows]
        grads = [stacked(do_ref[own, :]) for own in rows]
        scores = [dot_rows(kx[window(n), :], query) for n, query in zip(group, queries)]
        grad_probs = [dot_rows(vx[window(n), :], grad) for n, grad in zip(group, grads)]
        probs = []
        for n, score in zip(group, scores):
            mask = bias[n]
            mask = jnp.concatenate([mask, mask], axis=1)
            probs.append(jnp.exp(score + mask - lse_ref[0, n : n + 1, :]))
        inners = [jnp.sum(p * g, axis=0, keepdims=True) for p, g in zip(probs, grad_probs)]
        grad_scores = [
            (p * (g - inner)).astype(bf16) for p, g, inner in zip(probs, grad_probs, inners)
        ]
        grad_queries = [dot(kt[:, window(n)], ds) for n, ds in zip(group, grad_scores)]
        grad_values = [dot(p.astype(bf16), grad) for p, grad in zip(probs, grads)]
        grad_keys = [dot(ds, query) for ds, query in zip(grad_scores, queries)]
        for n, grad_value, grad_key in zip(group, grad_values, grad_keys):
            dvx[window(n), :] += grad_value
            dkx[window(n), :] += grad_key
        for n, own, grad_query in zip(group, rows, grad_queries):
            at = dq_at(n) * ROWS
            dq_ref[at : at + ROWS, :] = rope_back(
                unstacked(grad_query).T * 0.125, cos_ref[own, :], sin_ref[own, :]
            ).astype(bf16)


def attend_back_edges_kernel(
    meta_ref, q_ref, k_ref, v_ref, do_ref, kl_ref, vl_ref, kr_ref, vr_ref, lse_ref, cos_ref, sin_ref,
    dq_ref, wk_ref, wv_ref, head_ref, tail_ref, ek_ref, ev_ref,
    kx, vx, bias, kt, dkx, dvx,
):
    rows = q_ref.shape[0]
    blocks = rows // ROWS
    span = SPAN
    spans = (slice(0, span), slice(rows - ROWS, rows + 2 * HALF))

    @pl.when(pl.program_id(0) == 0)
    def _():
        for n in (0, blocks - 1):
            bias[n] = mask_bias(meta_ref, n)

    inside = span - HALF
    for x, left, own, right in ((kx, kl_ref, k_ref, kr_ref), (vx, vl_ref, v_ref, vr_ref)):
        x[0:HALF, :] = left[...]
        x[HALF:span, :] = own[:inside, :]
        x[HALF + rows - inside : HALF + rows, :] = own[rows - inside :, :]
        x[HALF + rows :, :] = right[...]
    for own in spans:
        flip(kt, kx, own.start, own.stop)
        for acc in (dkx, dvx):
            acc[own, :] = jnp.zeros((span, LANES), f32)
    back_blocks(
        (0, blocks - 1), lambda n: min(n, 1),
        q_ref, do_ref, kx, vx, bias, kt, lse_ref, cos_ref, sin_ref, dq_ref, dkx, dvx,
    )
    for ref, acc in ((wk_ref, dkx), (wv_ref, dvx)):
        ref[:span, :] = acc[spans[0], :]
        ref[span:, :] = acc[spans[1], :]
    for at, acc, ref in ((0, dkx, ek_ref), (1, dvx, ev_ref)):
        head_ref[at] = acc[0:HALF, :].astype(bf16)
        tail_ref[at] = acc[HALF + rows :, :].astype(bf16)
        ref[0:HALF, :] = acc[HALF : 2 * HALF, :]
        ref[HALF:, :] = acc[rows : rows + HALF, :]


def attend_back_kernel(
    meta_ref, q_ref, k_ref, v_ref, do_ref, kl_ref, vl_ref, kr_ref, vr_ref, lse_ref, cos_ref, sin_ref,
    eq_ref, wk_ref, wv_ref,
    dq_ref, dk_ref, dv_ref,
    kx, vx, bias, kt, dkx, dvx,
):
    rows = q_ref.shape[0]
    blocks = rows // ROWS
    span = SPAN

    @pl.when(pl.program_id(0) == 0)
    def _():
        for n in range(1, blocks - 1):
            bias[n] = mask_bias(meta_ref, n)

    fill(kx, kl_ref, k_ref, kr_ref)
    fill(vx, vl_ref, v_ref, vr_ref)
    flip(kt, kx, 0, kx.shape[0])
    last = slice(rows - ROWS, rows + 2 * HALF)
    for acc, ref in ((dkx, wk_ref), (dvx, wv_ref)):
        acc[:span, :] = ref[:span, :]
        acc[span : last.start, :] = jnp.zeros((last.start - span, LANES), f32)
        acc[last, :] = ref[span:, :]
    dq_ref[:ROWS, :] = eq_ref[:ROWS, :]
    dq_ref[rows - ROWS :, :] = eq_ref[ROWS:, :]
    back_blocks(
        range(1, blocks - 1), lambda n: n,
        q_ref, do_ref, kx, vx, bias, kt, lse_ref, cos_ref, sin_ref, dq_ref, dkx, dvx,
    )
    middle = slice(HALF, HALF + rows)
    dk_ref[...] = rope_back(dkx[middle, :], cos_ref[...], sin_ref[...]).astype(bf16)
    dv_ref[...] = dvx[middle, :].astype(bf16)


def pack_grads(ref, c, slots, acc_d, acc_m, acc_a):
    wide, narrow = acc_m.shape[1] // 2, acc_a.shape[1] // 2
    rows, down_rows = acc_m.shape[0] // slots, acc_d.shape[0] // slots
    ref[:, :wide] = acc_m[:, c * wide : (c + 1) * wide].astype(bf16)
    ref[:, wide : wide + narrow] = acc_a[:, c * narrow : (c + 1) * narrow].astype(bf16)
    fill_rows = jnp.zeros((2 * rows - down_rows, narrow), f32)
    for n in range(slots):
        own = slice(n * rows, (n + 1) * rows)
        block = acc_d[n * down_rows : (n + 1) * down_rows, c * narrow : (c + 1) * narrow]
        ref[own, wide + narrow : wide + 2 * narrow] = block[:rows].astype(bf16)
        rest = jnp.concatenate([block[rows:], fill_rows], axis=0)
        ref[own, wide + 2 * narrow :] = rest.astype(bf16)


def gather_middle(split, place_ref, step, parts, wa_ref, wm_ref, wd_ref):
    shards, quarters = split
    rows = parts[0].shape[0] // (shards * quarters)
    wide, narrow = wm_ref.shape[1] // 2, wa_ref.shape[1] // 2
    shard_rows = wd_ref.shape[0] // shards

    def copy(side, column, part, quarter, shard):
        own = slice(part * rows, (part + 1) * rows)
        ref = parts[side]
        lanes = slice(column * narrow, (column + 1) * narrow)
        at = pl.multiple_of((shard * quarters + quarter) * rows, 16)
        wm_ref[pl.ds(at, rows), column * wide : (column + 1) * wide] = ref[own, :wide]
        wa_ref[pl.ds(at, rows), lanes] = ref[own, wide : wide + narrow]
        at = shard * shard_rows + down_rows(quarter)
        first, second = wide + narrow, wide + 2 * narrow
        wd_ref[pl.ds(pl.multiple_of(at, 16), rows), lanes] = ref[own, first:second]
        rest = ref[own, second:]
        wd_ref[pl.ds(pl.multiple_of(at + rows, 16), 16), lanes] = rest[:16]

        @pl.when(quarter % 2 == 0)
        def _():
            wd_ref[pl.ds(pl.multiple_of(at + rows + 16, 16), 16), lanes] = rest[16:32]

    @pl.when(step == 0)
    def _():
        assemble(place_ref, shards, quarters, copy)


def middle_kernel(
    split, place_ref, x_ref, o_ref, ct_ref, gain_ref, *refs
):
    *refs, acc_d, acc_m, acc_a = refs
    step = pl.program_id(0)
    if split:
        own_part, other_part, out_ref, dmid_ref, do_ref, own_ref, other_ref, wa_ref, wm_ref, wd_ref = refs
        gather_middle(split, place_ref, step, (own_part, other_part), wa_ref, wm_ref, wd_ref)
    else:
        wa_ref, wm_ref, wd_ref, out_ref, dmid_ref, do_ref, *grad_refs = refs

    @pl.when(step == 0)
    def _():
        acc_d[...] = jnp.zeros_like(acc_d)
        acc_m[...] = jnp.zeros_like(acc_m)
        acc_a[...] = jnp.zeros_like(acc_a)

    gain = gain_ref[1:2, :]
    hidden = wd_ref.shape[0]
    chunk = hidden // 3
    ct = ct_ref[...]
    mid = x_ref[...].astype(f32) + dot_columns(o_ref[...], wa_ref[...])
    unit, inverse = normed(mid)
    low = (unit * gain).astype(bf16)
    low_t = low.T
    out = mid
    dh = jnp.zeros_like(mid)

    def ahead(at):
        first, second = slice(at, at + chunk), slice(hidden + at, hidden + at + chunk)
        products = dot(low, wm_ref[:, first]), dot(low, wm_ref[:, second])
        return first, second, *products, dot_rows(ct, wd_ref[first, :])

    begun = ahead(0)
    for at in range(0, hidden, chunk):
        first, second, a1, a2, du = begun
        if at + chunk < hidden:
            begun = ahead(at + chunk)
        phi = 0.5 * (1.0 + lax.erf(a1 * (1.0 / math.sqrt(2.0))))
        gate = a1 * phi
        u = (gate * a2).astype(bf16)
        slope = phi + a1 * (jnp.exp(-0.5 * a1 * a1) * (1.0 / math.sqrt(2.0 * math.pi)))
        da1 = (du * a2 * slope).astype(bf16)
        da2 = (du * gate).astype(bf16)
        out = out + dot(u, wd_ref[first, :])
        dh = dh + dot_rows(da1, wm_ref[:, first]) + dot_rows(da2, wm_ref[:, second])
        acc_d[first, :] += dot_columns(u, ct)
        acc_m[:, first] += dot(low_t, da1)
        acc_m[:, second] += dot(low_t, da2)
    out_ref[...] = out.astype(bf16)
    dmid = ct.astype(f32) + normed_back(dh, gain, unit, inverse)
    dmr = dmid.astype(bf16)
    dmid_ref[...] = dmr
    acc_a[...] += dot(o_ref[...], dmr)
    do_ref[...] = dot_rows(dmr, wa_ref[...]).astype(bf16)

    last = step == pl.num_programs(0) - 1
    if not split:

        @pl.when(last)
        def _():
            for ref, acc in zip(grad_refs, (acc_d, acc_m, acc_a)):
                ref[...] = acc[...].astype(bf16)

    else:
        slots = split[0] * split[1]
        for c in (0, 1):

            @pl.when(last & (place_ref[0] == c))
            def _(c=c):
                pack_grads(own_ref, c, slots, acc_d, acc_m, acc_a)
                pack_grads(other_ref, 1 - c, slots, acc_d, acc_m, acc_a)


def patched(step, steps, rows, value_ref, edge_ref):
    value = value_ref[...]
    edge = edge_ref[...]
    head = jnp.concatenate([edge[:HALF], value[HALF:]], axis=0)
    value = jnp.where(step == 0, head, value)
    tail = jnp.concatenate([value[: rows - HALF], edge[HALF:]], axis=0)
    return jnp.where(step == steps - 1, tail, value)


def qkv_grad_kernel(
    split, place_ref,
    h_ref, dq_ref, dk_ref, dv_ref, rk_ref, rv_ref, left_ref, right_ref, cos_ref, sin_ref,
    ek_ref, ev_ref, *refs,
):
    *grad_refs, acc = refs
    step, steps = pl.program_id(0), pl.num_programs(0)
    rows, width = h_ref.shape

    @pl.when(step == 0)
    def _():
        for at, side in ((0, left_ref), (HALF, right_ref)):
            own = slice(at, at + HALF)
            cos, sin = cos_ref[own, :], sin_ref[own, :]
            for j in range(0, width, LANES):
                lanes = slice(j, j + LANES)
                total = rk_ref[own, lanes] + side[0, :, lanes].astype(f32)
                ek_ref[own, lanes] = rope_back(total, cos, sin).astype(bf16)
            ev_ref[own, :] = (rv_ref[own, :] + side[1].astype(f32)).astype(bf16)

    @pl.when(step == 0)
    def _():
        acc[...] = jnp.zeros_like(acc)

    low = h_ref[...]
    acc[:, :width] += dot_columns(low, dq_ref[...])
    acc[:, width : 2 * width] += dot_columns(low, patched(step, steps, rows, dk_ref, ek_ref))
    acc[:, 2 * width :] += dot_columns(low, patched(step, steps, rows, dv_ref, ev_ref))

    last = step == steps - 1
    if not split:

        @pl.when(last)
        def _():
            grad_refs[0][...] = acc[...].astype(bf16)

    else:
        half = acc.shape[1] // 2
        for c in (0, 1):

            @pl.when(last & (place_ref[0] == c))
            def _(c=c):
                for ref, side in zip(grad_refs, (c, 1 - c)):
                    ref[...] = acc[:, side * half : (side + 1) * half].astype(bf16)


def input_kernel(x_ref, gain_ref, w_ref, dmid_ref, dq_ref, dk_ref, dv_ref, ek_ref, ev_ref, dx_ref):
    step, steps = pl.program_id(0), pl.num_programs(0)
    rows, width = x_ref.shape

    dh = dot_rows(dq_ref[...], w_ref[:, :width])
    dh = dh + dot_rows(patched(step, steps, rows, dk_ref, ek_ref), w_ref[:, width : 2 * width])
    dh = dh + dot_rows(patched(step, steps, rows, dv_ref, ev_ref), w_ref[:, 2 * width :])
    unit, inverse = normed(x_ref[...].astype(f32))
    dx = dmid_ref[...].astype(f32) + normed_back(dh, gain_ref[0:1, :], unit, inverse)
    dx_ref[...] = dx.astype(bf16)


def shaped(shape, dtype):
    return jax.ShapeDtypeStruct(shape, dtype)


def tiles(rows, columns):
    return pl.BlockSpec((rows, columns), lambda i: (i, 0))


def pairs(rows, offset=0):
    return pl.BlockSpec((rows, LANES), lambda i: (0, i + offset))


def kept(*shape):
    return pl.BlockSpec(shape, lambda i: (0,) * len(shape), pipeline_mode=pl.Buffered(1))


def held(*shape):
    return pl.BlockSpec(shape, lambda i: (0,) * len(shape))


def call(
    kernel, grid, in_specs, out_specs, out_shape, scratch, flops, moved, aliases=None
):
    return pl.pallas_call(
        kernel,
        grid=(grid,),
        in_specs=in_specs,
        out_specs=out_specs,
        out_shape=out_shape,
        scratch_shapes=scratch,
        input_output_aliases=aliases or {},
        compiler_params=pltpu.CompilerParams(
            vmem_limit_bytes=vmem_bytes, dimension_semantics=("arbitrary",)
        ),
        cost_estimate=pl.CostEstimate(
            flops=flops // 64, bytes_accessed=moved // 64, transcendentals=0
        ),
    )


def project(x, gains, weight, cos, sin):
    rows, width = x.shape
    tile = min(TILE, rows)
    return call(
        project_kernel,
        rows // tile,
        [tiles(tile, width), held(2, width), kept(*weight.shape), tiles(tile, LANES), tiles(tile, LANES)],
        [tiles(tile, width)] * 4,
        [shaped((rows, width), bf16)] * 4,
        [],
        2 * rows * width * 3 * width,
        rows * width * 10 + weight.size * 2,
    )(x, gains, weight, cos, sin)


def project_edges(split, place, x, gains, cos, sin, *parts):
    rows, width = x.shape
    return call(
        functools.partial(project_edges_kernel, split),
        1,
        [pl.BlockSpec(memory_space=pltpu.SMEM), held(rows, width), held(2, width)]
        + [held(rows, LANES)] * 2
        + [held(*part.shape) for part in parts],
        [held(HALF, 2 * width)] * 2 + [held(width, 3 * width)],
        [shaped((HALF, 2 * width), bf16)] * 2 + [shaped((width, 3 * width), bf16)],
        [],
        4 * rows * width * width,
        rows * width * 6 + width * width * 12,
    )(place, x, gains, cos, sin, *parts)


def attend_scratch(rows):
    extended = rows + 2 * HALF
    return [
        pltpu.VMEM((extended, LANES), bf16),
        pltpu.VMEM((extended, LANES), bf16),
        pltpu.VMEM((rows // ROWS, SPAN, ROWS), f32),
        pltpu.VMEM((LANES, extended), bf16),
    ]


def attend(meta, q, k, v, left, right, first, count, before=()):
    rows, width = q.shape
    steps = width // LANES

    def columns(height, offset=0):
        return pairs(height, first + offset)

    return call(
        attend_kernel,
        count,
        [pl.BlockSpec(memory_space=pltpu.SMEM)]
        + [columns(rows)] * 3
        + [columns(HALF), columns(HALF, steps)] * 2
        + [pl.BlockSpec(memory_space=pl.ANY)] * len(before),
        [
            pl.BlockSpec((LANES, rows), lambda i: (i + first, 0)),
            pl.BlockSpec((1, rows // ROWS, 2 * ROWS), lambda i: (i + first, 0, 0)),
        ],
        [shaped((width, rows), bf16), shaped((steps, rows // ROWS, 2 * ROWS), f32)],
        attend_scratch(rows),
        8 * rows * width * 256,
        rows * width * 8,
        {8 + at: at for at in range(len(before))},
    )(meta, q, k, v, left, left, right, right, *before)


def back_specs(rows, steps):
    return (
        [pl.BlockSpec(memory_space=pltpu.SMEM)]
        + [pairs(rows)] * 4
        + [pairs(HALF), pairs(HALF, steps)] * 2
        + [pl.BlockSpec((1, rows // ROWS, 2 * ROWS), lambda i: (i, 0, 0)), held(rows, LANES), held(rows, LANES)]
    )


def back_scratch(rows):
    extended = rows + 2 * HALF
    return attend_scratch(rows) + [pltpu.VMEM((extended, LANES), f32)] * 2


def attend_back_edges(meta, q, k, v, do, left, right, lse, cos, sin):
    rows, width = q.shape
    steps = width // LANES
    span = 2 * SPAN
    return call(
        attend_back_edges_kernel,
        steps,
        back_specs(rows, steps),
        [pairs(2 * ROWS)]
        + [pairs(span)] * 2
        + [pl.BlockSpec((2, HALF, LANES), lambda i: (0, 0, i))] * 2
        + [pairs(2 * HALF)] * 2,
        [shaped((2 * ROWS, width), bf16)]
        + [shaped((span, width), f32)] * 2
        + [shaped((2, HALF, width), bf16)] * 2
        + [shaped((2 * HALF, width), f32)] * 2,
        back_scratch(rows),
        20 * 2 * ROWS * width * 256,
        rows * width * 10,
    )(meta, q, k, v, do, left, left, right, right, lse, cos, sin)


def attend_back(meta, q, k, v, do, left, right, lse, cos, sin, edges):
    rows, width = q.shape
    steps = width // LANES
    span = 2 * SPAN
    return call(
        attend_back_kernel,
        steps,
        back_specs(rows, steps) + [pairs(2 * ROWS)] + [pairs(span)] * 2,
        [pairs(rows)] * 3,
        [shaped((rows, width), bf16)] * 3,
        back_scratch(rows),
        20 * rows * width * 256,
        rows * width * 14,
    )(meta, q, k, v, do, left, left, right, right, lse, cos, sin, *edges)


def middle(split, place, x, o, ct, gains, shapes, *weights):
    rows, width = x.shape
    tile = WIDE_TILE if rows % WIDE_TILE == 0 else rows
    wa, wm, wd = shapes
    if split:
        grads = [(width, wm[1] // 2 + 3 * (width // 2))] * 2
    else:
        grads = [wd, wm, wa]
    return call(
        functools.partial(middle_kernel, split),
        rows // tile,
        [
            pl.BlockSpec(memory_space=pltpu.SMEM),
            tiles(tile, width),
            pl.BlockSpec((width, tile), lambda i: (0, i)),
            tiles(tile, width),
            held(2, width),
        ]
        + [kept(*w.shape) for w in weights],
        [tiles(tile, width)] * 3 + [kept(*shape) for shape in grads],
        [shaped((rows, width), bf16)] * 3 + [shaped(shape, bf16) for shape in grads],
        ([pltpu.VMEM(w, bf16) for w in shapes] if split else [])
        + [pltpu.VMEM(wd, f32), pltpu.VMEM(wm, f32), pltpu.VMEM(wa, f32)],
        6 * rows * width * width * 5,
        rows * width * 14 + 20 * width * width,
    )(place, x, o, ct, gains, *weights)


def qkv_gradient(split, place, h, dq, dk, dv, ek, ev, left, right, cos, sin):
    rows, width = h.shape
    tile = min(TILE, rows)
    grads = [(width, 3 * width // 2)] * 2 if split else [(width, 3 * width)]
    return call(
        functools.partial(qkv_grad_kernel, split),
        rows // tile,
        [pl.BlockSpec(memory_space=pltpu.SMEM)]
        + [tiles(tile, width)] * 4
        + [held(2 * HALF, width)] * 2
        + [held(2, HALF, width)] * 2
        + [held(2 * HALF, LANES)] * 2,
        [held(2 * HALF, width)] * 2 + [held(*shape) for shape in grads],
        [shaped((2 * HALF, width), bf16)] * 2 + [shaped(shape, bf16) for shape in grads],
        [pltpu.VMEM((width, 3 * width), f32)],
        6 * rows * width * width,
        rows * width * 8 + 6 * width * width,
    )(place, h, dq, dk, dv, ek, ev, left, right, cos, sin)


def input_gradient(x, gains, weight, dmid, dq, dk, dv, ek, ev):
    rows, width = x.shape
    tile = min(TILE, rows)
    return call(
        input_kernel,
        rows // tile,
        [tiles(tile, width), held(2, width), kept(*weight.shape)]
        + [tiles(tile, width)] * 4
        + [held(2 * HALF, width)] * 2,
        tiles(tile, width),
        shaped((rows, width), bf16),
        [],
        6 * rows * width * width,
        rows * width * 14 + 6 * width * width,
    )(x, gains, weight, dmid, dq, dk, dv, ek, ev)


def rope_tables(positions, head_size):
    half_size = head_size // 2
    exponent = jnp.arange(half_size, dtype=f32) * (2.0 / head_size)
    inverse = rope_theta ** (-exponent)
    inverse = jnp.tile(inverse, LANES // half_size)
    angles = positions.astype(f32)[:, None] * inverse[None, :]
    sign = jnp.where(jnp.arange(LANES) % head_size < half_size, -1.0, 1.0).astype(f32)
    return jnp.cos(angles), jnp.sin(angles) * sign


def adam_update(master, first_moment, second_moment, gradient, step_rate):
    gradient = gradient.astype(f32)
    new_first = beta_first * first_moment + (1.0 - beta_first) * gradient
    new_second = beta_second * second_moment + (1.0 - beta_second) * gradient * gradient
    first_hat = new_first / (1.0 - beta_first**ADAM_STEP)
    second_hat = new_second / (1.0 - beta_second**ADAM_STEP)
    new_master = master - step_rate * (
        decay_rate * master + first_hat / (jnp.sqrt(second_hat) + adam_epsilon)
    )
    return (new_first, new_second, new_master)


def edge_rows(value):
    return value[:HALF], value[value.shape[0] - HALF :]


def per_device(
    tokens,
    positions,
    cotangent,
    qkv_weight,
    attn_weight,
    mlp_weight,
    down_weight,
    norm_gains,
    qkv_first,
    qkv_second,
    attn_first,
    attn_second,
    mlp_first,
    mlp_second,
    down_first,
    down_second,
    gains_first,
    gains_second,
):
    rows, width = tokens.shape
    device = lax.axis_index(("seq", "shard"))
    last_device = lax.axis_size(("seq", "shard")) - 1
    shards = lax.axis_size("shard")
    quarters = lax.axis_size("seq") // 2
    core = lax.axis_index("seq") % 2
    split = (shards, quarters) if split_pays() else None
    place = jnp.stack([core, lax.axis_index("seq") // 2, lax.axis_index("shard")])
    place = place.astype(jnp.int32)
    half = qkv_weight.shape[1] // 2
    slot = qkv_weight.shape[0] // quarters
    rest = down_weight.shape[0] // quarters - slot
    wide = mlp_weight.shape[1] // 2
    down_at = wide + attn_weight.shape[1] // 2
    quarter = lax.axis_index("seq") // 2
    edge_x = jnp.concatenate(edge_rows(tokens), axis=0)
    if split:
        part = own_block(qkv_weight, quarter * slot, slot)
        gain_rows = jnp.pad(norm_gains.astype(bf16), ((0, 6), (0, half - norm_gains.shape[1])))
        qkv_stack = stack(jnp.concatenate([part, gain_rows], axis=0), "shard", 1)
        rest_part = jnp.concatenate(
            [own_block(w, quarter * slot, slot) for w in (mlp_weight, attn_weight)]
            + down_part(down_weight, slot),
            axis=1,
        )
        qkv_part = jnp.concatenate([piece[:slot] for piece in qkv_stack], axis=0)
        rest_part = doubled(rest_part, 1)
        qkv_part = after(qkv_part, rest_part)
        rest_part = doubled(rest_part, 2)
        qkv_pieces = stack(qkv_part, "seq", 2)
        positions, edge_x = after((positions, edge_x), qkv_part)
        gains = jnp.zeros((shards, 2, norm_gains.shape[1]), bf16)
        for d, piece in enumerate(qkv_stack):
            piece = piece[None, slot : slot + 2, : norm_gains.shape[1]]
            gains = lax.dynamic_update_slice_in_dim(gains, piece, lax.axis_index("shard") ^ d, 0)
        gains = gains.astype(f32).transpose(1, 0, 2).reshape(2, -1)
    else:
        lows = [w.astype(bf16) for w in (qkv_weight, attn_weight, mlp_weight, down_weight)]
        full_qkv, full_attn, full_mlp, full_down = (
            lax.all_gather(w, "shard", axis=0, tiled=True) for w in lows
        )
        gains = lax.all_gather(norm_gains.astype(bf16), "shard", axis=1, tiled=True).astype(f32)
        qkv_parts = (full_qkv,)
    cos, sin = rope_tables(positions, width // HEADS)
    start = jnp.max(jnp.where(positions == 0, jnp.arange(rows, dtype=jnp.int32), 0))
    low = jnp.where(device > 0, -HALF, 0)
    high = jnp.where(device < last_device, rows + HALF, rows)
    meta = jnp.stack([start, low, high]).astype(jnp.int32)
    edge_cos, edge_sin = (jnp.concatenate(edge_rows(value), axis=0) for value in (cos, sin))
    if split:
        qkv_pieces = after(qkv_pieces, rest_part, gains, meta, place, edge_x, edge_cos, edge_sin)
        qkv_part = jnp.concatenate(qkv_pieces, axis=0)
        rest_part = after(rest_part, qkv_part)
        qkv_parts = qkv_part, swap(qkv_part, "seq", 1)
    kv_head, kv_tail, full_qkv = project_edges(
        split, place, edge_x, gains, edge_cos, edge_sin, *qkv_parts
    )
    left = to_right(kv_tail)
    right = to_left(kv_head)
    h, q, k, v = project(after(tokens, kv_head), gains, full_qkv, cos, sin)
    left = after(left, k)
    right = after(right, k)
    pair_count = width // LANES
    early = 2 * pair_count // 3
    before = attend(meta, q, k, v, left, right, 0, early)
    if split:
        rest_part = jnp.concatenate(stack(rest_part, "seq", 2, (before[0],)), axis=0)
        rest_weights = rest_part, swap(rest_part, "seq", 1)
        q = after(q, rest_part)
    else:
        rest_weights = full_attn, full_mlp, full_down
    o, lse = attend(meta, q, k, v, left, right, early, pair_count - early, before)
    shapes = (
        (width, attn_weight.shape[1]),
        (width, mlp_weight.shape[1]),
        (shards * down_weight.shape[0], width),
    )
    layer_output, dmid, do, *rest_grads = middle(
        split, place, tokens, o, cotangent, gains, shapes, *rest_weights
    )
    if split:
        rest_own, rest_other = rest_grads
        rest_got = swap(rest_other, "seq", 1)
    back_args = (meta, q, k, v, do, left, right, lse, cos, sin)
    *edges, halo_head, halo_tail, raw_k, raw_v = attend_back_edges(*back_args)
    from_right = to_left(halo_head)
    from_left = to_right(halo_tail)
    if split:
        rest_half = keep_half(rest_own, after(rest_got, halo_head))
        do = after(do, rest_half)
        back_args = (meta, q, k, v, do, left, right, lse, cos, sin)
        rest_pieces = quarter_pieces(rest_half)
    dq, dk, dv = attend_back(*back_args, edges)
    edge_k, edge_v, *qkv_grads = qkv_gradient(
        split, place, h, dq, dk, dv, raw_k, raw_v, after(from_left, dq), after(from_right, dq), edge_cos, edge_sin
    )
    if split:
        qkv_own, qkv_other = qkv_grads
        rest_part = sum_after(rest_pieces, qkv_own)
        qkv_got = swap(after(qkv_other, rest_part), "seq", 1)
        qkv_half = keep_half(qkv_own, qkv_got)
        dq = after(dq, qkv_half)
        qkv_pieces = quarter_pieces(qkv_half)
        rest_pieces = halve(rest_part, 2)
    input_grad = input_gradient(tokens, gains, full_qkv, dmid, dq, dk, dv, edge_k, edge_v)
    if split:
        qkv_part = sum_after(qkv_pieces, input_grad)
        rest_part = sum_after(list(rest_pieces), qkv_part)
        rest_pieces = halve(rest_part, 1)
        rest_part = sum_after(list(rest_pieces), qkv_part)[0]
        qkv_part = sum_after(shard_pieces(qkv_part), rest_part)
        rest_half = owners_half(rest_part, (qkv_part,))
        rest_got = swap(rest_half, "seq", 1)
        qkv_half = owners_half(qkv_part, (rest_half,))
        qkv_got = swap(qkv_half, "seq", 1)
        first, second = by_core(core, rest_half, after(rest_got, qkv_half))
        mlp_total = side_by_side(first[:, :wide], second[:, :wide])
        attn_total = side_by_side(first[:, wide:down_at], second[:, wide:down_at])
        down_total = side_by_side(
            *(unpack_down(x[:, down_at:], quarters, rest) for x in (first, second))
        )
    else:
        down_total, mlp_total, attn_total, qkv_total = (
            reduce_whole(g) for g in (*rest_grads, *qkv_grads)
        )
    attn_new = adam_update(attn_weight, attn_first, attn_second, attn_total, rate_matrix)
    mlp_new = adam_update(mlp_weight, mlp_first, mlp_second, mlp_total, rate_matrix)
    down_new = adam_update(down_weight, down_first, down_second, down_total, rate_matrix)
    if split:
        qkv_got = after(qkv_got, attn_new[0], mlp_new[0], down_new[0])
        qkv_total = side_by_side(*by_core(core, qkv_half, qkv_got))
    qkv_new = adam_update(qkv_weight, qkv_first, qkv_second, qkv_total, rate_matrix)
    gains_total = jnp.stack(
        [
            gain_grad(qkv_weight, qkv_total, norm_gains[0]),
            gain_grad(mlp_weight, mlp_total, norm_gains[1]),
        ]
    )
    gains_new = adam_update(norm_gains, gains_first, gains_second, gains_total, rate_gains)
    return (layer_output, input_grad, *qkv_new, *attn_new, *mlp_new, *down_new, *gains_new)


def solution(mesh):
    tokens, rows, columns = P(("seq", "shard"), None), P("shard", None), P(None, "shard")
    matrices = (rows,) * 4
    return jax.shard_map(
        per_device,
        mesh=mesh,
        in_specs=(tokens, P(("seq", "shard")), tokens, *matrices, columns)
        + (rows,) * 8
        + (columns,) * 2,
        out_specs=(tokens, tokens) + (rows,) * 12 + (columns,) * 3,
        check_vma=False,
    )
```
